32 devices in a mesh: tm: 16 (over z, x, core), sec: 2 (over y).
Axes of the slice: x: 2, y: 2, z: 4, core: 2. Of those that a mesh axis runs over, the one named last changes fastest.
Arguments:
- state: float32 [64, 6, 4, 32, 128], P('tm', None, None, 'sec'), may hold values from 0.05 to 1
- adjoint: float32 [64, 6, 4, 32, 128], P('tm', None, None, 'sec'), may hold values from -6 to 6
- plan: int32 [64, 4], P('tm'), may hold values from 1 to 3
- valve: int32 [64, 4], P('tm'), may hold values 0 or 1
Outputs:
- residual: float32 [64, 6, 4, 32, 128], P('tm', None, None, 'sec')
- adjoint_out: float32 [64, 6, 4, 32, 128], P('tm', None, None, 'sec')
The draws below stay inside these ranges and needn't reach their ends.
Inputs may be any that keep to these rules, and one draw needn't show every extreme that they name: Bed b at instance t takes purge gas from bed (b + plan) mod 4, never from itself.
All inputs are finite; a program needn't handle non-finite values. No bound on the sum of `valve` on one device may be relied on, other than what follows from the above.
Results may differ from the reference program's by a relative error of at most 0.0003.
Values sent between devices are 32-bit elements; how exact they have to be, the bound alone decides.
No kernel may reach another device: no remote copies, remote signals or barrier semaphores. Data moves between devices by JAX's collectives and lax.ppermute only.
A program may use at most 64 MiB of HBM per device.

```python
import jax
import jax.numpy as jnp
from jax import lax

I_DEV = 4
NR = 128
BEDS = 4
COMP = 6
NT = 64
NZ = 32


def with_ends(values, key, low, largest):
    shape = values.shape
    place = [jax.random.randint(jax.random.fold_in(key, axis), (), 0, shape[axis]) for axis in range(len(shape))]
    values = values.at[tuple(place)].set(low)
    longest = shape.index(max(shape))
    place[longest] = (place[longest] + 1) % shape[longest]
    return values.at[tuple(place)].set(largest)


def steps_of(rng, extent, cuts, low, high):
    def one(axis_at, parts):
        draws = jax.random.uniform(jax.random.fold_in(jax.random.fold_in(rng, 6), axis_at), (parts,), jnp.float32, low / len(cuts), high / len(cuts))
        return jnp.repeat(jnp.exp(draws), extent[axis_at] // parts).reshape((-1,) + (1,) * (len(extent) - axis_at - 1))

    factor_of = one(*cuts[0])
    for cut in cuts[1:]:
        factor_of = factor_of * one(*cut)
    return factor_of


def bell_draw(own_key, dims, scale, bound, shards=(), kind=jnp.bfloat16):
    factor_of = steps_of(own_key, dims, shards, -0.22, 0.18) if shards else 1.0
    array = jax.random.normal(own_key, dims, jnp.float32) * scale * factor_of
    return jnp.minimum(jnp.maximum(array, -bound), bound).astype(kind)


def setup_inputs(seed: int = 0) -> dict:
    key_of = jax.random.split(jax.random.key(seed), 5)
    state = jnp.clip(0.05 + 0.95 * jax.random.uniform(key_of[0], (NT, COMP, BEDS, NZ, NR), jnp.float32) ** steps_of(key_of[0], (NT, COMP, BEDS, NZ, NR), ((0, 16), (3, 2)), -0.2, 0.2), 0.05, 1.0)
    adjoint = bell_draw(key_of[1], (NT, COMP, BEDS, NZ, NR), 1.0, 6.0, ((0, 16), (3, 2)), jnp.float32)
    plan = with_ends(jax.random.randint(key_of[2], (NT, BEDS), 1, BEDS), jax.random.fold_in(key_of[2], 1), 1, BEDS - 1).astype(jnp.int32)
    valve = with_ends((jax.random.randint(key_of[3], (NT, BEDS), 0, 2) < 1).astype(jnp.int32), jax.random.fold_in(key_of[3], 1), 0, 1)
    return dict(state=state, adjoint=adjoint, plan=plan, valve=valve)


STENCIL = (0.8, -0.2, 4.0 / 105.0, -1.0 / 280.0)
TIME_SCALE = 4.0
FLOW_VELOCITY = 1.0
AXIAL_DISPERSION = 0.3
RADIAL_SPREADING = 0.2
BINDING_STRENGTH = (1.5, 0.6)
HEAT_EXPONENT = (0.5, 0.3)
KINETIC = (1.2, 0.7)
CAPACITY = (2.0, 1.0)
SORPTION_HEAT = (0.4, 0.25)
PURGE_GAIN = 1.5

def radial_diffusion_term(field):
    zero_edge = jnp.zeros_like(field[..., :1])
    upper = jnp.concatenate([field[..., 1:], zero_edge], axis=-1)
    lower = jnp.concatenate([zero_edge, field[..., :-1]], axis=-1)
    return upper - 2.0 * field + lower

def time_derivative(extended, instances):
    total_sum = jnp.zeros_like(extended[4:4 + instances])
    for offset, weight in enumerate(STENCIL):
        shift_by = offset + 1
        total_sum = total_sum + weight * (extended[4 + shift_by:4 + shift_by + instances] - extended[4 - shift_by:4 - shift_by + instances])
    return TIME_SCALE * total_sum

def spatial_residual(padded, offsets, valves, purge_mask):
    middle_cell = padded[:, :, :, 1:-1]
    cell_underneath = padded[:, :, :, :-2]
    cell_overhead = padded[:, :, :, 2:]
    gas_part = middle_cell[:, 0:3]
    transport = FLOW_VELOCITY * (gas_part - cell_underneath[:, 0:3]) - AXIAL_DISPERSION * (cell_overhead[:, 0:3] - 2.0 * gas_part + cell_underneath[:, 0:3])
    gas_res = transport - RADIAL_SPREADING * radial_diffusion_term(gas_part)
    thermal_field = middle_cell[:, 5]
    binding_first = BINDING_STRENGTH[0] * jnp.exp(HEAT_EXPONENT[0] * thermal_field)
    binding_second = BINDING_STRENGTH[1] * jnp.exp(HEAT_EXPONENT[1] * thermal_field)
    denominator = 1.0 + binding_first * middle_cell[:, 0] + binding_second * middle_cell[:, 1]
    uptake_first = KINETIC[0] * (CAPACITY[0] * binding_first * middle_cell[:, 0] / denominator - middle_cell[:, 3])
    uptake_second = KINETIC[1] * (CAPACITY[1] * binding_second * middle_cell[:, 1] / denominator - middle_cell[:, 4])
    bed_count = padded.shape[2]
    bed_ids = jnp.arange(bed_count, dtype=jnp.int32)
    product = lax.optimization_barrier(jnp.sum(gas_part * purge_mask[None, None, None, :, None], axis=3))
    source = (bed_ids[None, :] + offsets) % bed_count
    lookup_table = (source[:, :, None] == bed_ids[None, None, :]).astype(jnp.float32)
    incoming = lax.optimization_barrier(jnp.sum(lookup_table[:, None, :, :, None] * product[:, :, None, :, :], axis=3))
    purge_term = PURGE_GAIN * valves.astype(jnp.float32)[:, None, :, None] * (product - incoming)
    gas_res = gas_res + purge_term[:, :, :, None, :] * purge_mask[None, None, None, :, None]
    energy_residual = FLOW_VELOCITY * (thermal_field - cell_underneath[:, 5]) - AXIAL_DISPERSION * (cell_overhead[:, 5] - 2.0 * thermal_field + cell_underneath[:, 5])
    energy_residual = energy_residual - RADIAL_SPREADING * radial_diffusion_term(thermal_field) - (SORPTION_HEAT[0] * uptake_first + SORPTION_HEAT[1] * uptake_second)
    rows = [gas_res[:, 0] + uptake_first, gas_res[:, 1] + uptake_second, gas_res[:, 2], -uptake_first, -uptake_second, energy_residual]
    return jnp.stack(rows, axis=1)

def reference(state, adjoint, plan, valve):
    instance_total = state.shape[0]
    state_ext = jnp.concatenate([state[-4:], state, state[:4]], axis=0)
    adjoint_ext = jnp.concatenate([adjoint[-4:], adjoint, adjoint[:4]], axis=0)
    purge_mask = (jnp.arange(NZ, dtype=jnp.int32) == NZ - 1).astype(jnp.float32)
    block_count = instance_total // I_DEV

    def per_block(block_index):
        first_row = block_index * I_DEV
        state_block = lax.dynamic_slice_in_dim(state_ext, first_row, I_DEV + 8, 0)
        adjoint_block = lax.dynamic_slice_in_dim(adjoint_ext, first_row, I_DEV + 8, 0)
        offsets = lax.dynamic_slice_in_dim(plan, first_row, I_DEV, 0)
        valves = lax.dynamic_slice_in_dim(valve, first_row, I_DEV, 0)
        middle_cell = state_block[4:4 + I_DEV]
        multiplier = adjoint_block[4:4 + I_DEV]
        padded = jnp.pad(middle_cell, ((0, 0), (0, 0), (0, 0), (1, 1), (0, 0)))
        forward, pullback = jax.vjp(lambda field: spatial_residual(field, offsets, valves, purge_mask), padded)
        pulled = pullback(multiplier)[0][:, :, :, 1:-1]
        return (time_derivative(state_block, I_DEV) + forward, pulled - time_derivative(adjoint_block, I_DEV))
    residual_out, adjoint_res = lax.map(per_block, jnp.arange(block_count, dtype=jnp.int32))
    return (residual_out.reshape(state.shape), adjoint_res.reshape(state.shape))
```

```python
import functools

import jax
import jax.numpy as jnp
from jax import lax
from jax.experimental import pallas as pl
from jax.experimental.pallas import tpu as pltpu
from jax.sharding import PartitionSpec as P

STENCIL = (0.8, -0.2, 4.0 / 105.0, -1.0 / 280.0)
TIME_SCALE = 4.0
FLOW_VELOCITY = 1.0
AXIAL_DISPERSION = 0.3
RADIAL_SPREADING = 0.2
BINDING_STRENGTH = (1.5, 0.6)
HEAT_EXPONENT = (0.5, 0.3)
KINETIC = (1.2, 0.7)
CAPACITY = (2.0, 1.0)
SORPTION_HEAT = (0.4, 0.25)
PURGE_GAIN = 1.5

REACH = len(STENCIL)
WEIGHTS = tuple(TIME_SCALE * c for c in STENCIL)
MOVING = (0, 1, 2, 5)
CENTRE = FLOW_VELOCITY + 2.0 * AXIAL_DISPERSION + 2.0 * RADIAL_SPREADING
UPWIND = FLOW_VELOCITY + AXIAL_DISPERSION


def shifted(x, step, edge):
    cells = x.shape[0]
    row = lax.broadcasted_iota(jnp.int32, x.shape, 0)
    if step > 0:
        return jnp.where(row == 0, edge, pltpu.roll(x, 1, 0))
    return jnp.where(row == cells - 1, edge, pltpu.roll(x, cells - 1, 0))


def radial_pair(x):
    width = x.shape[1]
    lane = lax.broadcasted_iota(jnp.int32, x.shape, 1)
    lower = jnp.where(lane == 0, 0.0, pltpu.roll(x, 1, 1))
    upper = jnp.where(lane == width - 1, 0.0, pltpu.roll(x, width - 1, 1))
    return lower + upper


def transport(x, near, far):
    return CENTRE * x - UPWIND * near - AXIAL_DISPERSION * far - RADIAL_SPREADING * radial_pair(x)


def main_kernel(flags, plan, valve, state, adjoint, edge, in_state, in_adjoint, res, adj):
    instances, comps, beds, cells, _ = state.shape
    odd = flags[0]
    first, last = flags[1], flags[2]

    def cell_block(i, carry):
        t = i // beds
        b = lax.rem(i, beds)
        x = [state[t, c, b] for c in range(comps)]
        m = [adjoint[t, c, b] for c in range(comps)]
        y1, y2, _, q1, q2, temp = x
        b1 = BINDING_STRENGTH[0] * jnp.exp(HEAT_EXPONENT[0] * temp)
        b2 = BINDING_STRENGTH[1] * jnp.exp(HEAT_EXPONENT[1] * temp)
        over = 1.0 / (1.0 + b1 * y1 + b2 * y2)
        slope1 = b1 * over
        slope2 = b2 * over
        cover1 = slope1 * y1
        cover2 = slope2 * y2
        rate1 = KINETIC[0] * (CAPACITY[0] * cover1 - q1)
        rate2 = KINETIC[1] * (CAPACITY[1] * cover2 - q2)
        m1 = m[0] - m[3] - SORPTION_HEAT[0] * m[5]
        m2 = m[1] - m[4] - SORPTION_HEAT[1] * m[5]
        g1 = (KINETIC[0] * CAPACITY[0]) * m1
        g2 = (KINETIC[1] * CAPACITY[1]) * m2
        h = g1 * cover1 + g2 * cover2
        e1 = g1 - h
        e2 = g2 - h
        source = {0: rate1, 1: rate2, 5: -SORPTION_HEAT[0] * rate1 - SORPTION_HEAT[1] * rate2}
        pulled = {
            0: slope1 * e1,
            1: slope2 * e2,
            5: HEAT_EXPONENT[0] * cover1 * e1 + HEAT_EXPONENT[1] * cover2 * e2,
        }
        for c in MOVING:
            from_x = edge[0, t, c, b][None]
            from_m = edge[1, t, c, b][None]
            below_x = jnp.where(first == 1, 0.0, from_x)
            above_x = jnp.where(last == 1, 0.0, from_x)
            below_m = jnp.where(first == 1, 0.0, from_m)
            above_m = jnp.where(last == 1, 0.0, from_m)
            r = transport(x[c], shifted(x[c], 1, below_x), shifted(x[c], -1, above_x))
            a = transport(m[c], shifted(m[c], -1, above_m), shifted(m[c], 1, below_m))
            res[t, c, b] = r + source[c] if c in source else r
            adj[t, c, b] = a + pulled[c] if c in pulled else a
        res[t, 3, b] = -rate1
        res[t, 4, b] = -rate2
        adj[t, 3, b] = -KINETIC[0] * m1
        adj[t, 4, b] = -KINETIC[1] * m2
        return carry

    lax.fori_loop(0, instances * beds, cell_block, 0)

    @pl.when(last == 1)
    def _():
        def purge(i, carry):
            t = i // beds
            b = lax.rem(i, beds)
            s = lax.rem(b + plan[t, b], beds)
            gain = PURGE_GAIN * valve[t, b].astype(jnp.float32)
            end = pl.ds(cells - 1, 1)
            for c in range(3):
                res[t, c, b, end] += gain * (state[t, c, b, end] - state[t, c, s, end])
                flow = gain * adjoint[t, c, b, end]
                adj[t, c, b, end] += flow
                adj[t, c, s, end] -= flow
            return carry

        lax.fori_loop(0, instances * beds, purge, 0)

    sign = jnp.where(odd == 1, -1.0, 1.0)
    at = [jnp.where(odd == 1, instances - 1 - t, t) for t in range(instances)]

    def time_block(i, carry):
        c = i // beds
        b = lax.rem(i, beds)
        for own, other, out, factor in ((state, in_state, res, sign), (adjoint, in_adjoint, adj, -sign)):
            line = [own[at[t], c, b] for t in range(instances)]
            line += [other[at[t], c, b] for t in range(instances)]
            for t in range(instances):
                total = 0.0
                for k in range(1, REACH + 1):
                    diff = line[t + k]
                    if t - k >= 0:
                        diff = diff - line[t - k]
                    total = total + WEIGHTS[k - 1] * diff
                out[at[t], c, b] += factor * total
        return carry

    lax.fori_loop(0, comps * beds, time_block, 0)


def finish_kernel(scale, flags, part, came, out):
    instances, comps, beds, _, _ = part.shape
    odd = flags[0]
    sign = jnp.where(odd == 1, -scale, scale)
    at = [jnp.where(odd == 1, instances - 1 - t, t) for t in range(instances)]

    def block(i, carry):
        c = i // beds
        b = lax.rem(i, beds)
        line = [came[at[t], c, b] for t in range(instances)]
        for t in range(instances):
            total = 0.0
            for j in range(t, instances):
                total = total + WEIGHTS[t + instances - j - 1] * line[j]
            out[at[t], c, b] = part[at[t], c, b] - sign * total
        return carry

    lax.fori_loop(0, comps * beds, block, 0)


VMEM = pl.BlockSpec(memory_space=pltpu.VMEM)
SMEM = pl.BlockSpec(memory_space=pltpu.SMEM)


def local(state, adjoint, plan, valve):
    count = lax.axis_size("tm")
    sections = lax.axis_size("sec")
    swap_out = [(i, (i + 1) % count if i % 2 else (i - 1) % count) for i in range(count)]
    swap_in = [(i, i ^ 1) for i in range(count)]
    out_state = lax.ppermute(state, "tm", swap_out)
    out_adjoint = lax.ppermute(adjoint, "tm", swap_out)
    in_state = lax.ppermute(state, "tm", swap_in)
    in_adjoint = lax.ppermute(adjoint, "tm", swap_in)

    sec = lax.axis_index("sec")
    flags = jnp.stack(
        [lax.axis_index("tm") % 2, (sec == 0).astype(jnp.int32), (sec == sections - 1).astype(jnp.int32)]
    ).astype(jnp.int32)
    ends = [jnp.where(sec == 0, a[:, :, :, -1], a[:, :, :, 0]) for a in (state, adjoint)]
    edge = lax.ppermute(jnp.stack(ends), "sec", [(i, i ^ 1) for i in range(sections)])

    block = jax.ShapeDtypeStruct(state.shape, state.dtype)
    res, adj = pl.pallas_call(
        main_kernel,
        out_shape=(block, block),
        in_specs=[SMEM] * 3 + [VMEM] * 5,
        out_specs=(VMEM, VMEM),
        compiler_params=pltpu.CompilerParams(vmem_limit_bytes=24 * 2**20),
        cost_estimate=pl.CostEstimate(flops=12_000_000, bytes_accessed=5_000_000, transcendentals=70_000),
        name="local_part",
    )(flags, plan, valve, state, adjoint, edge, in_state, in_adjoint)

    def finish(scale, part, came, name):
        return pl.pallas_call(
            functools.partial(finish_kernel, scale),
            out_shape=block,
            in_specs=[SMEM, VMEM, VMEM],
            out_specs=VMEM,
            compiler_params=pltpu.CompilerParams(vmem_limit_bytes=16 * 2**20),
            cost_estimate=pl.CostEstimate(flops=4_000_000, bytes_accessed=2_400_000, transcendentals=0),
            name=name,
        )(flags, part, came)

    return (finish(1.0, res, out_state, "finish_residual"), finish(-1.0, adj, out_adjoint, "finish_adjoint"))


def solution(mesh):
    spec = P("tm", None, None, "sec", None)
    return jax.shard_map(
        local,
        mesh=mesh,
        in_specs=(spec, spec, P("tm", None), P("tm", None)),
        out_specs=(spec, spec),
        check_vma=False,
    )
```

```python
import functools

import jax
import jax.numpy as jnp
from jax import lax
from jax.experimental import pallas as pl
from jax.experimental.pallas import tpu as pltpu
from jax.sharding import PartitionSpec as P

STENCIL = (0.8, -0.2, 4.0 / 105.0, -1.0 / 280.0)
TIME_SCALE = 4.0
FLOW_VELOCITY = 1.0
AXIAL_DISPERSION = 0.3
RADIAL_SPREADING = 0.2
BINDING_STRENGTH = (1.5, 0.6)
HEAT_EXPONENT = (0.5, 0.3)
KINETIC = (1.2, 0.7)
CAPACITY = (2.0, 1.0)
SORPTION_HEAT = (0.4, 0.25)
PURGE_GAIN = 1.5

REACH = len(STENCIL)
WEIGHTS = tuple(TIME_SCALE * c for c in STENCIL)
MOVING = (0, 1, 2, 5)
CENTRE = FLOW_VELOCITY + 2.0 * AXIAL_DISPERSION + 2.0 * RADIAL_SPREADING
UPWIND = FLOW_VELOCITY + AXIAL_DISPERSION
CHUNKS = ((0, 3), (3, 2), (5, 1))


def shifted(x, step, edge):
    cells = x.shape[0]
    row = lax.broadcasted_iota(jnp.int32, x.shape, 0)
    if step > 0:
        return jnp.where(row == 0, edge, pltpu.roll(x, 1, 0))
    return jnp.where(row == cells - 1, edge, pltpu.roll(x, cells - 1, 0))


def radial_pair(x):
    width = x.shape[1]
    lane = lax.broadcasted_iota(jnp.int32, x.shape, 1)
    lower = jnp.where(lane == 0, 0.0, pltpu.roll(x, 1, 1))
    upper = jnp.where(lane == width - 1, 0.0, pltpu.roll(x, width - 1, 1))
    return lower + upper


def transport(x, near, far):
    return CENTRE * x - UPWIND * near - AXIAL_DISPERSION * far - RADIAL_SPREADING * radial_pair(x)


def place(c):
    for n, (low, size) in enumerate(CHUNKS):
        if low <= c < low + size:
            return n, c - low


def load_kernel(flags, state, adjoint, both, edge, *rest):
    chunks, sem = rest[:-1], rest[-1]
    instances, comps, beds, cells, _ = state.shape
    copies = [
        pltpu.make_async_copy(state, both.at[:, pl.ds(0, comps)], sem.at[0]),
        pltpu.make_async_copy(adjoint, both.at[:, pl.ds(comps, comps)], sem.at[1]),
    ]
    for n, (low, size) in enumerate(CHUNKS):
        copies.append(pltpu.make_async_copy(adjoint.at[:, pl.ds(low, size)], chunks[n], sem.at[2 + n]))
    for copy in copies:
        copy.start()
    for copy in copies:
        copy.wait()
    first = flags[1]

    def pick(i, carry):
        t = i // len(MOVING)
        for k, c in enumerate(MOVING):

            @pl.when(lax.rem(i, len(MOVING)) == k)
            def _():
                for a in range(2):
                    for b in range(beds):
                        x = both[t, a * comps + c, b]
                        edge[t, a * len(MOVING) + k, pl.ds(b, 1)] = jnp.where(first == 1, x[cells - 1 :], x[:1])

        return carry

    lax.fori_loop(0, instances * len(MOVING), pick, 0)


def main_kernel(flags, plan, valve, both, edge, near, res, *adj):
    instances, comps, beds, cells, _ = res.shape
    odd, first, last = flags[0], flags[1], flags[2]

    def adj_at(t, c, *where):
        n, k = place(c)
        return adj[n].at[(t, k) + where]

    def cell_block(i, carry):
        t = i // beds
        b = lax.rem(i, beds)
        x = [both[t, c, b] for c in range(comps)]
        m = [both[t, comps + c, b] for c in range(comps)]
        y1, y2, _, q1, q2, temp = x
        b1 = BINDING_STRENGTH[0] * jnp.exp(HEAT_EXPONENT[0] * temp)
        b2 = BINDING_STRENGTH[1] * jnp.exp(HEAT_EXPONENT[1] * temp)
        over = 1.0 / (1.0 + b1 * y1 + b2 * y2)
        slope1 = b1 * over
        slope2 = b2 * over
        cover1 = slope1 * y1
        cover2 = slope2 * y2
        rate1 = KINETIC[0] * (CAPACITY[0] * cover1 - q1)
        rate2 = KINETIC[1] * (CAPACITY[1] * cover2 - q2)
        m1 = m[0] - m[3] - SORPTION_HEAT[0] * m[5]
        m2 = m[1] - m[4] - SORPTION_HEAT[1] * m[5]
        g1 = (KINETIC[0] * CAPACITY[0]) * m1
        g2 = (KINETIC[1] * CAPACITY[1]) * m2
        h = g1 * cover1 + g2 * cover2
        e1 = g1 - h
        e2 = g2 - h
        source = {0: rate1, 1: rate2, 5: -SORPTION_HEAT[0] * rate1 - SORPTION_HEAT[1] * rate2}
        pulled = {
            0: slope1 * e1,
            1: slope2 * e2,
            5: HEAT_EXPONENT[0] * cover1 * e1 + HEAT_EXPONENT[1] * cover2 * e2,
        }
        for k, c in enumerate(MOVING):
            from_x = edge[t, k, b][None]
            from_m = edge[t, len(MOVING) + k, b][None]
            below_x = jnp.where(first == 1, 0.0, from_x)
            above_x = jnp.where(last == 1, 0.0, from_x)
            below_m = jnp.where(first == 1, 0.0, from_m)
            above_m = jnp.where(last == 1, 0.0, from_m)
            r = transport(x[c], shifted(x[c], 1, below_x), shifted(x[c], -1, above_x))
            a = transport(m[c], shifted(m[c], -1, above_m), shifted(m[c], 1, below_m))
            res[t, c, b] = r + source[c] if c in source else r
            adj_at(t, c, b)[...] = a + pulled[c] if c in pulled else a
        res[t, 3, b] = -rate1
        res[t, 4, b] = -rate2
        adj_at(t, 3, b)[...] = -KINETIC[0] * m1
        adj_at(t, 4, b)[...] = -KINETIC[1] * m2
        return carry

    lax.fori_loop(0, instances * beds, cell_block, 0)

    @pl.when(last == 1)
    def _():
        def purge(i, carry):
            t = i // beds
            b = lax.rem(i, beds)
            s = lax.rem(b + plan[t, b], beds)
            gain = PURGE_GAIN * valve[t, b].astype(jnp.float32)
            end = pl.ds(cells - 1, 1)
            for c in range(3):
                res[t, c, b, end] += gain * (both[t, c, b, end] - both[t, c, s, end])
                flow = gain * both[t, comps + c, b, end]
                adj_at(t, c, b, end)[...] += flow
                adj_at(t, c, s, end)[...] -= flow
            return carry

        lax.fori_loop(0, instances * beds, purge, 0)

    sign = jnp.where(odd == 1, -1.0, 1.0)
    at = [jnp.where(odd == 1, instances - 1 - t, t) for t in range(instances)]

    def time_block(out, low, size, factor):
        def step(i, carry):
            c = i // beds
            b = lax.rem(i, beds)
            line = [both[at[t], low + c, b] for t in range(instances)]
            line += [near[at[t], low + c, b] for t in range(instances)]
            for t in range(instances):
                total = 0.0
                for k in range(1, REACH + 1):
                    diff = line[t + k]
                    if t - k >= 0:
                        diff = diff - line[t - k]
                    total = total + WEIGHTS[k - 1] * diff
                out[at[t], c, b] += factor * total
            return carry

        lax.fori_loop(0, size * beds, step, 0)

    time_block(res, 0, comps, sign)
    for n, (low, size) in enumerate(CHUNKS):
        time_block(adj[n], comps + low, size, -sign)


def reach(odd, scale, part, came, b, c):
    instances = part.shape[0]
    sign = jnp.where(odd == 1, -scale, scale)
    at = [jnp.where(odd == 1, instances - 1 - t, t) for t in range(instances)]
    line = [came[at[t], c, b] for t in range(instances)]
    for t in range(instances):
        total = 0.0
        for j in range(t, instances):
            total = total + WEIGHTS[t + instances - j - 1] * line[j]
        yield at[t], part[at[t], c, b] - sign * total


def finish_kernel(flags, part, came, out, flags_after):
    _, comps, beds, _, _ = part.shape
    for i in range(flags.shape[0]):
        flags_after[i] = flags[i]

    def block(i, carry):
        c = i // beds
        b = lax.rem(i, beds)
        for t, value in reach(flags[0], 1.0, part, came, b, c):
            out[t, c, b] = value
        return carry

    lax.fori_loop(0, comps * beds, block, 0)


def finish_chunk_kernel(low, flags, part, came, *rest):
    out, done, sem = rest[-3:]
    _, size, beds, _, _ = part.shape
    copies = []
    for c in range(size):
        for b in range(beds):
            for t, value in reach(flags[0], -1.0, part, came, b, c):
                done[t, c, b] = value
        copy = pltpu.make_async_copy(done.at[:, pl.ds(c, 1)], out.at[:, pl.ds(low + c, 1)], sem.at[c])
        copy.start()
        copies.append(copy)
    for copy in copies:
        copy.wait()


VMEM = pl.BlockSpec(memory_space=pltpu.VMEM)
SMEM = pl.BlockSpec(memory_space=pltpu.SMEM)
ANY = pl.BlockSpec(memory_space=pl.ANY)
HBM = pl.BlockSpec(memory_space=pltpu.HBM)


def params(mib):
    return pltpu.CompilerParams(vmem_limit_bytes=mib * 2**20)


def local(state, adjoint, plan, valve):
    count = lax.axis_size("tm")
    sections = lax.axis_size("sec")
    instances, comps, beds, cells, width = state.shape
    f32 = lambda *shape: jax.ShapeDtypeStruct(shape, jnp.float32)
    block = f32(*state.shape)
    pieces = [f32(instances, size, beds, cells, width) for _, size in CHUNKS]
    swap_out = [(i, (i + 1) % count if i % 2 else (i - 1) % count) for i in range(count)]
    swap_in = [(i, i ^ 1) for i in range(count)]
    out_state = lax.ppermute(state, "tm", swap_out)

    sec = lax.axis_index("sec")
    flags = jnp.stack(
        [lax.axis_index("tm") % 2, (sec == 0).astype(jnp.int32), (sec == sections - 1).astype(jnp.int32)]
    ).astype(jnp.int32)
    both, edge, *sent = pl.pallas_call(
        load_kernel,
        out_shape=[f32(instances, 2 * comps, beds, cells, width), f32(instances, 2 * len(MOVING), beds, width)] + pieces,
        in_specs=[SMEM, HBM, HBM],
        out_specs=[VMEM] * (2 + len(CHUNKS)),
        scratch_shapes=[pltpu.SemaphoreType.DMA((2 + len(CHUNKS),))],
        compiler_params=params(16),
        cost_estimate=pl.CostEstimate(flops=1000, bytes_accessed=1000, transcendentals=0),
        name="load",
    )(flags, state, adjoint)
    out_adjoint = [lax.ppermute(chunk, "tm", swap_out) for chunk in sent]

    def on_chip(both, edge):
        near = lax.ppermute(both, "tm", swap_in)
        far_edge = lax.ppermute(edge, "sec", [(i, i ^ 1) for i in range(sections)])
        return tuple(
            pl.pallas_call(
                main_kernel,
                out_shape=[block] + pieces,
                in_specs=[SMEM] * 3 + [VMEM] * 3,
                out_specs=[VMEM] * (1 + len(CHUNKS)),
                compiler_params=params(24),
                cost_estimate=pl.CostEstimate(flops=1000, bytes_accessed=1000, transcendentals=0),
                name="local_part",
            )(flags, plan, valve, both, far_edge, near)
        )

    def nothing(both, edge):
        return tuple(jnp.zeros(x.shape, x.dtype) for x in [block] + pieces)

    res, *adj = lax.cond(flags[0] >= 0, on_chip, nothing, both, edge)

    residual, flags_after = pl.pallas_call(
        finish_kernel,
        out_shape=(block, jax.ShapeDtypeStruct(flags.shape, flags.dtype)),
        in_specs=[SMEM, VMEM, VMEM],
        out_specs=(VMEM, SMEM),
        compiler_params=params(16),
        cost_estimate=pl.CostEstimate(flops=1000, bytes_accessed=1000, transcendentals=0),
        name="finish_residual",
    )(flags, res, out_state)

    total = ()
    for n, (low, size) in enumerate(CHUNKS):
        total = (
            pl.pallas_call(
                functools.partial(finish_chunk_kernel, low),
                out_shape=block,
                in_specs=[SMEM, VMEM, VMEM] + [ANY] * len(total),
                out_specs=ANY,
                scratch_shapes=[pltpu.VMEM(pieces[n].shape, jnp.float32), pltpu.SemaphoreType.DMA((size,))],
                input_output_aliases={3: 0} if total else {},
                compiler_params=params(16),
                cost_estimate=pl.CostEstimate(flops=1000, bytes_accessed=1000, transcendentals=0),
                name=f"finish_adjoint_{n}",
            )(flags if n else flags_after, adj[n], out_adjoint[n], *total),
        )
    return (residual, total[0])


def solution(mesh):
    spec = P("tm", None, None, "sec", None)
    return jax.shard_map(
        local,
        mesh=mesh,
        in_specs=(spec, spec, P("tm", None), P("tm", None)),
        out_specs=(spec, spec),
        check_vma=False,
    )
```

```python
import functools

import jax
import jax.numpy as jnp
from jax import lax
from jax.experimental import pallas as pl
from jax.experimental.pallas import tpu as pltpu
from jax.sharding import PartitionSpec as P

STENCIL = (0.8, -0.2, 4.0 / 105.0, -1.0 / 280.0)
TIME_SCALE = 4.0
FLOW_VELOCITY = 1.0
AXIAL_DISPERSION = 0.3
RADIAL_SPREADING = 0.2
BINDING_STRENGTH = (1.5, 0.6)
HEAT_EXPONENT = (0.5, 0.3)
KINETIC = (1.2, 0.7)
CAPACITY = (2.0, 1.0)
SORPTION_HEAT = (0.4, 0.25)
PURGE_GAIN = 1.5

REACH = len(STENCIL)
WEIGHTS = tuple(TIME_SCALE * c for c in STENCIL)
MOVING = (0, 1, 2, 5)
CENTRE = FLOW_VELOCITY + 2.0 * AXIAL_DISPERSION + 2.0 * RADIAL_SPREADING
UPWIND = FLOW_VELOCITY + AXIAL_DISPERSION
CHUNKS = ((0, 3), (3, 2), (5, 1))


def is_odd():
    return lax.rem(lax.axis_index("tm"), 2) == 1


def shifted(x, step, edge):
    cells = x.shape[0]
    row = lax.broadcasted_iota(jnp.int32, x.shape, 0)
    if step > 0:
        return jnp.where(row == 0, edge, pltpu.roll(x, 1, 0))
    return jnp.where(row == cells - 1, edge, pltpu.roll(x, cells - 1, 0))


def radial_pair(x):
    width = x.shape[1]
    lane = lax.broadcasted_iota(jnp.int32, x.shape, 1)
    lower = jnp.where(lane == 0, 0.0, pltpu.roll(x, 1, 1))
    upper = jnp.where(lane == width - 1, 0.0, pltpu.roll(x, width - 1, 1))
    return lower + upper


def transport(x, near, far):
    return CENTRE * x - UPWIND * near - AXIAL_DISPERSION * far - RADIAL_SPREADING * radial_pair(x)


def place(c):
    for n, (low, size) in enumerate(CHUNKS):
        if low <= c < low + size:
            return n, c - low


def main_kernel(plan, valve, state, adjoint, edge, in_state, in_adjoint, res, *adj):
    instances, comps, beds, cells, _ = res.shape
    odd = is_odd()
    first = lax.axis_index("sec") == 0
    last = lax.axis_index("sec") == lax.axis_size("sec") - 1

    def adj_at(t, c, *where):
        n, k = place(c)
        return adj[n].at[(t, k) + where]

    def cell_block(i, carry):
        t = i // beds
        b = lax.rem(i, beds)
        x = [state[t, c, b] for c in range(comps)]
        m = [adjoint[t, c, b] for c in range(comps)]
        y1, y2, _, q1, q2, temp = x
        b1 = BINDING_STRENGTH[0] * jnp.exp(HEAT_EXPONENT[0] * temp)
        b2 = BINDING_STRENGTH[1] * jnp.exp(HEAT_EXPONENT[1] * temp)
        over = 1.0 / (1.0 + b1 * y1 + b2 * y2)
        slope1 = b1 * over
        slope2 = b2 * over
        cover1 = slope1 * y1
        cover2 = slope2 * y2
        rate1 = KINETIC[0] * (CAPACITY[0] * cover1 - q1)
        rate2 = KINETIC[1] * (CAPACITY[1] * cover2 - q2)
        m1 = m[0] - m[3] - SORPTION_HEAT[0] * m[5]
        m2 = m[1] - m[4] - SORPTION_HEAT[1] * m[5]
        g1 = (KINETIC[0] * CAPACITY[0]) * m1
        g2 = (KINETIC[1] * CAPACITY[1]) * m2
        h = g1 * cover1 + g2 * cover2
        e1 = g1 - h
        e2 = g2 - h
        source = {0: rate1, 1: rate2, 5: -SORPTION_HEAT[0] * rate1 - SORPTION_HEAT[1] * rate2}
        pulled = {
            0: slope1 * e1,
            1: slope2 * e2,
            5: HEAT_EXPONENT[0] * cover1 * e1 + HEAT_EXPONENT[1] * cover2 * e2,
        }
        for c in MOVING:
            from_x = edge[0, t, c, b][None]
            from_m = edge[1, t, c, b][None]
            below_x = jnp.where(first, 0.0, from_x)
            above_x = jnp.where(last, 0.0, from_x)
            below_m = jnp.where(first, 0.0, from_m)
            above_m = jnp.where(last, 0.0, from_m)
            r = transport(x[c], shifted(x[c], 1, below_x), shifted(x[c], -1, above_x))
            a = transport(m[c], shifted(m[c], -1, above_m), shifted(m[c], 1, below_m))
            res[t, c, b] = r + source[c] if c in source else r
            adj_at(t, c, b)[...] = a + pulled[c] if c in pulled else a
        res[t, 3, b] = -rate1
        res[t, 4, b] = -rate2
        adj_at(t, 3, b)[...] = -KINETIC[0] * m1
        adj_at(t, 4, b)[...] = -KINETIC[1] * m2
        return carry

    lax.fori_loop(0, instances * beds, cell_block, 0)

    @pl.when(last)
    def _():
        def purge(i, carry):
            t = i // beds
            b = lax.rem(i, beds)
            s = lax.rem(b + plan[t, b], beds)
            gain = PURGE_GAIN * valve[t, b].astype(jnp.float32)
            end = pl.ds(cells - 1, 1)
            for c in range(3):
                res[t, c, b, end] += gain * (state[t, c, b, end] - state[t, c, s, end])
                flow = gain * adjoint[t, c, b, end]
                adj_at(t, c, b, end)[...] += flow
                adj_at(t, c, s, end)[...] -= flow
            return carry

        lax.fori_loop(0, instances * beds, purge, 0)

    sign = jnp.where(odd, -1.0, 1.0)
    at = [jnp.where(odd, instances - 1 - t, t) for t in range(instances)]

    def time_block(own, near, out, low, size, factor):
        def step(i, carry):
            c = i // beds
            b = lax.rem(i, beds)
            line = [own[at[t], low + c, b] for t in range(instances)]
            line += [near[at[t], low + c, b] for t in range(instances)]
            for t in range(instances):
                total = 0.0
                for k in range(1, REACH + 1):
                    diff = line[t + k]
                    if t - k >= 0:
                        diff = diff - line[t - k]
                    total = total + WEIGHTS[k - 1] * diff
                out[at[t], c, b] += factor * total
            return carry

        lax.fori_loop(0, size * beds, step, 0)

    time_block(state, in_state, res, 0, comps, sign)
    for n, (low, size) in enumerate(CHUNKS):
        time_block(adjoint, in_adjoint, adj[n], low, size, -sign)


def reach(scale, part, came, b, c):
    instances = part.shape[0]
    odd = is_odd()
    sign = jnp.where(odd, -scale, scale)
    at = [jnp.where(odd, instances - 1 - t, t) for t in range(instances)]
    line = [came[at[t], c, b] for t in range(instances)]
    for t in range(instances):
        total = 0.0
        for j in range(t, instances):
            total = total + WEIGHTS[t + instances - j - 1] * line[j]
        yield at[t], part[at[t], c, b] - sign * total


def finish_kernel(part, came, out, done):
    _, comps, beds, _, _ = part.shape
    done[...] = jnp.zeros_like(done)

    def block(i, carry):
        c = i // beds
        b = lax.rem(i, beds)
        for t, value in reach(1.0, part, came, b, c):
            out[t, c, b] = value
        return carry

    lax.fori_loop(0, comps * beds, block, 0)


def finish_chunk_kernel(low, part, came, *rest):
    out, done, sem = rest[-3:]
    _, size, beds, _, _ = part.shape
    copies = []
    for c in range(size):
        for b in range(beds):
            for t, value in reach(-1.0, part, came, b, c):
                done[t, c, b] = value
        copy = pltpu.make_async_copy(done.at[:, pl.ds(c, 1)], out.at[:, pl.ds(low + c, 1)], sem.at[c])
        copy.start()
        copies.append(copy)
    for copy in copies:
        copy.wait()


VMEM = pl.BlockSpec(memory_space=pltpu.VMEM)
SMEM = pl.BlockSpec(memory_space=pltpu.SMEM)
ANY = pl.BlockSpec(memory_space=pl.ANY)
SMALL = pl.CostEstimate(flops=1000, bytes_accessed=1000, transcendentals=0)


def params(mib):
    return pltpu.CompilerParams(vmem_limit_bytes=mib * 2**20)


def neighbours(count):
    first = {0: -4, 1: 1, 2: -1, 3: 4}
    second = {0: 3, 1: 0, 2: 0, 3: -3}
    return [[(i, (i + hop[i % 4]) % count) for i in range(count)] for hop in (first, second)]


def local(state, adjoint, plan, valve):
    count = lax.axis_size("tm")
    sections = lax.axis_size("sec")
    instances, comps, beds, cells, width = state.shape
    block = jax.ShapeDtypeStruct(state.shape, state.dtype)
    pieces = [jax.ShapeDtypeStruct((instances, size, beds, cells, width), state.dtype) for _, size in CHUNKS]
    hop1, hop2 = neighbours(count)
    on_chip = [(i, i ^ 1) for i in range(count)]
    passed_state = lax.ppermute(state, "tm", hop1)
    passed_adjoint = lax.ppermute(adjoint, "tm", hop1)
    far_state = lax.ppermute(passed_state, "tm", hop2)
    far_adjoint = [lax.ppermute(passed_adjoint[:, low : low + size], "tm", hop2) for low, size in CHUNKS]
    in_state = lax.ppermute(state, "tm", on_chip)
    in_adjoint = lax.ppermute(adjoint, "tm", on_chip)
    sec = lax.axis_index("sec")
    ends = [jnp.where(sec == 0, a[:, :, :, -1], a[:, :, :, 0]) for a in (state, adjoint)]
    edge = lax.ppermute(jnp.stack(ends), "sec", [(i, i ^ 1) for i in range(sections)])

    res, *adj = pl.pallas_call(
        main_kernel,
        out_shape=[block] + pieces,
        in_specs=[SMEM] * 2 + [VMEM] * 5,
        out_specs=[VMEM] * (1 + len(CHUNKS)),
        compiler_params=params(24),
        cost_estimate=SMALL,
        name="local_part",
    )(plan, valve, state, adjoint, edge, in_state, in_adjoint)

    residual, done = pl.pallas_call(
        finish_kernel,
        out_shape=(block, jax.ShapeDtypeStruct((8, 128), jnp.float32)),
        in_specs=[VMEM, VMEM],
        out_specs=(VMEM, VMEM),
        compiler_params=params(16),
        cost_estimate=SMALL,
        name="finish_residual",
    )(res, far_state)

    total = (done,)
    for n, (low, size) in enumerate(CHUNKS):
        total = (
            pl.pallas_call(
                functools.partial(finish_chunk_kernel, low),
                out_shape=block,
                in_specs=[VMEM, VMEM, ANY],
                out_specs=ANY,
                scratch_shapes=[pltpu.VMEM(pieces[n].shape, jnp.float32), pltpu.SemaphoreType.DMA((size,))],
                input_output_aliases={2: 0} if n else {},
                compiler_params=params(16),
                cost_estimate=SMALL,
                name=f"finish_adjoint_{n}",
            )(adj[n], far_adjoint[n], *total),
        )
    return (residual, total[0])


def solution(mesh):
    spec = P("tm", None, None, "sec", None)
    return jax.shard_map(
        local,
        mesh=mesh,
        in_specs=(spec, spec, P("tm", None), P("tm", None)),
        out_specs=(spec, spec),
        check_vma=False,
    )
```

```python
import functools

import jax
import jax.numpy as jnp
from jax import lax
from jax.experimental import pallas as pl
from jax.experimental.pallas import tpu as pltpu
from jax.sharding import PartitionSpec as P

STENCIL = (0.8, -0.2, 4.0 / 105.0, -1.0 / 280.0)
TIME_SCALE = 4.0
FLOW_VELOCITY = 1.0
AXIAL_DISPERSION = 0.3
RADIAL_SPREADING = 0.2
BINDING_STRENGTH = (1.5, 0.6)
HEAT_EXPONENT = (0.5, 0.3)
KINETIC = (1.2, 0.7)
CAPACITY = (2.0, 1.0)
SORPTION_HEAT = (0.4, 0.25)
PURGE_GAIN = 1.5

REACH = len(STENCIL)
WEIGHTS = tuple(TIME_SCALE * c for c in STENCIL)
MOVING = (0, 1, 2, 5)
CENTRE = FLOW_VELOCITY + 2.0 * AXIAL_DISPERSION + 2.0 * RADIAL_SPREADING
UPWIND = FLOW_VELOCITY + AXIAL_DISPERSION
CHUNKS = ((0, 4), (4, 2))


def is_odd():
    return lax.rem(lax.axis_index("tm"), 2) == 1


def shifted(x, step, edge):
    cells = x.shape[0]
    row = lax.broadcasted_iota(jnp.int32, x.shape, 0)
    if step > 0:
        return jnp.where(row == 0, edge, pltpu.roll(x, 1, 0))
    return jnp.where(row == cells - 1, edge, pltpu.roll(x, cells - 1, 0))


def radial_pair(x):
    width = x.shape[1]
    lane = lax.broadcasted_iota(jnp.int32, x.shape, 1)
    lower = jnp.where(lane == 0, 0.0, pltpu.roll(x, 1, 1))
    upper = jnp.where(lane == width - 1, 0.0, pltpu.roll(x, width - 1, 1))
    return lower + upper


def transport(x, near, far):
    return CENTRE * x - UPWIND * near - AXIAL_DISPERSION * far - RADIAL_SPREADING * radial_pair(x)


def place(c):
    for n, (low, size) in enumerate(CHUNKS):
        if low <= c < low + size:
            return n, c - low


def main_kernel(plan, valve, state, adjoint, edge, in_state, in_adjoint, done, res, *adj):
    instances, comps, beds, cells, _ = res.shape
    done[...] = jnp.zeros_like(done)
    odd = is_odd()
    first = lax.axis_index("sec") == 0
    last = lax.axis_index("sec") == lax.axis_size("sec") - 1

    def adj_at(t, c, *where):
        n, k = place(c)
        return adj[n].at[(t, k) + where]

    def cell_block(i, carry):
        t = i // beds
        b = lax.rem(i, beds)
        x = [state[t, c, b] for c in range(comps)]
        m = [adjoint[t, c, b] for c in range(comps)]
        y1, y2, _, q1, q2, temp = x
        b1 = BINDING_STRENGTH[0] * jnp.exp(HEAT_EXPONENT[0] * temp)
        b2 = BINDING_STRENGTH[1] * jnp.exp(HEAT_EXPONENT[1] * temp)
        over = 1.0 / (1.0 + b1 * y1 + b2 * y2)
        slope1 = b1 * over
        slope2 = b2 * over
        cover1 = slope1 * y1
        cover2 = slope2 * y2
        rate1 = KINETIC[0] * (CAPACITY[0] * cover1 - q1)
        rate2 = KINETIC[1] * (CAPACITY[1] * cover2 - q2)
        m1 = m[0] - m[3] - SORPTION_HEAT[0] * m[5]
        m2 = m[1] - m[4] - SORPTION_HEAT[1] * m[5]
        g1 = (KINETIC[0] * CAPACITY[0]) * m1
        g2 = (KINETIC[1] * CAPACITY[1]) * m2
        h = g1 * cover1 + g2 * cover2
        e1 = g1 - h
        e2 = g2 - h
        source = {0: rate1, 1: rate2, 5: -SORPTION_HEAT[0] * rate1 - SORPTION_HEAT[1] * rate2}
        pulled = {
            0: slope1 * e1,
            1: slope2 * e2,
            5: HEAT_EXPONENT[0] * cover1 * e1 + HEAT_EXPONENT[1] * cover2 * e2,
        }
        for c in MOVING:
            from_x = edge[0, t, c, b][None]
            from_m = edge[1, t, c, b][None]
            below_x = jnp.where(first, 0.0, from_x)
            above_x = jnp.where(last, 0.0, from_x)
            below_m = jnp.where(first, 0.0, from_m)
            above_m = jnp.where(last, 0.0, from_m)
            r = transport(x[c], shifted(x[c], 1, below_x), shifted(x[c], -1, above_x))
            a = transport(m[c], shifted(m[c], -1, above_m), shifted(m[c], 1, below_m))
            res[t, c, b] = r + source[c] if c in source else r
            adj_at(t, c, b)[...] = a + pulled[c] if c in pulled else a
        res[t, 3, b] = -rate1
        res[t, 4, b] = -rate2
        adj_at(t, 3, b)[...] = -KINETIC[0] * m1
        adj_at(t, 4, b)[...] = -KINETIC[1] * m2
        return carry

    lax.fori_loop(0, instances * beds, cell_block, 0)

    @pl.when(last)
    def _():
        def purge(i, carry):
            t = i // beds
            b = lax.rem(i, beds)
            s = lax.rem(b + plan[t, b], beds)
            gain = PURGE_GAIN * valve[t, b].astype(jnp.float32)
            end = pl.ds(cells - 1, 1)
            for c in range(3):
                res[t, c, b, end] += gain * (state[t, c, b, end] - state[t, c, s, end])
                flow = gain * adjoint[t, c, b, end]
                adj_at(t, c, b, end)[...] += flow
                adj_at(t, c, s, end)[...] -= flow
            return carry

        lax.fori_loop(0, instances * beds, purge, 0)

    sign = jnp.where(odd, -1.0, 1.0)
    at = [jnp.where(odd, instances - 1 - t, t) for t in range(instances)]

    def time_block(own, near, out, low, size, factor):
        def step(i, carry):
            c = i // beds
            b = lax.rem(i, beds)
            line = [own[at[t], low + c, b] for t in range(instances)]
            line += [near[at[t], low + c, b] for t in range(instances)]
            for t in range(instances):
                total = 0.0
                for k in range(1, REACH + 1):
                    diff = line[t + k]
                    if t - k >= 0:
                        diff = diff - line[t - k]
                    total = total + WEIGHTS[k - 1] * diff
                out[at[t], c, b] += factor * total
            return carry

        lax.fori_loop(0, size * beds, step, 0)

    time_block(state, in_state, res, 0, comps, sign)
    for n, (low, size) in enumerate(CHUNKS):
        time_block(adjoint, in_adjoint, adj[n], low, size, -sign)


def reach(scale, part, came, b, c):
    instances = part.shape[0]
    odd = is_odd()
    sign = jnp.where(odd, -scale, scale)
    at = [jnp.where(odd, instances - 1 - t, t) for t in range(instances)]
    line = [came[at[t], c, b] for t in range(instances)]
    for t in range(instances):
        total = 0.0
        for j in range(t, instances):
            total = total + WEIGHTS[t + instances - j - 1] * line[j]
        yield at[t], part[at[t], c, b] - sign * total


def finish_kernel(part, came, out, done):
    _, comps, beds, _, _ = part.shape
    done[...] = jnp.zeros_like(done)

    def block(i, carry):
        c = i // beds
        b = lax.rem(i, beds)
        for t, value in reach(1.0, part, came, b, c):
            out[t, c, b] = value
        return carry

    lax.fori_loop(0, comps * beds, block, 0)


def finish_chunk_kernel(low, part, came, *rest):
    out, done, sem = rest[-3:]
    _, size, beds, _, _ = part.shape
    copies = []
    for c in range(size):
        for b in range(beds):
            for t, value in reach(-1.0, part, came, b, c):
                done[t, c, b] = value
        copy = pltpu.make_async_copy(done.at[:, pl.ds(c, 1)], out.at[:, pl.ds(low + c, 1)], sem.at[c])
        copy.start()
        copies.append(copy)
    for copy in copies:
        copy.wait()


def after_kernel(passed, done, out):
    del passed, done, out


VMEM = pl.BlockSpec(memory_space=pltpu.VMEM)
SMEM = pl.BlockSpec(memory_space=pltpu.SMEM)
ANY = pl.BlockSpec(memory_space=pl.ANY)
SMALL = pl.CostEstimate(flops=1000, bytes_accessed=1000, transcendentals=0)


def params(mib):
    return pltpu.CompilerParams(vmem_limit_bytes=mib * 2**20)


def neighbours(count):
    first = {0: -4, 1: 1, 2: -1, 3: 4}
    second = {0: 3, 1: 0, 2: 0, 3: -3}
    return [[(i, (i + hop[i % 4]) % count) for i in range(count)] for hop in (first, second)]


def local(state, adjoint, plan, valve):
    count = lax.axis_size("tm")
    sections = lax.axis_size("sec")
    instances, comps, beds, cells, width = state.shape
    block = jax.ShapeDtypeStruct(state.shape, state.dtype)
    pieces = [jax.ShapeDtypeStruct((instances, size, beds, cells, width), state.dtype) for _, size in CHUNKS]
    hop1, hop2 = neighbours(count)
    on_chip = [(i, i ^ 1) for i in range(count)]
    passed_state = lax.ppermute(state, "tm", hop1)
    passed_adjoint = lax.ppermute(adjoint, "tm", hop1)
    in_state = lax.ppermute(state, "tm", on_chip)
    in_adjoint = lax.ppermute(adjoint, "tm", on_chip)
    sec = lax.axis_index("sec")
    ends = [jnp.where(sec == 0, a[:, :, :, -1], a[:, :, :, 0]) for a in (state, adjoint)]
    edge = lax.ppermute(jnp.stack(ends), "sec", [(i, i ^ 1) for i in range(sections)])

    token = jax.ShapeDtypeStruct((8, 128), jnp.float32)
    done, res, *adj = pl.pallas_call(
        main_kernel,
        out_shape=[token, block] + pieces,
        in_specs=[SMEM] * 2 + [VMEM] * 5,
        out_specs=[VMEM] * (2 + len(CHUNKS)),
        compiler_params=params(24),
        cost_estimate=SMALL,
        name="local_part",
    )(plan, valve, state, adjoint, edge, in_state, in_adjoint)

    def after_local(passed, name):
        return pl.pallas_call(
            after_kernel,
            out_shape=block,
            in_specs=[ANY, ANY],
            out_specs=ANY,
            input_output_aliases={0: 0},
            compiler_params=params(1),
            cost_estimate=SMALL,
            name=name,
        )(passed, done)

    far_state = lax.ppermute(after_local(passed_state, "state_after"), "tm", hop2)
    passed_adjoint = after_local(passed_adjoint, "adjoint_after")
    far_adjoint = [lax.ppermute(passed_adjoint[:, low : low + size], "tm", hop2) for low, size in CHUNKS]

    residual, done = pl.pallas_call(
        finish_kernel,
        out_shape=(block, token),
        in_specs=[VMEM, VMEM],
        out_specs=(VMEM, VMEM),
        compiler_params=params(16),
        cost_estimate=SMALL,
        name="finish_residual",
    )(res, far_state)

    total = (done,)
    for n, (low, size) in enumerate(CHUNKS):
        total = (
            pl.pallas_call(
                functools.partial(finish_chunk_kernel, low),
                out_shape=block,
                in_specs=[VMEM, VMEM, ANY],
                out_specs=ANY,
                scratch_shapes=[pltpu.VMEM(pieces[n].shape, jnp.float32), pltpu.SemaphoreType.DMA((size,))],
                input_output_aliases={2: 0} if n else {},
                compiler_params=params(16),
                cost_estimate=SMALL,
                name=f"finish_adjoint_{n}",
            )(adj[n], far_adjoint[n], *total),
        )
    return (residual, total[0])


def solution(mesh):
    spec = P("tm", None, None, "sec", None)
    return jax.shard_map(
        local,
        mesh=mesh,
        in_specs=(spec, spec, P("tm", None), P("tm", None)),
        out_specs=(spec, spec),
        check_vma=False,
    )
```

```python
import functools

import jax
import jax.numpy as jnp
from jax import lax
from jax.experimental import pallas as pl
from jax.experimental.pallas import tpu as pltpu
from jax.sharding import PartitionSpec as P

STENCIL = (0.8, -0.2, 4.0 / 105.0, -1.0 / 280.0)
TIME_SCALE = 4.0
FLOW_VELOCITY = 1.0
AXIAL_DISPERSION = 0.3
RADIAL_SPREADING = 0.2
BINDING_STRENGTH = (1.5, 0.6)
HEAT_EXPONENT = (0.5, 0.3)
KINETIC = (1.2, 0.7)
CAPACITY = (2.0, 1.0)
SORPTION_HEAT = (0.4, 0.25)
PURGE_GAIN = 1.5

REACH = len(STENCIL)
WEIGHTS = tuple(TIME_SCALE * c for c in STENCIL)
MOVING = (0, 1, 2, 5)
CENTRE = FLOW_VELOCITY + 2.0 * AXIAL_DISPERSION + 2.0 * RADIAL_SPREADING
UPWIND = FLOW_VELOCITY + AXIAL_DISPERSION


def is_odd():
    return lax.rem(lax.axis_index("tm"), 2) == 1


def shifted(x, step, edge):
    cells = x.shape[0]
    row = lax.broadcasted_iota(jnp.int32, x.shape, 0)
    if step > 0:
        return jnp.where(row == 0, edge, pltpu.roll(x, 1, 0))
    return jnp.where(row == cells - 1, edge, pltpu.roll(x, cells - 1, 0))


def radial_pair(x):
    width = x.shape[1]
    lane = lax.broadcasted_iota(jnp.int32, x.shape, 1)
    lower = jnp.where(lane == 0, 0.0, pltpu.roll(x, 1, 1))
    upper = jnp.where(lane == width - 1, 0.0, pltpu.roll(x, width - 1, 1))
    return lower + upper


def transport(x, near, far):
    return CENTRE * x - UPWIND * near - AXIAL_DISPERSION * far - RADIAL_SPREADING * radial_pair(x)


def main_kernel(plan, valve, state, adjoint, edge, in_state, in_adjoint, res, adj):
    instances, comps, beds, cells, _ = res.shape
    odd = is_odd()
    first = lax.axis_index("sec") == 0
    last = lax.axis_index("sec") == lax.axis_size("sec") - 1

    def cell_block(i, carry):
        t = i // beds
        b = lax.rem(i, beds)
        x = [state[t, c, b] for c in range(comps)]
        m = [adjoint[t, c, b] for c in range(comps)]
        y1, y2, _, q1, q2, temp = x
        b1 = BINDING_STRENGTH[0] * jnp.exp(HEAT_EXPONENT[0] * temp)
        b2 = BINDING_STRENGTH[1] * jnp.exp(HEAT_EXPONENT[1] * temp)
        over = 1.0 / (1.0 + b1 * y1 + b2 * y2)
        slope1 = b1 * over
        slope2 = b2 * over
        cover1 = slope1 * y1
        cover2 = slope2 * y2
        rate1 = KINETIC[0] * (CAPACITY[0] * cover1 - q1)
        rate2 = KINETIC[1] * (CAPACITY[1] * cover2 - q2)
        m1 = m[0] - m[3] - SORPTION_HEAT[0] * m[5]
        m2 = m[1] - m[4] - SORPTION_HEAT[1] * m[5]
        g1 = (KINETIC[0] * CAPACITY[0]) * m1
        g2 = (KINETIC[1] * CAPACITY[1]) * m2
        h = g1 * cover1 + g2 * cover2
        e1 = g1 - h
        e2 = g2 - h
        source = {0: rate1, 1: rate2, 5: -SORPTION_HEAT[0] * rate1 - SORPTION_HEAT[1] * rate2}
        pulled = {
            0: slope1 * e1,
            1: slope2 * e2,
            5: HEAT_EXPONENT[0] * cover1 * e1 + HEAT_EXPONENT[1] * cover2 * e2,
        }
        for c in MOVING:
            from_x = edge[0, t, c, b][None]
            from_m = edge[1, t, c, b][None]
            below_x = jnp.where(first, 0.0, from_x)
            above_x = jnp.where(last, 0.0, from_x)
            below_m = jnp.where(first, 0.0, from_m)
            above_m = jnp.where(last, 0.0, from_m)
            r = transport(x[c], shifted(x[c], 1, below_x), shifted(x[c], -1, above_x))
            a = transport(m[c], shifted(m[c], -1, above_m), shifted(m[c], 1, below_m))
            res[t, c, b] = r + source[c] if c in source else r
            adj[t, c, b] = a + pulled[c] if c in pulled else a
        res[t, 3, b] = -rate1
        res[t, 4, b] = -rate2
        adj[t, 3, b] = -KINETIC[0] * m1
        adj[t, 4, b] = -KINETIC[1] * m2
        return carry

    lax.fori_loop(0, instances * beds, cell_block, 0)

    @pl.when(last)
    def _():
        def purge(i, carry):
            t = i // beds
            b = lax.rem(i, beds)
            s = lax.rem(b + plan[t, b], beds)
            gain = PURGE_GAIN * valve[t, b].astype(jnp.float32)
            end = pl.ds(cells - 1, 1)
            for c in range(3):
                res[t, c, b, end] += gain * (state[t, c, b, end] - state[t, c, s, end])
                flow = gain * adjoint[t, c, b, end]
                adj[t, c, b, end] += flow
                adj[t, c, s, end] -= flow
            return carry

        lax.fori_loop(0, instances * beds, purge, 0)

    sign = jnp.where(odd, -1.0, 1.0)
    at = [jnp.where(odd, instances - 1 - t, t) for t in range(instances)]

    def time_block(i, carry):
        c = i // beds
        b = lax.rem(i, beds)
        for own, near, out, factor in ((state, in_state, res, sign), (adjoint, in_adjoint, adj, -sign)):
            line = [own[at[t], c, b] for t in range(instances)]
            line += [near[at[t], c, b] for t in range(instances)]
            for t in range(instances):
                total = 0.0
                for k in range(1, REACH + 1):
                    diff = line[t + k]
                    if t - k >= 0:
                        diff = diff - line[t - k]
                    total = total + WEIGHTS[k - 1] * diff
                out[at[t], c, b] += factor * total
        return carry

    lax.fori_loop(0, comps * beds, time_block, 0)


def finish_kernel(scale, part, came, *rest):
    out, whole, sem = rest[-3:]
    instances, comps, beds, _, _ = part.shape
    odd = is_odd()
    sign = jnp.where(odd, -scale, scale)
    at = [jnp.where(odd, instances - 1 - t, t) for t in range(instances)]
    copies = []
    for c in range(comps):
        for b in range(beds):
            line = [came[at[t], c, b] for t in range(instances)]
            for t in range(instances):
                total = 0.0
                for j in range(t, instances):
                    total = total + WEIGHTS[t + instances - j - 1] * line[j]
                whole[at[t], c, b] = part[at[t], c, b] - sign * total
        copy = pltpu.make_async_copy(whole.at[:, pl.ds(c, 1)], out.at[:, pl.ds(c, 1)], sem.at[c])
        copy.start()
        copies.append(copy)
    for copy in copies:
        copy.wait()


VMEM = pl.BlockSpec(memory_space=pltpu.VMEM)
SMEM = pl.BlockSpec(memory_space=pltpu.SMEM)
ANY = pl.BlockSpec(memory_space=pl.ANY)
SMALL = pl.CostEstimate(flops=1000, bytes_accessed=1000, transcendentals=0)


def params(mib):
    return pltpu.CompilerParams(vmem_limit_bytes=mib * 2**20)


def local(state, adjoint, plan, valve):
    count = lax.axis_size("tm")
    sections = lax.axis_size("sec")
    comps = state.shape[1]
    block = jax.ShapeDtypeStruct(state.shape, state.dtype)
    across = [(i, (i + 1) % count if i % 2 else (i - 1) % count) for i in range(count)]
    on_chip = [(i, i ^ 1) for i in range(count)]
    far_state = lax.ppermute(state, "tm", across)
    far_adjoint = lax.ppermute(adjoint, "tm", across)

    def local_part():
        in_state = lax.ppermute(state, "tm", on_chip)
        in_adjoint = lax.ppermute(adjoint, "tm", on_chip)
        sec = lax.axis_index("sec")
        ends = [jnp.where(sec == 0, a[:, :, :, -1], a[:, :, :, 0]) for a in (state, adjoint)]
        edge = lax.ppermute(jnp.stack(ends), "sec", [(i, i ^ 1) for i in range(sections)])
        return pl.pallas_call(
            main_kernel,
            out_shape=(block, block),
            in_specs=[SMEM] * 2 + [VMEM] * 5,
            out_specs=(VMEM, VMEM),
            compiler_params=params(24),
            cost_estimate=SMALL,
            name="local_part",
        )(plan, valve, state, adjoint, edge, in_state, in_adjoint)

    res, adj = lax.cond(
        lax.axis_index("tm") % 2 >= 0, local_part, lambda: (jnp.zeros_like(state), jnp.zeros_like(adjoint))
    )

    def finish(scale, name, *operands):
        return pl.pallas_call(
            functools.partial(finish_kernel, scale),
            out_shape=block,
            in_specs=[VMEM, VMEM] + [ANY] * (len(operands) - 2),
            out_specs=ANY,
            scratch_shapes=[pltpu.VMEM(block.shape, block.dtype), pltpu.SemaphoreType.DMA((comps,))],
            compiler_params=params(16),
            cost_estimate=SMALL,
            name=name,
        )(*operands)

    return finish(1.0, "finish_residual", res, far_state), finish(-1.0, "finish_adjoint", adj, far_adjoint)


def solution(mesh):
    spec = P("tm", None, None, "sec", None)
    return jax.shard_map(
        local,
        mesh=mesh,
        in_specs=(spec, spec, P("tm", None), P("tm", None)),
        out_specs=(spec, spec),
        check_vma=False,
    )
```

```python
import functools

import jax
import jax.numpy as jnp
from jax import lax
from jax.experimental import pallas as pl
from jax.experimental.pallas import tpu as pltpu
from jax.sharding import PartitionSpec as P

STENCIL = (0.8, -0.2, 4.0 / 105.0, -1.0 / 280.0)
TIME_SCALE = 4.0
FLOW_VELOCITY = 1.0
AXIAL_DISPERSION = 0.3
RADIAL_SPREADING = 0.2
BINDING_STRENGTH = (1.5, 0.6)
HEAT_EXPONENT = (0.5, 0.3)
KINETIC = (1.2, 0.7)
CAPACITY = (2.0, 1.0)
SORPTION_HEAT = (0.4, 0.25)
PURGE_GAIN = 1.5

REACH = len(STENCIL)
WEIGHTS = tuple(TIME_SCALE * c for c in STENCIL)
MOVING = (0, 1, 2, 5)
CENTRE = FLOW_VELOCITY + 2.0 * AXIAL_DISPERSION + 2.0 * RADIAL_SPREADING
UPWIND = FLOW_VELOCITY + AXIAL_DISPERSION


def is_odd():
    return lax.rem(lax.axis_index("tm"), 2) == 1


def shifted(x, step, edge):
    cells = x.shape[0]
    row = lax.broadcasted_iota(jnp.int32, x.shape, 0)
    if step > 0:
        return jnp.where(row == 0, edge, pltpu.roll(x, 1, 0))
    return jnp.where(row == cells - 1, edge, pltpu.roll(x, cells - 1, 0))


def radial_pair(x):
    width = x.shape[1]
    lane = lax.broadcasted_iota(jnp.int32, x.shape, 1)
    lower = jnp.where(lane == 0, 0.0, pltpu.roll(x, 1, 1))
    upper = jnp.where(lane == width - 1, 0.0, pltpu.roll(x, width - 1, 1))
    return lower + upper


def transport(x, near, far):
    return CENTRE * x - UPWIND * near - AXIAL_DISPERSION * far - RADIAL_SPREADING * radial_pair(x)


def main_kernel(plan, valve, state, adjoint, edge, in_state, in_adjoint, res, adj):
    instances, comps, beds, cells, _ = res.shape
    odd = is_odd()
    first = lax.axis_index("sec") == 0
    last = lax.axis_index("sec") == lax.axis_size("sec") - 1

    def cell_block(i, carry):
        t = i // beds
        b = lax.rem(i, beds)
        x = [state[t, c, b] for c in range(comps)]
        m = [adjoint[t, c, b] for c in range(comps)]
        y1, y2, _, q1, q2, temp = x
        b1 = BINDING_STRENGTH[0] * jnp.exp(HEAT_EXPONENT[0] * temp)
        b2 = BINDING_STRENGTH[1] * jnp.exp(HEAT_EXPONENT[1] * temp)
        over = 1.0 / (1.0 + b1 * y1 + b2 * y2)
        slope1 = b1 * over
        slope2 = b2 * over
        cover1 = slope1 * y1
        cover2 = slope2 * y2
        rate1 = KINETIC[0] * (CAPACITY[0] * cover1 - q1)
        rate2 = KINETIC[1] * (CAPACITY[1] * cover2 - q2)
        m1 = m[0] - m[3] - SORPTION_HEAT[0] * m[5]
        m2 = m[1] - m[4] - SORPTION_HEAT[1] * m[5]
        g1 = (KINETIC[0] * CAPACITY[0]) * m1
        g2 = (KINETIC[1] * CAPACITY[1]) * m2
        h = g1 * cover1 + g2 * cover2
        e1 = g1 - h
        e2 = g2 - h
        source = {0: rate1, 1: rate2, 5: -SORPTION_HEAT[0] * rate1 - SORPTION_HEAT[1] * rate2}
        pulled = {
            0: slope1 * e1,
            1: slope2 * e2,
            5: HEAT_EXPONENT[0] * cover1 * e1 + HEAT_EXPONENT[1] * cover2 * e2,
        }
        for c in MOVING:
            from_x = edge[0, t, c, b][None]
            from_m = edge[1, t, c, b][None]
            below_x = jnp.where(first, 0.0, from_x)
            above_x = jnp.where(last, 0.0, from_x)
            below_m = jnp.where(first, 0.0, from_m)
            above_m = jnp.where(last, 0.0, from_m)
            r = transport(x[c], shifted(x[c], 1, below_x), shifted(x[c], -1, above_x))
            a = transport(m[c], shifted(m[c], -1, above_m), shifted(m[c], 1, below_m))
            res[t, c, b] = r + source[c] if c in source else r
            adj[t, c, b] = a + pulled[c] if c in pulled else a
        res[t, 3, b] = -rate1
        res[t, 4, b] = -rate2
        adj[t, 3, b] = -KINETIC[0] * m1
        adj[t, 4, b] = -KINETIC[1] * m2
        return carry

    lax.fori_loop(0, instances * beds, cell_block, 0)

    @pl.when(last)
    def _():
        def purge(i, carry):
            t = i // beds
            b = lax.rem(i, beds)
            s = lax.rem(b + plan[t, b], beds)
            gain = PURGE_GAIN * valve[t, b].astype(jnp.float32)
            end = pl.ds(cells - 1, 1)
            for c in range(3):
                res[t, c, b, end] += gain * (state[t, c, b, end] - state[t, c, s, end])
                flow = gain * adjoint[t, c, b, end]
                adj[t, c, b, end] += flow
                adj[t, c, s, end] -= flow
            return carry

        lax.fori_loop(0, instances * beds, purge, 0)

    sign = jnp.where(odd, -1.0, 1.0)
    at = [jnp.where(odd, instances - 1 - t, t) for t in range(instances)]

    def time_block(i, carry):
        c = i // beds
        b = lax.rem(i, beds)
        for own, near, out, factor in ((state, in_state, res, sign), (adjoint, in_adjoint, adj, -sign)):
            line = [own[at[t], c, b] for t in range(instances)]
            line += [near[at[t], c, b] for t in range(instances)]
            for t in range(instances):
                total = 0.0
                for k in range(1, REACH + 1):
                    diff = line[t + k]
                    if t - k >= 0:
                        diff = diff - line[t - k]
                    total = total + WEIGHTS[k - 1] * diff
                out[at[t], c, b] += factor * total
        return carry

    lax.fori_loop(0, comps * beds, time_block, 0)


def finish_kernel(scale, part, came, out, whole, sem):
    instances, comps, beds, _, _ = part.shape

    def moved(c):
        return pltpu.make_async_copy(whole.at[:, pl.ds(c, 1)], out.at[:, pl.ds(c, 1)], sem.at[c])

    def finish(sign, at):
        def component(c, carry):
            for b in range(beds):
                line = [came[at[t], c, b] for t in range(instances)]
                for t in range(instances):
                    total = part[at[t], c, b]
                    for j in range(t, instances):
                        total = total - sign * WEIGHTS[t + instances - j - 1] * line[j]
                    whole[at[t], c, b] = total
            moved(c).start()
            return carry

        lax.fori_loop(0, comps, component, 0)

    odd = is_odd()

    @pl.when(odd)
    def _():
        finish(-scale, list(reversed(range(instances))))

    @pl.when(jnp.logical_not(odd))
    def _():
        finish(scale, list(range(instances)))

    for c in range(comps):
        moved(c).wait()


VMEM = pl.BlockSpec(memory_space=pltpu.VMEM)
SMEM = pl.BlockSpec(memory_space=pltpu.SMEM)
ANY = pl.BlockSpec(memory_space=pl.ANY)
SMALL = pl.CostEstimate(flops=1000, bytes_accessed=1000, transcendentals=0)


def params(mib):
    return pltpu.CompilerParams(vmem_limit_bytes=mib * 2**20)


def local(state, adjoint, plan, valve):
    count = lax.axis_size("tm")
    sections = lax.axis_size("sec")
    comps = state.shape[1]
    block = jax.ShapeDtypeStruct(state.shape, state.dtype)
    across = [(i, (i + 1) % count if i % 2 else (i - 1) % count) for i in range(count)]
    on_chip = [(i, i ^ 1) for i in range(count)]
    far_state = lax.ppermute(state, "tm", across)
    far_adjoint = lax.ppermute(adjoint, "tm", across)

    def local_part():
        in_state = lax.ppermute(state, "tm", on_chip)
        in_adjoint = lax.ppermute(adjoint, "tm", on_chip)
        sec = lax.axis_index("sec")
        ends = [jnp.where(sec == 0, a[:, :, :, -1], a[:, :, :, 0]) for a in (state, adjoint)]
        edge = lax.ppermute(jnp.stack(ends), "sec", [(i, i ^ 1) for i in range(sections)])
        return pl.pallas_call(
            main_kernel,
            out_shape=(block, block),
            in_specs=[SMEM] * 2 + [VMEM] * 5,
            out_specs=(VMEM, VMEM),
            compiler_params=params(24),
            cost_estimate=SMALL,
            name="local_part",
        )(plan, valve, state, adjoint, edge, in_state, in_adjoint)

    res, adj = lax.cond(
        lax.axis_index("tm") % 2 >= 0, local_part, lambda: (jnp.zeros_like(state), jnp.zeros_like(adjoint))
    )

    def finish(scale, name, part, came):
        return pl.pallas_call(
            functools.partial(finish_kernel, scale),
            out_shape=block,
            in_specs=[VMEM, VMEM],
            out_specs=ANY,
            scratch_shapes=[pltpu.VMEM(block.shape, block.dtype), pltpu.SemaphoreType.DMA((comps,))],
            compiler_params=params(16),
            cost_estimate=SMALL,
            name=name,
        )(part, came)

    return finish(1.0, "finish_residual", res, far_state), finish(-1.0, "finish_adjoint", adj, far_adjoint)


def solution(mesh):
    spec = P("tm", None, None, "sec", None)
    return jax.shard_map(
        local,
        mesh=mesh,
        in_specs=(spec, spec, P("tm", None), P("tm", None)),
        out_specs=(spec, spec),
        check_vma=False,
    )
```

```python
import functools

import jax
import jax.numpy as jnp
from jax import lax
from jax.experimental import pallas as pl
from jax.experimental.pallas import tpu as pltpu
from jax.sharding import PartitionSpec as P

STENCIL = (0.8, -0.2, 4.0 / 105.0, -1.0 / 280.0)
TIME_SCALE = 4.0
FLOW_VELOCITY = 1.0
AXIAL_DISPERSION = 0.3
RADIAL_SPREADING = 0.2
BINDING_STRENGTH = (1.5, 0.6)
HEAT_EXPONENT = (0.5, 0.3)
KINETIC = (1.2, 0.7)
CAPACITY = (2.0, 1.0)
SORPTION_HEAT = (0.4, 0.25)
PURGE_GAIN = 1.5

REACH = len(STENCIL)
WEIGHTS = tuple(TIME_SCALE * c for c in STENCIL)
MOVING = (0, 1, 2, 5)
CENTRE = FLOW_VELOCITY + 2.0 * AXIAL_DISPERSION + 2.0 * RADIAL_SPREADING
UPWIND = FLOW_VELOCITY + AXIAL_DISPERSION


def is_odd():
    return lax.rem(lax.axis_index("tm"), 2) == 1


def shifted(x, step, edge):
    cells = x.shape[0]
    row = lax.broadcasted_iota(jnp.int32, x.shape, 0)
    if step > 0:
        return jnp.where(row == 0, edge, pltpu.roll(x, 1, 0))
    return jnp.where(row == cells - 1, edge, pltpu.roll(x, cells - 1, 0))


def radial_pair(x):
    width = x.shape[1]
    lane = lax.broadcasted_iota(jnp.int32, x.shape, 1)
    lower = jnp.where(lane == 0, 0.0, pltpu.roll(x, 1, 1))
    upper = jnp.where(lane == width - 1, 0.0, pltpu.roll(x, width - 1, 1))
    return lower + upper


def transport(x, near, far):
    return CENTRE * x - UPWIND * near - AXIAL_DISPERSION * far - RADIAL_SPREADING * radial_pair(x)


def main_kernel(plan, valve, state, adjoint, edge, in_state, in_adjoint, res, adj):
    instances, comps, beds, cells, _ = res.shape
    odd = is_odd()
    first = lax.axis_index("sec") == 0
    last = lax.axis_index("sec") == lax.axis_size("sec") - 1

    def cell_block(i, carry):
        t = i // beds
        b = lax.rem(i, beds)
        x = [state[t, c, b] for c in range(comps)]
        m = [adjoint[t, c, b] for c in range(comps)]
        y1, y2, _, q1, q2, temp = x
        b1 = BINDING_STRENGTH[0] * jnp.exp(HEAT_EXPONENT[0] * temp)
        b2 = BINDING_STRENGTH[1] * jnp.exp(HEAT_EXPONENT[1] * temp)
        over = 1.0 / (1.0 + b1 * y1 + b2 * y2)
        slope1 = b1 * over
        slope2 = b2 * over
        cover1 = slope1 * y1
        cover2 = slope2 * y2
        rate1 = KINETIC[0] * (CAPACITY[0] * cover1 - q1)
        rate2 = KINETIC[1] * (CAPACITY[1] * cover2 - q2)
        m1 = m[0] - m[3] - SORPTION_HEAT[0] * m[5]
        m2 = m[1] - m[4] - SORPTION_HEAT[1] * m[5]
        g1 = (KINETIC[0] * CAPACITY[0]) * m1
        g2 = (KINETIC[1] * CAPACITY[1]) * m2
        h = g1 * cover1 + g2 * cover2
        e1 = g1 - h
        e2 = g2 - h
        source = {0: rate1, 1: rate2, 5: -SORPTION_HEAT[0] * rate1 - SORPTION_HEAT[1] * rate2}
        pulled = {
            0: slope1 * e1,
            1: slope2 * e2,
            5: HEAT_EXPONENT[0] * cover1 * e1 + HEAT_EXPONENT[1] * cover2 * e2,
        }
        for c in MOVING:
            from_x = edge[0, t, c, b][None]
            from_m = edge[1, t, c, b][None]
            below_x = jnp.where(first, 0.0, from_x)
            above_x = jnp.where(last, 0.0, from_x)
            below_m = jnp.where(first, 0.0, from_m)
            above_m = jnp.where(last, 0.0, from_m)
            r = transport(x[c], shifted(x[c], 1, below_x), shifted(x[c], -1, above_x))
            a = transport(m[c], shifted(m[c], -1, above_m), shifted(m[c], 1, below_m))
            res[t, c, b] = r + source[c] if c in source else r
            adj[t, c, b] = a + pulled[c] if c in pulled else a
        res[t, 3, b] = -rate1
        res[t, 4, b] = -rate2
        adj[t, 3, b] = -KINETIC[0] * m1
        adj[t, 4, b] = -KINETIC[1] * m2
        return carry

    lax.fori_loop(0, instances * beds, cell_block, 0)

    @pl.when(last)
    def _():
        def purge(i, carry):
            t = i // beds
            b = lax.rem(i, beds)
            s = lax.rem(b + plan[t, b], beds)
            gain = PURGE_GAIN * valve[t, b].astype(jnp.float32)
            end = pl.ds(cells - 1, 1)
            for c in range(3):
                res[t, c, b, end] += gain * (state[t, c, b, end] - state[t, c, s, end])
                flow = gain * adjoint[t, c, b, end]
                adj[t, c, b, end] += flow
                adj[t, c, s, end] -= flow
            return carry

        lax.fori_loop(0, instances * beds, purge, 0)

    sign = jnp.where(odd, -1.0, 1.0)
    at = [jnp.where(odd, instances - 1 - t, t) for t in range(instances)]

    def time_block(i, carry):
        c = i // beds
        b = lax.rem(i, beds)
        for own, near, out, factor in ((state, in_state, res, sign), (adjoint, in_adjoint, adj, -sign)):
            line = [own[at[t], c, b] for t in range(instances)]
            line += [near[at[t], c, b] for t in range(instances)]
            for t in range(instances):
                total = 0.0
                for k in range(1, REACH + 1):
                    diff = line[t + k]
                    if t - k >= 0:
                        diff = diff - line[t - k]
                    total = total + WEIGHTS[k - 1] * diff
                out[at[t], c, b] += factor * total
        return carry

    lax.fori_loop(0, comps * beds, time_block, 0)


def finish_kernel(scale, part, came, out, whole, sem):
    instances, comps, beds, _, _ = part.shape

    def moved(c):
        return pltpu.make_async_copy(whole.at[:, pl.ds(c, 1)], out.at[:, pl.ds(c, 1)], sem.at[c])

    def finish(sign, at):
        def component(c, carry):
            for b in range(beds):
                line = [came[at[t], c, b] for t in range(instances)]
                for t in range(instances):
                    total = part[at[t], c, b]
                    for j in range(t, instances):
                        total = total - sign * WEIGHTS[t + instances - j - 1] * line[j]
                    whole[at[t], c, b] = total
            moved(c).start()
            return carry

        lax.fori_loop(0, comps, component, 0)

    odd = is_odd()

    @pl.when(odd)
    def _():
        finish(-scale, list(reversed(range(instances))))

    @pl.when(jnp.logical_not(odd))
    def _():
        finish(scale, list(range(instances)))

    for c in range(comps):
        moved(c).wait()


VMEM = pl.BlockSpec(memory_space=pltpu.VMEM)
SMEM = pl.BlockSpec(memory_space=pltpu.SMEM)
ANY = pl.BlockSpec(memory_space=pl.ANY)
SMALL = pl.CostEstimate(flops=1000, bytes_accessed=1000, transcendentals=0)


def params(mib):
    return pltpu.CompilerParams(vmem_limit_bytes=mib * 2**20)


def local(state, adjoint, plan, valve):
    count = lax.axis_size("tm")
    sections = lax.axis_size("sec")
    comps = state.shape[1]
    block = jax.ShapeDtypeStruct(state.shape, state.dtype)
    across = [(i, (i + 1) % count if i % 2 else (i - 1) % count) for i in range(count)]
    on_chip = [(i, i ^ 1) for i in range(count)]
    far_state = lax.ppermute(state, "tm", across)
    far_adjoint = lax.ppermute(adjoint, "tm", across)

    def near_transfers():
        in_state = lax.ppermute(state, "tm", on_chip)
        in_adjoint = lax.ppermute(adjoint, "tm", on_chip)
        sec = lax.axis_index("sec")
        ends = [jnp.where(sec == 0, a[:, :, :, -1], a[:, :, :, 0]) for a in (state, adjoint)]
        edge = lax.ppermute(jnp.stack(ends), "sec", [(i, i ^ 1) for i in range(sections)])
        return edge, in_state, in_adjoint

    def nothing():
        return jnp.zeros((2,) + state.shape[:3] + state.shape[4:], state.dtype), state, adjoint

    near = lax.cond(lax.axis_index("tm") % 2 >= 0, near_transfers, nothing)
    res, adj = pl.pallas_call(
        main_kernel,
        out_shape=(block, block),
        in_specs=[SMEM] * 2 + [VMEM] * 5,
        out_specs=(VMEM, VMEM),
        compiler_params=params(24),
        cost_estimate=SMALL,
        name="local_part",
    )(plan, valve, state, adjoint, *near)

    def finish(scale, name, part, came):
        return pl.pallas_call(
            functools.partial(finish_kernel, scale),
            out_shape=block,
            in_specs=[VMEM, VMEM],
            out_specs=ANY,
            scratch_shapes=[pltpu.VMEM(block.shape, block.dtype), pltpu.SemaphoreType.DMA((comps,))],
            compiler_params=params(16),
            cost_estimate=SMALL,
            name=name,
        )(part, came)

    return finish(1.0, "finish_residual", res, far_state), finish(-1.0, "finish_adjoint", adj, far_adjoint)


def solution(mesh):
    spec = P("tm", None, None, "sec", None)
    return jax.shard_map(
        local,
        mesh=mesh,
        in_specs=(spec, spec, P("tm", None), P("tm", None)),
        out_specs=(spec, spec),
        check_vma=False,
    )
```

```python
import functools

import jax
import jax.numpy as jnp
from jax import lax
from jax.experimental import pallas as pl
from jax.experimental.pallas import tpu as pltpu
from jax.sharding import PartitionSpec as P

STENCIL = (0.8, -0.2, 4.0 / 105.0, -1.0 / 280.0)
TIME_SCALE = 4.0
FLOW_VELOCITY = 1.0
AXIAL_DISPERSION = 0.3
RADIAL_SPREADING = 0.2
BINDING_STRENGTH = (1.5, 0.6)
HEAT_EXPONENT = (0.5, 0.3)
KINETIC = (1.2, 0.7)
CAPACITY = (2.0, 1.0)
SORPTION_HEAT = (0.4, 0.25)
PURGE_GAIN = 1.5

REACH = len(STENCIL)
WEIGHTS = tuple(TIME_SCALE * c for c in STENCIL)
MOVING = (0, 1, 2, 5)
CENTRE = FLOW_VELOCITY + 2.0 * AXIAL_DISPERSION + 2.0 * RADIAL_SPREADING
UPWIND = FLOW_VELOCITY + AXIAL_DISPERSION


def is_odd():
    return lax.rem(lax.axis_index("tm"), 2) == 1


def is_inner():
    place = lax.rem(lax.axis_index("tm"), 4)
    return jnp.logical_or(place == 1, place == 2)


def shifted(x, step, edge):
    cells = x.shape[0]
    row = lax.broadcasted_iota(jnp.int32, x.shape, 0)
    if step > 0:
        return jnp.where(row == 0, edge, pltpu.roll(x, 1, 0))
    return jnp.where(row == cells - 1, edge, pltpu.roll(x, cells - 1, 0))


def radial_pair(x):
    width = x.shape[1]
    lane = lax.broadcasted_iota(jnp.int32, x.shape, 1)
    lower = jnp.where(lane == 0, 0.0, pltpu.roll(x, 1, 1))
    upper = jnp.where(lane == width - 1, 0.0, pltpu.roll(x, width - 1, 1))
    return lower + upper


def transport(x, near, far):
    return CENTRE * x - UPWIND * near - AXIAL_DISPERSION * far - RADIAL_SPREADING * radial_pair(x)


def pick_kernel(state, adjoint, edge):
    instances, _, beds, cells, _ = state.shape
    first = lax.axis_index("sec") == 0

    def step(t, carry):
        for n, x in enumerate((state, adjoint)):
            for k, c in enumerate(MOVING):
                for b in range(beds):
                    row = jnp.where(first, x[t, c, b, cells - 1 :], x[t, c, b, :1])
                    edge[t, n * len(MOVING) + k, b : b + 1] = row
        return carry

    lax.fori_loop(0, instances, step, 0)


def main_kernel(plan, valve, state, adjoint, *refs):
    refs, res, adj = refs[:-2], refs[-2], refs[-1]
    instances, comps, beds, cells, _ = res.shape
    odd = is_odd()
    inner = is_inner()

    def take(n, *where):
        return jnp.where(inner, refs[n][where], refs[n + 3][where])

    first = lax.axis_index("sec") == 0
    last = lax.axis_index("sec") == lax.axis_size("sec") - 1

    def cell_block(i, carry):
        t = i // beds
        b = lax.rem(i, beds)
        x = [state[t, c, b] for c in range(comps)]
        m = [adjoint[t, c, b] for c in range(comps)]
        y1, y2, _, q1, q2, temp = x
        b1 = BINDING_STRENGTH[0] * jnp.exp(HEAT_EXPONENT[0] * temp)
        b2 = BINDING_STRENGTH[1] * jnp.exp(HEAT_EXPONENT[1] * temp)
        over = 1.0 / (1.0 + b1 * y1 + b2 * y2)
        slope1 = b1 * over
        slope2 = b2 * over
        cover1 = slope1 * y1
        cover2 = slope2 * y2
        rate1 = KINETIC[0] * (CAPACITY[0] * cover1 - q1)
        rate2 = KINETIC[1] * (CAPACITY[1] * cover2 - q2)
        m1 = m[0] - m[3] - SORPTION_HEAT[0] * m[5]
        m2 = m[1] - m[4] - SORPTION_HEAT[1] * m[5]
        g1 = (KINETIC[0] * CAPACITY[0]) * m1
        g2 = (KINETIC[1] * CAPACITY[1]) * m2
        h = g1 * cover1 + g2 * cover2
        e1 = g1 - h
        e2 = g2 - h
        source = {0: rate1, 1: rate2, 5: -SORPTION_HEAT[0] * rate1 - SORPTION_HEAT[1] * rate2}
        pulled = {
            0: slope1 * e1,
            1: slope2 * e2,
            5: HEAT_EXPONENT[0] * cover1 * e1 + HEAT_EXPONENT[1] * cover2 * e2,
        }
        for k, c in enumerate(MOVING):
            from_x = take(0, t, k, b)[None]
            from_m = take(0, t, len(MOVING) + k, b)[None]
            below_x = jnp.where(first, 0.0, from_x)
            above_x = jnp.where(last, 0.0, from_x)
            below_m = jnp.where(first, 0.0, from_m)
            above_m = jnp.where(last, 0.0, from_m)
            r = transport(x[c], shifted(x[c], 1, below_x), shifted(x[c], -1, above_x))
            a = transport(m[c], shifted(m[c], -1, above_m), shifted(m[c], 1, below_m))
            res[t, c, b] = r + source[c] if c in source else r
            adj[t, c, b] = a + pulled[c] if c in pulled else a
        res[t, 3, b] = -rate1
        res[t, 4, b] = -rate2
        adj[t, 3, b] = -KINETIC[0] * m1
        adj[t, 4, b] = -KINETIC[1] * m2
        return carry

    lax.fori_loop(0, instances * beds, cell_block, 0)

    @pl.when(last)
    def _():
        def purge(i, carry):
            t = i // beds
            b = lax.rem(i, beds)
            s = lax.rem(b + plan[t, b], beds)
            gain = PURGE_GAIN * valve[t, b].astype(jnp.float32)
            end = pl.ds(cells - 1, 1)
            for c in range(3):
                res[t, c, b, end] += gain * (state[t, c, b, end] - state[t, c, s, end])
                flow = gain * adjoint[t, c, b, end]
                adj[t, c, b, end] += flow
                adj[t, c, s, end] -= flow
            return carry

        lax.fori_loop(0, instances * beds, purge, 0)

    sign = jnp.where(odd, -1.0, 1.0)
    at = [jnp.where(odd, instances - 1 - t, t) for t in range(instances)]

    def time_block(i, carry):
        c = i // beds
        b = lax.rem(i, beds)
        for own, near, out, factor in ((state, 1, res, sign), (adjoint, 2, adj, -sign)):
            line = [own[at[t], c, b] for t in range(instances)]
            line += [take(near, at[t], c, b) for t in range(instances)]
            for t in range(instances):
                total = 0.0
                for k in range(1, REACH + 1):
                    diff = line[t + k]
                    if t - k >= 0:
                        diff = diff - line[t - k]
                    total = total + WEIGHTS[k - 1] * diff
                out[at[t], c, b] += factor * total
        return carry

    lax.fori_loop(0, comps * beds, time_block, 0)


def finish_kernel(scale, part, came, out, whole, sem):
    instances, comps, beds, _, _ = part.shape

    def moved(c):
        return pltpu.make_async_copy(whole.at[:, pl.ds(c, 1)], out.at[:, pl.ds(c, 1)], sem.at[c])

    def finish(sign, at):
        def component(c, carry):
            for b in range(beds):
                line = [came[at[t], c, b] for t in range(instances)]
                for t in range(instances):
                    total = part[at[t], c, b]
                    for j in range(t, instances):
                        total = total - sign * WEIGHTS[t + instances - j - 1] * line[j]
                    whole[at[t], c, b] = total
            moved(c).start()
            return carry

        lax.fori_loop(0, comps, component, 0)

    odd = is_odd()

    @pl.when(odd)
    def _():
        finish(-scale, list(reversed(range(instances))))

    @pl.when(jnp.logical_not(odd))
    def _():
        finish(scale, list(range(instances)))

    for c in range(comps):
        moved(c).wait()


VMEM = pl.BlockSpec(memory_space=pltpu.VMEM)
SMEM = pl.BlockSpec(memory_space=pltpu.SMEM)
ANY = pl.BlockSpec(memory_space=pl.ANY)
SMALL = pl.CostEstimate(flops=1000, bytes_accessed=1000, transcendentals=0)


def params(mib):
    return pltpu.CompilerParams(vmem_limit_bytes=mib * 2**20)


def local(state, adjoint, plan, valve):
    count = lax.axis_size("tm")
    sections = lax.axis_size("sec")
    instances, comps, beds, cells, width = state.shape
    block = jax.ShapeDtypeStruct(state.shape, state.dtype)
    across = [(i, (i + 1) % count if i % 2 else (i - 1) % count) for i in range(count)]
    far_state = lax.ppermute(state, "tm", across)
    far_adjoint = lax.ppermute(adjoint, "tm", across)

    def near(kind, edge):
        senders = [i for i in range(count) if i % 4 in kind]
        on_chip = [(i, i ^ 1) for i in senders]
        over = [(i * sections + j, i * sections + (j ^ 1)) for i in senders for j in range(sections)]
        return (
            lax.ppermute(edge, ("tm", "sec"), over),
            lax.ppermute(state, "tm", on_chip),
            lax.ppermute(adjoint, "tm", on_chip),
        )

    def from_inner():
        edge = pl.pallas_call(
            pick_kernel,
            out_shape=jax.ShapeDtypeStruct((instances, 2 * len(MOVING), beds, width), state.dtype),
            in_specs=[VMEM, VMEM],
            out_specs=VMEM,
            compiler_params=params(16),
            cost_estimate=SMALL,
            name="pick",
        )(state, adjoint)
        return edge, *near((1, 2), edge)

    def unsent():
        edge = jnp.zeros((instances, 2 * len(MOVING), beds, width), state.dtype)
        return edge, edge, state, adjoint

    always = lax.axis_index("tm") % 2 >= 0
    edge, edge_inner, state_outer, adjoint_outer = lax.cond(always, from_inner, unsent)
    edge_outer, state_inner, adjoint_inner = lax.cond(
        always, lambda edge: near((0, 3), edge), lambda edge: (edge, state, adjoint), edge
    )
    res, adj = pl.pallas_call(
        main_kernel,
        out_shape=(block, block),
        in_specs=[SMEM] * 2 + [VMEM] * 8,
        out_specs=(VMEM, VMEM),
        compiler_params=params(24),
        cost_estimate=SMALL,
        name="local_part",
    )(plan, valve, state, adjoint, edge_inner, state_inner, adjoint_inner, edge_outer, state_outer, adjoint_outer)

    def finish(scale, name, part, came):
        return pl.pallas_call(
            functools.partial(finish_kernel, scale),
            out_shape=block,
            in_specs=[VMEM, VMEM],
            out_specs=ANY,
            scratch_shapes=[pltpu.VMEM(block.shape, block.dtype), pltpu.SemaphoreType.DMA((comps,))],
            compiler_params=params(16),
            cost_estimate=SMALL,
            name=name,
        )(part, came)

    return finish(1.0, "finish_residual", res, far_state), finish(-1.0, "finish_adjoint", adj, far_adjoint)


def solution(mesh):
    spec = P("tm", None, None, "sec", None)
    return jax.shard_map(
        local,
        mesh=mesh,
        in_specs=(spec, spec, P("tm", None), P("tm", None)),
        out_specs=(spec, spec),
        check_vma=False,
    )
```

```python
import functools

import jax
import jax.numpy as jnp
from jax import lax
from jax.experimental import pallas as pl
from jax.experimental.pallas import tpu as pltpu
from jax.sharding import PartitionSpec as P

STENCIL = (0.8, -0.2, 4.0 / 105.0, -1.0 / 280.0)
TIME_SCALE = 4.0
FLOW_VELOCITY = 1.0
AXIAL_DISPERSION = 0.3
RADIAL_SPREADING = 0.2
BINDING_STRENGTH = (1.5, 0.6)
HEAT_EXPONENT = (0.5, 0.3)
KINETIC = (1.2, 0.7)
CAPACITY = (2.0, 1.0)
SORPTION_HEAT = (0.4, 0.25)
PURGE_GAIN = 1.5

REACH = len(STENCIL)
WEIGHTS = tuple(TIME_SCALE * c for c in STENCIL)
MOVING = (0, 1, 2, 5)
CENTRE = FLOW_VELOCITY + 2.0 * AXIAL_DISPERSION + 2.0 * RADIAL_SPREADING
UPWIND = FLOW_VELOCITY + AXIAL_DISPERSION
LAST = 1


def is_odd():
    return lax.rem(lax.axis_index("tm"), 2) == 1


def shifted(x, step, edge):
    cells = x.shape[0]
    row = lax.broadcasted_iota(jnp.int32, x.shape, 0)
    if step > 0:
        return jnp.where(row == 0, edge, pltpu.roll(x, 1, 0))
    return jnp.where(row == cells - 1, edge, pltpu.roll(x, cells - 1, 0))


def radial_pair(x):
    width = x.shape[1]
    lane = lax.broadcasted_iota(jnp.int32, x.shape, 1)
    lower = jnp.where(lane == 0, 0.0, pltpu.roll(x, 1, 1))
    upper = jnp.where(lane == width - 1, 0.0, pltpu.roll(x, width - 1, 1))
    return lower + upper


def transport(x, near, far):
    return CENTRE * x - UPWIND * near - AXIAL_DISPERSION * far - RADIAL_SPREADING * radial_pair(x)


def main_kernel(plan, valve, state, adjoint, edge, in_state, in_adjoint, res, adj):
    instances, comps, beds, cells, _ = res.shape
    odd = is_odd()
    first = lax.axis_index("sec") == 0
    last = lax.axis_index("sec") == lax.axis_size("sec") - 1

    def cell_block(i, carry):
        t = i // beds
        b = lax.rem(i, beds)
        x = [state[t, c, b] for c in range(comps)]
        m = [adjoint[t, c, b] for c in range(comps)]
        y1, y2, _, q1, q2, temp = x
        b1 = BINDING_STRENGTH[0] * jnp.exp(HEAT_EXPONENT[0] * temp)
        b2 = BINDING_STRENGTH[1] * jnp.exp(HEAT_EXPONENT[1] * temp)
        over = 1.0 / (1.0 + b1 * y1 + b2 * y2)
        slope1 = b1 * over
        slope2 = b2 * over
        cover1 = slope1 * y1
        cover2 = slope2 * y2
        rate1 = KINETIC[0] * (CAPACITY[0] * cover1 - q1)
        rate2 = KINETIC[1] * (CAPACITY[1] * cover2 - q2)
        m1 = m[0] - m[3] - SORPTION_HEAT[0] * m[5]
        m2 = m[1] - m[4] - SORPTION_HEAT[1] * m[5]
        g1 = (KINETIC[0] * CAPACITY[0]) * m1
        g2 = (KINETIC[1] * CAPACITY[1]) * m2
        h = g1 * cover1 + g2 * cover2
        e1 = g1 - h
        e2 = g2 - h
        source = {0: rate1, 1: rate2, 5: -SORPTION_HEAT[0] * rate1 - SORPTION_HEAT[1] * rate2}
        pulled = {
            0: slope1 * e1,
            1: slope2 * e2,
            5: HEAT_EXPONENT[0] * cover1 * e1 + HEAT_EXPONENT[1] * cover2 * e2,
        }
        for c in MOVING:
            from_x = edge[0, t, c, b][None]
            from_m = edge[1, t, c, b][None]
            below_x = jnp.where(first, 0.0, from_x)
            above_x = jnp.where(last, 0.0, from_x)
            below_m = jnp.where(first, 0.0, from_m)
            above_m = jnp.where(last, 0.0, from_m)
            r = transport(x[c], shifted(x[c], 1, below_x), shifted(x[c], -1, above_x))
            a = transport(m[c], shifted(m[c], -1, above_m), shifted(m[c], 1, below_m))
            res[t, c, b] = r + source[c] if c in source else r
            adj[t, c, b] = a + pulled[c] if c in pulled else a
        res[t, 3, b] = -rate1
        res[t, 4, b] = -rate2
        adj[t, 3, b] = -KINETIC[0] * m1
        adj[t, 4, b] = -KINETIC[1] * m2
        return carry

    lax.fori_loop(0, instances * beds, cell_block, 0)

    @pl.when(last)
    def _():
        def purge(i, carry):
            t = i // beds
            b = lax.rem(i, beds)
            s = lax.rem(b + plan[t, b], beds)
            gain = PURGE_GAIN * valve[t, b].astype(jnp.float32)
            end = pl.ds(cells - 1, 1)
            for c in range(3):
                res[t, c, b, end] += gain * (state[t, c, b, end] - state[t, c, s, end])
                flow = gain * adjoint[t, c, b, end]
                adj[t, c, b, end] += flow
                adj[t, c, s, end] -= flow
            return carry

        lax.fori_loop(0, instances * beds, purge, 0)

    sign = jnp.where(odd, -1.0, 1.0)
    at = [jnp.where(odd, instances - 1 - t, t) for t in range(instances)]

    def time_block(i, carry):
        c = i // beds
        b = lax.rem(i, beds)
        for own, near, out, factor in ((state, in_state, res, sign), (adjoint, in_adjoint, adj, -sign)):
            line = [own[at[t], c, b] for t in range(instances)]
            line += [near[at[t], c, b] for t in range(instances)]
            for t in range(instances):
                total = 0.0
                for k in range(1, REACH + 1):
                    diff = line[t + k]
                    if t - k >= 0:
                        diff = diff - line[t - k]
                    total = total + WEIGHTS[k - 1] * diff
                out[at[t], c, b] += factor * total
        return carry

    lax.fori_loop(0, comps * beds, time_block, 0)


def finish_kernel(scale, low, part, came, *rest):
    out, _, whole, sem = rest[-4:]
    instances, size, beds, _, _ = came.shape

    def moved(c):
        return pltpu.make_async_copy(whole.at[:, pl.ds(c, 1)], out.at[:, pl.ds(low + c, 1)], sem.at[c])

    def finish(sign, at):
        def component(c, carry):
            for b in range(beds):
                line = [came[at[t], c, b] for t in range(instances)]
                for t in range(instances):
                    total = part[at[t], low + c, b]
                    for j in range(t, instances):
                        total = total - sign * WEIGHTS[t + instances - j - 1] * line[j]
                    whole[at[t], c, b] = total
            moved(c).start()
            return carry

        lax.fori_loop(0, size, component, 0)

    odd = is_odd()

    @pl.when(odd)
    def _():
        finish(-scale, list(reversed(range(instances))))

    @pl.when(jnp.logical_not(odd))
    def _():
        finish(scale, list(range(instances)))

    for c in range(size):
        moved(c).wait()


VMEM = pl.BlockSpec(memory_space=pltpu.VMEM)
SMEM = pl.BlockSpec(memory_space=pltpu.SMEM)
ANY = pl.BlockSpec(memory_space=pl.ANY)
SMALL = pl.CostEstimate(flops=1000, bytes_accessed=1000, transcendentals=0)


def params(mib):
    return pltpu.CompilerParams(vmem_limit_bytes=mib * 2**20)


def local(state, adjoint, plan, valve):
    count = lax.axis_size("tm")
    sections = lax.axis_size("sec")
    comps = state.shape[1]
    block = jax.ShapeDtypeStruct(state.shape, state.dtype)
    across = [(i, (i + 1) % count if i % 2 else (i - 1) % count) for i in range(count)]
    on_chip = [(i, i ^ 1) for i in range(count)]
    far_state = lax.ppermute(state, "tm", across)
    cut = comps - LAST
    far_adjoint = [lax.ppermute(x, "tm", across) for x in (adjoint[:, :cut], adjoint[:, cut:])]

    def near_transfers():
        in_state = lax.ppermute(state, "tm", on_chip)
        in_adjoint = lax.ppermute(adjoint, "tm", on_chip)
        sec = lax.axis_index("sec")
        ends = [jnp.where(sec == 0, a[:, :, :, -1], a[:, :, :, 0]) for a in (state, adjoint)]
        edge = lax.ppermute(jnp.stack(ends), "sec", [(i, i ^ 1) for i in range(sections)])
        return edge, in_state, in_adjoint

    def nothing():
        return jnp.zeros((2,) + state.shape[:3] + state.shape[4:], state.dtype), state, adjoint

    near = lax.cond(lax.axis_index("tm") % 2 >= 0, near_transfers, nothing)
    res, adj = pl.pallas_call(
        main_kernel,
        out_shape=(block, block),
        in_specs=[SMEM] * 2 + [VMEM] * 5,
        out_specs=(VMEM, VMEM),
        compiler_params=params(24),
        cost_estimate=SMALL,
        name="local_part",
    )(plan, valve, state, adjoint, *near)

    def finish(name, scale, low, part, came, before, begun):
        return pl.pallas_call(
            functools.partial(finish_kernel, scale, low),
            out_shape=(block, jax.ShapeDtypeStruct((8, 128), jnp.float32)),
            in_specs=[VMEM, VMEM, ANY],
            out_specs=(ANY, ANY),
            scratch_shapes=[pltpu.VMEM(came.shape, came.dtype), pltpu.SemaphoreType.DMA((came.shape[1],))],
            input_output_aliases={2: 0} if begun else {},
            compiler_params=params(16),
            cost_estimate=SMALL,
            name=name,
        )(part, came, before)

    residual, token = finish("finish_residual", 1.0, 0, res, far_state, plan, False)
    begun, _ = finish("finish_adjoint", -1.0, 0, adj, far_adjoint[0], token, False)
    adjoint_out, _ = finish("finish_last", -1.0, cut, adj, far_adjoint[1], begun, True)
    return residual, adjoint_out


def solution(mesh):
    spec = P("tm", None, None, "sec", None)
    return jax.shard_map(
        local,
        mesh=mesh,
        in_specs=(spec, spec, P("tm", None), P("tm", None)),
        out_specs=(spec, spec),
        check_vma=False,
    )
```

```python
import functools

import jax
import jax.numpy as jnp
from jax import lax
from jax.experimental import pallas as pl
from jax.experimental.pallas import tpu as pltpu
from jax.sharding import PartitionSpec as P

STENCIL = (0.8, -0.2, 4.0 / 105.0, -1.0 / 280.0)
TIME_SCALE = 4.0
FLOW_VELOCITY = 1.0
AXIAL_DISPERSION = 0.3
RADIAL_SPREADING = 0.2
BINDING_STRENGTH = (1.5, 0.6)
HEAT_EXPONENT = (0.5, 0.3)
KINETIC = (1.2, 0.7)
CAPACITY = (2.0, 1.0)
SORPTION_HEAT = (0.4, 0.25)
PURGE_GAIN = 1.5

REACH = len(STENCIL)
WEIGHTS = tuple(TIME_SCALE * c for c in STENCIL)
MOVING = (0, 1, 2, 5)
CENTRE = FLOW_VELOCITY + 2.0 * AXIAL_DISPERSION + 2.0 * RADIAL_SPREADING
UPWIND = FLOW_VELOCITY + AXIAL_DISPERSION
LAST = 1
SPARED = (2, 1)
VIA = (5, 9)


def is_odd():
    return lax.rem(lax.axis_index("tm"), 2) == 1


def shifted(x, step, edge):
    cells = x.shape[0]
    row = lax.broadcasted_iota(jnp.int32, x.shape, 0)
    if step > 0:
        return jnp.where(row == 0, edge, pltpu.roll(x, 1, 0))
    return jnp.where(row == cells - 1, edge, pltpu.roll(x, cells - 1, 0))


def radial_pair(x):
    width = x.shape[1]
    lane = lax.broadcasted_iota(jnp.int32, x.shape, 1)
    lower = jnp.where(lane == 0, 0.0, pltpu.roll(x, 1, 1))
    upper = jnp.where(lane == width - 1, 0.0, pltpu.roll(x, width - 1, 1))
    return lower + upper


def transport(x, near, far):
    return CENTRE * x - UPWIND * near - AXIAL_DISPERSION * far - RADIAL_SPREADING * radial_pair(x)


def from_before(line, t):
    total = 0.0
    for j in range(t, len(line)):
        total = total + WEIGHTS[t + len(line) - j - 1] * line[j]
    return total


def main_kernel(plan, valve, state, adjoint, edge, in_state, in_adjoint, *rest):
    relayed, res, adj = rest[:-2], rest[-2], rest[-1]
    instances, comps, beds, cells, _ = res.shape
    odd = is_odd()
    first = lax.axis_index("sec") == 0
    last = lax.axis_index("sec") == lax.axis_size("sec") - 1

    def cell_block(i, carry):
        t = i // beds
        b = lax.rem(i, beds)
        x = [state[t, c, b] for c in range(comps)]
        m = [adjoint[t, c, b] for c in range(comps)]
        y1, y2, _, q1, q2, temp = x
        b1 = BINDING_STRENGTH[0] * jnp.exp(HEAT_EXPONENT[0] * temp)
        b2 = BINDING_STRENGTH[1] * jnp.exp(HEAT_EXPONENT[1] * temp)
        over = 1.0 / (1.0 + b1 * y1 + b2 * y2)
        slope1 = b1 * over
        slope2 = b2 * over
        cover1 = slope1 * y1
        cover2 = slope2 * y2
        rate1 = KINETIC[0] * (CAPACITY[0] * cover1 - q1)
        rate2 = KINETIC[1] * (CAPACITY[1] * cover2 - q2)
        m1 = m[0] - m[3] - SORPTION_HEAT[0] * m[5]
        m2 = m[1] - m[4] - SORPTION_HEAT[1] * m[5]
        g1 = (KINETIC[0] * CAPACITY[0]) * m1
        g2 = (KINETIC[1] * CAPACITY[1]) * m2
        h = g1 * cover1 + g2 * cover2
        e1 = g1 - h
        e2 = g2 - h
        source = {0: rate1, 1: rate2, 5: -SORPTION_HEAT[0] * rate1 - SORPTION_HEAT[1] * rate2}
        pulled = {
            0: slope1 * e1,
            1: slope2 * e2,
            5: HEAT_EXPONENT[0] * cover1 * e1 + HEAT_EXPONENT[1] * cover2 * e2,
        }
        for c in MOVING:
            from_x = edge[0, t, c, b][None]
            from_m = edge[1, t, c, b][None]
            below_x = jnp.where(first, 0.0, from_x)
            above_x = jnp.where(last, 0.0, from_x)
            below_m = jnp.where(first, 0.0, from_m)
            above_m = jnp.where(last, 0.0, from_m)
            r = transport(x[c], shifted(x[c], 1, below_x), shifted(x[c], -1, above_x))
            a = transport(m[c], shifted(m[c], -1, above_m), shifted(m[c], 1, below_m))
            res[t, c, b] = r + source[c] if c in source else r
            adj[t, c, b] = a + pulled[c] if c in pulled else a
        res[t, 3, b] = -rate1
        res[t, 4, b] = -rate2
        adj[t, 3, b] = -KINETIC[0] * m1
        adj[t, 4, b] = -KINETIC[1] * m2
        return carry

    lax.fori_loop(0, instances * beds, cell_block, 0)

    @pl.when(last)
    def _():
        def purge(i, carry):
            t = i // beds
            b = lax.rem(i, beds)
            s = lax.rem(b + plan[t, b], beds)
            gain = PURGE_GAIN * valve[t, b].astype(jnp.float32)
            end = pl.ds(cells - 1, 1)
            for c in range(3):
                res[t, c, b, end] += gain * (state[t, c, b, end] - state[t, c, s, end])
                flow = gain * adjoint[t, c, b, end]
                adj[t, c, b, end] += flow
                adj[t, c, s, end] -= flow
            return carry

        lax.fori_loop(0, instances * beds, purge, 0)

    sign = jnp.where(odd, -1.0, 1.0)
    at = [jnp.where(odd, instances - 1 - t, t) for t in range(instances)]

    def time_block(i, carry):
        c = i // beds
        b = lax.rem(i, beds)
        for own, near, out, factor in ((state, in_state, res, sign), (adjoint, in_adjoint, adj, -sign)):
            line = [own[at[t], c, b] for t in range(instances)]
            line += [near[at[t], c, b] for t in range(instances)]
            for t in range(instances):
                total = 0.0
                for k in range(1, REACH + 1):
                    diff = line[t + k]
                    if t - k >= 0:
                        diff = diff - line[t - k]
                    total = total + WEIGHTS[k - 1] * diff
                out[at[t], c, b] += factor * total
        return carry

    lax.fori_loop(0, comps * beds, time_block, 0)

    for n, came in enumerate(relayed):
        b = beds - len(relayed) + n
        for c in range(LAST):
            line = [came[at[t], c, 0] for t in range(instances)]
            for t in range(instances):
                adj[at[t], comps - LAST + c, b] += sign * from_before(line, t)


def finish_kernel(scale, low, part, *rest):
    came, (out, _, whole, sem) = rest[:-5], rest[-4:]
    instances, size, beds, _, _ = whole.shape
    bed = [(ref, b) for ref in came for b in range(ref.shape[2])]

    def moved(c):
        return pltpu.make_async_copy(whole.at[:, pl.ds(c, 1)], out.at[:, pl.ds(low + c, 1)], sem.at[c])

    def finish(sign, at):
        def component(c, carry):
            for b, (ref, place) in enumerate(bed):
                line = [ref[at[t], c, place] for t in range(instances)]
                for t in range(instances):
                    whole[at[t], c, b] = part[at[t], low + c, b] - sign * from_before(line, t)
            moved(c).start()
            return carry

        lax.fori_loop(0, size, component, 0)

    odd = is_odd()

    @pl.when(odd)
    def _():
        finish(-scale, list(reversed(range(instances))))

    @pl.when(jnp.logical_not(odd))
    def _():
        finish(scale, list(range(instances)))

    for c in range(size):
        moved(c).wait()


VMEM = pl.BlockSpec(memory_space=pltpu.VMEM)
SMEM = pl.BlockSpec(memory_space=pltpu.SMEM)
ANY = pl.BlockSpec(memory_space=pl.ANY)
SMALL = pl.CostEstimate(flops=1000, bytes_accessed=1000, transcendentals=0)


def params(mib):
    return pltpu.CompilerParams(vmem_limit_bytes=mib * 2**20)


def local(state, adjoint, plan, valve):
    count = lax.axis_size("tm")
    sections = lax.axis_size("sec")
    comps = state.shape[1]
    block = jax.ShapeDtypeStruct(state.shape, state.dtype)
    across = [(i, (i + 1) % count if i % 2 else (i - 1) % count) for i in range(count)]
    on_chip = [(i, i ^ 1) for i in range(count)]
    far_state = lax.ppermute(state, "tm", across)
    beds = state.shape[2]
    cut = comps - LAST
    via = [i for i in VIA if i < count]
    kept = beds - len(via)
    far_adjoint = [
        lax.ppermute(adjoint[:, :cut], "tm", across),
        lax.ppermute(adjoint[:, cut:, :kept], "tm", across),
        lax.ppermute(adjoint[:, cut:, kept:], "tm", [pair for pair in across if pair != SPARED]),
    ]

    def near_transfers():
        in_state = lax.ppermute(state, "tm", on_chip)
        in_adjoint = lax.ppermute(adjoint, "tm", on_chip)
        sec = lax.axis_index("sec")
        ends = [jnp.where(sec == 0, a[:, :, :, -1], a[:, :, :, 0]) for a in (state, adjoint)]
        edge = lax.ppermute(jnp.stack(ends), "sec", [(i, i ^ 1) for i in range(sections)])
        beds_of = [adjoint[:, cut:, kept + n : kept + n + 1] for n in range(len(via))]
        half_way = [lax.ppermute(x, "tm", [(SPARED[0], i)]) for x, i in zip(beds_of, via)]
        relayed = [lax.ppermute(x, "tm", [(i, SPARED[1])]) for x, i in zip(half_way, via)]
        return edge, in_state, in_adjoint, *relayed

    def nothing():
        edge = jnp.zeros((2,) + state.shape[:3] + state.shape[4:], state.dtype)
        return edge, state, adjoint, *(adjoint[:, cut:, :1] for _ in via)

    near = lax.cond(lax.axis_index("tm") % 2 >= 0, near_transfers, nothing)
    res, adj = pl.pallas_call(
        main_kernel,
        out_shape=(block, block),
        in_specs=[SMEM] * 2 + [VMEM] * (2 + len(near)),
        out_specs=(VMEM, VMEM),
        compiler_params=params(24),
        cost_estimate=SMALL,
        name="local_part",
    )(plan, valve, state, adjoint, *near)

    def finish(name, scale, low, part, came, before, begun):
        size = came[0].shape[1]
        return pl.pallas_call(
            functools.partial(finish_kernel, scale, low),
            out_shape=(block, jax.ShapeDtypeStruct((8, 128), jnp.float32)),
            in_specs=[VMEM] * (1 + len(came)) + [ANY],
            out_specs=(ANY, ANY),
            scratch_shapes=[
                pltpu.VMEM((state.shape[0], size) + state.shape[2:], state.dtype),
                pltpu.SemaphoreType.DMA((size,)),
            ],
            input_output_aliases={1 + len(came): 0} if begun else {},
            compiler_params=params(16),
            cost_estimate=SMALL,
            name=name,
        )(part, *came, before)

    residual, token = finish("finish_residual", 1.0, 0, res, [far_state], plan, False)
    begun, _ = finish("finish_adjoint", -1.0, 0, adj, far_adjoint[:1], token, False)
    adjoint_out, _ = finish("finish_last", -1.0, cut, adj, far_adjoint[1:], begun, True)
    return residual, adjoint_out


def solution(mesh):
    spec = P("tm", None, None, "sec", None)
    return jax.shard_map(
        local,
        mesh=mesh,
        in_specs=(spec, spec, P("tm", None), P("tm", None)),
        out_specs=(spec, spec),
        check_vma=False,
    )
```

```python
import functools

import jax
import jax.numpy as jnp
from jax import lax
from jax.experimental import pallas as pl
from jax.experimental.pallas import tpu as pltpu
from jax.sharding import PartitionSpec as P

STENCIL = (0.8, -0.2, 4.0 / 105.0, -1.0 / 280.0)
TIME_SCALE = 4.0
FLOW_VELOCITY = 1.0
AXIAL_DISPERSION = 0.3
RADIAL_SPREADING = 0.2
BINDING_STRENGTH = (1.5, 0.6)
HEAT_EXPONENT = (0.5, 0.3)
KINETIC = (1.2, 0.7)
CAPACITY = (2.0, 1.0)
SORPTION_HEAT = (0.4, 0.25)
PURGE_GAIN = 1.5

REACH = len(STENCIL)
WEIGHTS = tuple(TIME_SCALE * c for c in STENCIL)
MOVING = (0, 1, 2, 5)
CENTRE = FLOW_VELOCITY + 2.0 * AXIAL_DISPERSION + 2.0 * RADIAL_SPREADING
UPWIND = FLOW_VELOCITY + AXIAL_DISPERSION
LAST = 1
SPARED = (2, 1)
VIA = (5, 9)


def is_odd():
    return lax.rem(lax.axis_index("tm"), 2) == 1


def shifted(x, step, edge):
    cells = x.shape[0]
    row = lax.broadcasted_iota(jnp.int32, x.shape, 0)
    if step > 0:
        return jnp.where(row == 0, edge, pltpu.roll(x, 1, 0))
    return jnp.where(row == cells - 1, edge, pltpu.roll(x, cells - 1, 0))


def radial_pair(x):
    width = x.shape[1]
    lane = lax.broadcasted_iota(jnp.int32, x.shape, 1)
    lower = jnp.where(lane == 0, 0.0, pltpu.roll(x, 1, 1))
    upper = jnp.where(lane == width - 1, 0.0, pltpu.roll(x, width - 1, 1))
    return lower + upper


def transport(x, near, far):
    return CENTRE * x - UPWIND * near - AXIAL_DISPERSION * far - RADIAL_SPREADING * radial_pair(x)


def from_before(line, t):
    total = 0.0
    for j in range(t, len(line)):
        total = total + WEIGHTS[t + len(line) - j - 1] * line[j]
    return total


def main_kernel(plan, valve, state, adjoint, edge, in_state, in_adjoint, *rest):
    relayed, res, adj = rest[:-2], rest[-2], rest[-1]
    instances, comps, beds, cells, _ = res.shape
    odd = is_odd()
    first = lax.axis_index("sec") == 0
    last = lax.axis_index("sec") == lax.axis_size("sec") - 1

    def cell_block(i, carry):
        t = i // beds
        b = lax.rem(i, beds)
        x = [state[t, c, b] for c in range(comps)]
        m = [adjoint[t, c, b] for c in range(comps)]
        y1, y2, _, q1, q2, temp = x
        b1 = BINDING_STRENGTH[0] * jnp.exp(HEAT_EXPONENT[0] * temp)
        b2 = BINDING_STRENGTH[1] * jnp.exp(HEAT_EXPONENT[1] * temp)
        over = 1.0 / (1.0 + b1 * y1 + b2 * y2)
        slope1 = b1 * over
        slope2 = b2 * over
        cover1 = slope1 * y1
        cover2 = slope2 * y2
        rate1 = KINETIC[0] * (CAPACITY[0] * cover1 - q1)
        rate2 = KINETIC[1] * (CAPACITY[1] * cover2 - q2)
        m1 = m[0] - m[3] - SORPTION_HEAT[0] * m[5]
        m2 = m[1] - m[4] - SORPTION_HEAT[1] * m[5]
        g1 = (KINETIC[0] * CAPACITY[0]) * m1
        g2 = (KINETIC[1] * CAPACITY[1]) * m2
        h = g1 * cover1 + g2 * cover2
        e1 = g1 - h
        e2 = g2 - h
        source = {0: rate1, 1: rate2, 5: -SORPTION_HEAT[0] * rate1 - SORPTION_HEAT[1] * rate2}
        pulled = {
            0: slope1 * e1,
            1: slope2 * e2,
            5: HEAT_EXPONENT[0] * cover1 * e1 + HEAT_EXPONENT[1] * cover2 * e2,
        }
        for c in MOVING:
            from_x = edge[0, t, c, b][None]
            from_m = edge[1, t, c, b][None]
            below_x = jnp.where(first, 0.0, from_x)
            above_x = jnp.where(last, 0.0, from_x)
            below_m = jnp.where(first, 0.0, from_m)
            above_m = jnp.where(last, 0.0, from_m)
            r = transport(x[c], shifted(x[c], 1, below_x), shifted(x[c], -1, above_x))
            a = transport(m[c], shifted(m[c], -1, above_m), shifted(m[c], 1, below_m))
            res[t, c, b] = r + source[c] if c in source else r
            adj[t, c, b] = a + pulled[c] if c in pulled else a
        res[t, 3, b] = -rate1
        res[t, 4, b] = -rate2
        adj[t, 3, b] = -KINETIC[0] * m1
        adj[t, 4, b] = -KINETIC[1] * m2
        return carry

    lax.fori_loop(0, instances * beds, cell_block, 0)

    @pl.when(last)
    def _():
        def purge(i, carry):
            t = i // beds
            b = lax.rem(i, beds)
            s = lax.rem(b + plan[t, b], beds)
            gain = PURGE_GAIN * valve[t, b].astype(jnp.float32)
            end = pl.ds(cells - 1, 1)
            for c in range(3):
                res[t, c, b, end] += gain * (state[t, c, b, end] - state[t, c, s, end])
                flow = gain * adjoint[t, c, b, end]
                adj[t, c, b, end] += flow
                adj[t, c, s, end] -= flow
            return carry

        lax.fori_loop(0, instances * beds, purge, 0)

    sign = jnp.where(odd, -1.0, 1.0)
    at = [jnp.where(odd, instances - 1 - t, t) for t in range(instances)]

    def time_block(i, carry):
        c = i // beds
        b = lax.rem(i, beds)
        for own, near, out, factor in ((state, in_state, res, sign), (adjoint, in_adjoint, adj, -sign)):
            line = [own[at[t], c, b] for t in range(instances)]
            line += [near[at[t], c, b] for t in range(instances)]
            for t in range(instances):
                total = 0.0
                for k in range(1, REACH + 1):
                    diff = line[t + k]
                    if t - k >= 0:
                        diff = diff - line[t - k]
                    total = total + WEIGHTS[k - 1] * diff
                out[at[t], c, b] += factor * total
        return carry

    lax.fori_loop(0, comps * beds, time_block, 0)

    for n, came in enumerate(relayed):
        b = beds - len(relayed) + n
        for c in range(LAST):
            line = [came[at[t], c, 0] for t in range(instances)]
            for t in range(instances):
                adj[at[t], comps - LAST + c, b] += sign * from_before(line, t)


def finish_kernel(scale, low, part, *rest):
    came, (out, _, whole, sem) = rest[:-5], rest[-4:]
    instances, size, beds, _, _ = whole.shape
    bed = [(ref, b) for ref in came for b in range(ref.shape[2])]

    def moved(c):
        return pltpu.make_async_copy(whole.at[:, pl.ds(c, 1)], out.at[:, pl.ds(low + c, 1)], sem.at[c])

    def finish(sign, at):
        def component(c, carry):
            for b, (ref, place) in enumerate(bed):
                line = [ref[at[t], c, place] for t in range(instances)]
                for t in range(instances):
                    whole[at[t], c, b] = part[at[t], low + c, b] - sign * from_before(line, t)
            moved(c).start()
            return carry

        lax.fori_loop(0, size, component, 0)

    odd = is_odd()

    @pl.when(odd)
    def _():
        finish(-scale, list(reversed(range(instances))))

    @pl.when(jnp.logical_not(odd))
    def _():
        finish(scale, list(range(instances)))

    for c in range(size):
        moved(c).wait()


VMEM = pl.BlockSpec(memory_space=pltpu.VMEM)
SMEM = pl.BlockSpec(memory_space=pltpu.SMEM)
ANY = pl.BlockSpec(memory_space=pl.ANY)
SMALL = pl.CostEstimate(flops=1000, bytes_accessed=1000, transcendentals=0)


def params(mib):
    return pltpu.CompilerParams(vmem_limit_bytes=mib * 2**20)


def local(state, adjoint, plan, valve):
    count = lax.axis_size("tm")
    sections = lax.axis_size("sec")
    comps = state.shape[1]
    block = jax.ShapeDtypeStruct(state.shape, state.dtype)
    across = [(i, (i + 1) % count if i % 2 else (i - 1) % count) for i in range(count)]
    on_chip = [(i, i ^ 1) for i in range(count)]
    far_state = lax.ppermute(state, "tm", across)
    beds = state.shape[2]
    cut = comps - LAST
    via = [i for i in VIA if i < count]
    kept = beds - len(via)
    far_adjoint = [
        lax.ppermute(adjoint[:, :cut], "tm", across),
        lax.ppermute(adjoint[:, cut:, :kept], "tm", across),
        lax.ppermute(adjoint[:, cut:, kept:], "tm", [pair for pair in across if pair != SPARED]),
    ]

    def near_transfers():
        in_state = lax.ppermute(state, "tm", on_chip)
        in_adjoint = lax.ppermute(adjoint, "tm", on_chip)
        sec = lax.axis_index("sec")
        ends = [jnp.where(sec == 0, a[:, :, :, -1], a[:, :, :, 0]) for a in (state, adjoint)]
        edge = lax.ppermute(jnp.stack(ends), "sec", [(i, i ^ 1) for i in range(sections)])
        return edge, in_state, in_adjoint

    def nothing():
        edge = jnp.zeros((2,) + state.shape[:3] + state.shape[4:], state.dtype)
        return edge, state, adjoint

    near = lax.cond(lax.axis_index("tm") % 2 >= 0, near_transfers, nothing)
    beds_of = [adjoint[:, cut:, kept + n : kept + n + 1] for n in range(len(via))]
    half_way = [lax.ppermute(x, "tm", [(SPARED[0], i)]) for x, i in zip(beds_of, via)]
    near += tuple(lax.ppermute(x, "tm", [(i, SPARED[1])]) for x, i in zip(half_way, via))
    res, adj = pl.pallas_call(
        main_kernel,
        out_shape=(block, block),
        in_specs=[SMEM] * 2 + [VMEM] * (2 + len(near)),
        out_specs=(VMEM, VMEM),
        compiler_params=params(24),
        cost_estimate=SMALL,
        name="local_part",
    )(plan, valve, state, adjoint, *near)

    def finish(name, scale, low, part, came, before, begun):
        size = came[0].shape[1]
        return pl.pallas_call(
            functools.partial(finish_kernel, scale, low),
            out_shape=(block, jax.ShapeDtypeStruct((8, 128), jnp.float32)),
            in_specs=[VMEM] * (1 + len(came)) + [ANY],
            out_specs=(ANY, ANY),
            scratch_shapes=[
                pltpu.VMEM((state.shape[0], size) + state.shape[2:], state.dtype),
                pltpu.SemaphoreType.DMA((size,)),
            ],
            input_output_aliases={1 + len(came): 0} if begun else {},
            compiler_params=params(16),
            cost_estimate=SMALL,
            name=name,
        )(part, *came, before)

    residual, token = finish("finish_residual", 1.0, 0, res, [far_state], plan, False)
    begun, _ = finish("finish_adjoint", -1.0, 0, adj, far_adjoint[:1], token, False)
    adjoint_out, _ = finish("finish_last", -1.0, cut, adj, far_adjoint[1:], begun, True)
    return residual, adjoint_out


def solution(mesh):
    spec = P("tm", None, None, "sec", None)
    return jax.shard_map(
        local,
        mesh=mesh,
        in_specs=(spec, spec, P("tm", None), P("tm", None)),
        out_specs=(spec, spec),
        check_vma=False,
    )
```

```python
import functools

import jax
import jax.numpy as jnp
from jax import lax
from jax.experimental import pallas as pl
from jax.experimental.pallas import tpu as pltpu
from jax.sharding import PartitionSpec as P

STENCIL = (0.8, -0.2, 4.0 / 105.0, -1.0 / 280.0)
TIME_SCALE = 4.0
FLOW_VELOCITY = 1.0
AXIAL_DISPERSION = 0.3
RADIAL_SPREADING = 0.2
BINDING_STRENGTH = (1.5, 0.6)
HEAT_EXPONENT = (0.5, 0.3)
KINETIC = (1.2, 0.7)
CAPACITY = (2.0, 1.0)
SORPTION_HEAT = (0.4, 0.25)
PURGE_GAIN = 1.5

REACH = len(STENCIL)
WEIGHTS = tuple(TIME_SCALE * c for c in STENCIL)
MOVING = (0, 1, 2, 5)
CENTRE = FLOW_VELOCITY + 2.0 * AXIAL_DISPERSION + 2.0 * RADIAL_SPREADING
UPWIND = FLOW_VELOCITY + AXIAL_DISPERSION
LAST = 1
SPARED = (2, 1)
VIA = (9,)


def is_odd():
    return lax.rem(lax.axis_index("tm"), 2) == 1


def shifted(x, step, edge):
    cells = x.shape[0]
    row = lax.broadcasted_iota(jnp.int32, x.shape, 0)
    if step > 0:
        return jnp.where(row == 0, edge, pltpu.roll(x, 1, 0))
    return jnp.where(row == cells - 1, edge, pltpu.roll(x, cells - 1, 0))


def radial_pair(x):
    width = x.shape[1]
    lane = lax.broadcasted_iota(jnp.int32, x.shape, 1)
    lower = jnp.where(lane == 0, 0.0, pltpu.roll(x, 1, 1))
    upper = jnp.where(lane == width - 1, 0.0, pltpu.roll(x, width - 1, 1))
    return lower + upper


def transport(x, near, far):
    return CENTRE * x - UPWIND * near - AXIAL_DISPERSION * far - RADIAL_SPREADING * radial_pair(x)


def from_before(line, t):
    total = 0.0
    for j in range(t, len(line)):
        total = total + WEIGHTS[t + len(line) - j - 1] * line[j]
    return total


def main_kernel(plan, valve, state, adjoint, edge, in_state, in_adjoint, res, adj):
    instances, comps, beds, cells, _ = res.shape
    odd = is_odd()
    first = lax.axis_index("sec") == 0
    last = lax.axis_index("sec") == lax.axis_size("sec") - 1

    def cell_block(i, carry):
        t = i // beds
        b = lax.rem(i, beds)
        x = [state[t, c, b] for c in range(comps)]
        m = [adjoint[t, c, b] for c in range(comps)]
        y1, y2, _, q1, q2, temp = x
        b1 = BINDING_STRENGTH[0] * jnp.exp(HEAT_EXPONENT[0] * temp)
        b2 = BINDING_STRENGTH[1] * jnp.exp(HEAT_EXPONENT[1] * temp)
        over = 1.0 / (1.0 + b1 * y1 + b2 * y2)
        slope1 = b1 * over
        slope2 = b2 * over
        cover1 = slope1 * y1
        cover2 = slope2 * y2
        rate1 = KINETIC[0] * (CAPACITY[0] * cover1 - q1)
        rate2 = KINETIC[1] * (CAPACITY[1] * cover2 - q2)
        m1 = m[0] - m[3] - SORPTION_HEAT[0] * m[5]
        m2 = m[1] - m[4] - SORPTION_HEAT[1] * m[5]
        g1 = (KINETIC[0] * CAPACITY[0]) * m1
        g2 = (KINETIC[1] * CAPACITY[1]) * m2
        h = g1 * cover1 + g2 * cover2
        e1 = g1 - h
        e2 = g2 - h
        source = {0: rate1, 1: rate2, 5: -SORPTION_HEAT[0] * rate1 - SORPTION_HEAT[1] * rate2}
        pulled = {
            0: slope1 * e1,
            1: slope2 * e2,
            5: HEAT_EXPONENT[0] * cover1 * e1 + HEAT_EXPONENT[1] * cover2 * e2,
        }
        for c in MOVING:
            from_x = edge[0, t, c, b][None]
            from_m = edge[1, t, c, b][None]
            below_x = jnp.where(first, 0.0, from_x)
            above_x = jnp.where(last, 0.0, from_x)
            below_m = jnp.where(first, 0.0, from_m)
            above_m = jnp.where(last, 0.0, from_m)
            r = transport(x[c], shifted(x[c], 1, below_x), shifted(x[c], -1, above_x))
            a = transport(m[c], shifted(m[c], -1, above_m), shifted(m[c], 1, below_m))
            res[t, c, b] = r + source[c] if c in source else r
            adj[t, c, b] = a + pulled[c] if c in pulled else a
        res[t, 3, b] = -rate1
        res[t, 4, b] = -rate2
        adj[t, 3, b] = -KINETIC[0] * m1
        adj[t, 4, b] = -KINETIC[1] * m2
        return carry

    lax.fori_loop(0, instances * beds, cell_block, 0)

    @pl.when(last)
    def _():
        def purge(i, carry):
            t = i // beds
            b = lax.rem(i, beds)
            s = lax.rem(b + plan[t, b], beds)
            gain = PURGE_GAIN * valve[t, b].astype(jnp.float32)
            end = pl.ds(cells - 1, 1)
            for c in range(3):
                res[t, c, b, end] += gain * (state[t, c, b, end] - state[t, c, s, end])
                flow = gain * adjoint[t, c, b, end]
                adj[t, c, b, end] += flow
                adj[t, c, s, end] -= flow
            return carry

        lax.fori_loop(0, instances * beds, purge, 0)

    sign = jnp.where(odd, -1.0, 1.0)
    at = [jnp.where(odd, instances - 1 - t, t) for t in range(instances)]

    def time_block(i, carry):
        c = i // beds
        b = lax.rem(i, beds)
        for own, near, out, factor in ((state, in_state, res, sign), (adjoint, in_adjoint, adj, -sign)):
            line = [own[at[t], c, b] for t in range(instances)]
            line += [near[at[t], c, b] for t in range(instances)]
            for t in range(instances):
                total = 0.0
                for k in range(1, REACH + 1):
                    diff = line[t + k]
                    if t - k >= 0:
                        diff = diff - line[t - k]
                    total = total + WEIGHTS[k - 1] * diff
                out[at[t], c, b] += factor * total
        return carry

    lax.fori_loop(0, comps * beds, time_block, 0)


def finish_kernel(scale, low, part, *rest):
    came, (out, _, whole, sem) = rest[:-5], rest[-4:]
    instances, size, beds, _, _ = whole.shape
    ways = [(ref, b) for ref in came for b in range(ref.shape[2])]
    extra = len(ways) - beds

    def moved(c):
        return pltpu.make_async_copy(whole.at[:, pl.ds(c, 1)], out.at[:, pl.ds(low + c, 1)], sem.at[c])

    def finish(sign, at):
        def component(c, carry):
            for b in range(beds):
                both = ways[b : b + 1] + (ways[b + extra : b + extra + 1] if b >= beds - extra else [])
                line = [sum(ref[at[t], c, place] for ref, place in both) for t in range(instances)]
                for t in range(instances):
                    whole[at[t], c, b] = part[at[t], low + c, b] - sign * from_before(line, t)
            moved(c).start()
            return carry

        lax.fori_loop(0, size, component, 0)

    odd = is_odd()

    @pl.when(odd)
    def _():
        finish(-scale, list(reversed(range(instances))))

    @pl.when(jnp.logical_not(odd))
    def _():
        finish(scale, list(range(instances)))

    for c in range(size):
        moved(c).wait()


VMEM = pl.BlockSpec(memory_space=pltpu.VMEM)
SMEM = pl.BlockSpec(memory_space=pltpu.SMEM)
ANY = pl.BlockSpec(memory_space=pl.ANY)
SMALL = pl.CostEstimate(flops=1000, bytes_accessed=1000, transcendentals=0)


def params(mib):
    return pltpu.CompilerParams(vmem_limit_bytes=mib * 2**20)


def local(state, adjoint, plan, valve):
    count = lax.axis_size("tm")
    sections = lax.axis_size("sec")
    comps = state.shape[1]
    block = jax.ShapeDtypeStruct(state.shape, state.dtype)
    across = [(i, (i + 1) % count if i % 2 else (i - 1) % count) for i in range(count)]
    on_chip = [(i, i ^ 1) for i in range(count)]
    far_state = lax.ppermute(state, "tm", across)
    beds = state.shape[2]
    cut = comps - LAST
    via = [i for i in VIA if i < count]
    kept = beds - len(via)
    far_adjoint = [
        lax.ppermute(adjoint[:, :cut], "tm", across),
        lax.ppermute(adjoint[:, cut:, :kept], "tm", across),
        lax.ppermute(adjoint[:, cut:, kept:], "tm", [pair for pair in across if pair != SPARED]),
    ]

    def near_transfers():
        in_state = lax.ppermute(state, "tm", on_chip)
        in_adjoint = lax.ppermute(adjoint, "tm", on_chip)
        sec = lax.axis_index("sec")
        ends = [jnp.where(sec == 0, a[:, :, :, -1], a[:, :, :, 0]) for a in (state, adjoint)]
        edge = lax.ppermute(jnp.stack(ends), "sec", [(i, i ^ 1) for i in range(sections)])
        return edge, in_state, in_adjoint

    def nothing():
        edge = jnp.zeros((2,) + state.shape[:3] + state.shape[4:], state.dtype)
        return edge, state, adjoint

    near = lax.cond(lax.axis_index("tm") % 2 >= 0, near_transfers, nothing)
    beds_of = [adjoint[:, cut:, kept + n : kept + n + 1] for n in range(len(via))]
    half_way = [lax.ppermute(x, "tm", [(SPARED[0], i)]) for x, i in zip(beds_of, via)]
    far_adjoint += [lax.ppermute(x, "tm", [(i, SPARED[1])]) for x, i in zip(half_way, via)]
    res, adj = pl.pallas_call(
        main_kernel,
        out_shape=(block, block),
        in_specs=[SMEM] * 2 + [VMEM] * 5,
        out_specs=(VMEM, VMEM),
        compiler_params=params(24),
        cost_estimate=SMALL,
        name="local_part",
    )(plan, valve, state, adjoint, *near)

    def finish(name, scale, low, part, came, before, begun):
        size = came[0].shape[1]
        return pl.pallas_call(
            functools.partial(finish_kernel, scale, low),
            out_shape=(block, jax.ShapeDtypeStruct((8, 128), jnp.float32)),
            in_specs=[VMEM] * (1 + len(came)) + [ANY],
            out_specs=(ANY, ANY),
            scratch_shapes=[
                pltpu.VMEM((state.shape[0], size) + state.shape[2:], state.dtype),
                pltpu.SemaphoreType.DMA((size,)),
            ],
            input_output_aliases={1 + len(came): 0} if begun else {},
            compiler_params=params(16),
            cost_estimate=SMALL,
            name=name,
        )(part, *came, before)

    residual, token = finish("finish_residual", 1.0, 0, res, [far_state], plan, False)
    begun, _ = finish("finish_adjoint", -1.0, 0, adj, far_adjoint[:1], token, False)
    adjoint_out, _ = finish("finish_last", -1.0, cut, adj, far_adjoint[1:], begun, True)
    return residual, adjoint_out


def solution(mesh):
    spec = P("tm", None, None, "sec", None)
    return jax.shard_map(
        local,
        mesh=mesh,
        in_specs=(spec, spec, P("tm", None), P("tm", None)),
        out_specs=(spec, spec),
        check_vma=False,
    )
```

```python
import functools

import jax
import jax.numpy as jnp
from jax import lax
from jax.experimental import pallas as pl
from jax.experimental.pallas import tpu as pltpu
from jax.sharding import PartitionSpec as P

STENCIL = (0.8, -0.2, 4.0 / 105.0, -1.0 / 280.0)
TIME_SCALE = 4.0
FLOW_VELOCITY = 1.0
AXIAL_DISPERSION = 0.3
RADIAL_SPREADING = 0.2
BINDING_STRENGTH = (1.5, 0.6)
HEAT_EXPONENT = (0.5, 0.3)
KINETIC = (1.2, 0.7)
CAPACITY = (2.0, 1.0)
SORPTION_HEAT = (0.4, 0.25)
PURGE_GAIN = 1.5

REACH = len(STENCIL)
WEIGHTS = tuple(TIME_SCALE * c for c in STENCIL)
MOVING = (0, 1, 2, 5)
CENTRE = FLOW_VELOCITY + 2.0 * AXIAL_DISPERSION + 2.0 * RADIAL_SPREADING
UPWIND = FLOW_VELOCITY + AXIAL_DISPERSION
LAST = 1
SPARED = (2, 1)
VIA = (9,)


def is_odd():
    return lax.rem(lax.axis_index("tm"), 2) == 1


def shifted(x, step, edge):
    cells = x.shape[0]
    row = lax.broadcasted_iota(jnp.int32, x.shape, 0)
    if step > 0:
        return jnp.where(row == 0, edge, pltpu.roll(x, 1, 0))
    return jnp.where(row == cells - 1, edge, pltpu.roll(x, cells - 1, 0))


def radial_pair(x):
    width = x.shape[1]
    lane = lax.broadcasted_iota(jnp.int32, x.shape, 1)
    lower = jnp.where(lane == 0, 0.0, pltpu.roll(x, 1, 1))
    upper = jnp.where(lane == width - 1, 0.0, pltpu.roll(x, width - 1, 1))
    return lower + upper


def transport(x, near, far):
    return CENTRE * x - UPWIND * near - AXIAL_DISPERSION * far - RADIAL_SPREADING * radial_pair(x)


def pick_kernel(state, adjoint, edge):
    instances, _, beds, cells, _ = state.shape
    first = lax.axis_index("sec") == 0

    def step(t, carry):
        for n, x in enumerate((state, adjoint)):
            for k, c in enumerate(MOVING):
                for b in range(beds):
                    row = jnp.where(first, x[t, c, b, cells - 1 :], x[t, c, b, :1])
                    edge[t, n * len(MOVING) + k, b : b + 1] = row
        return carry

    lax.fori_loop(0, instances, step, 0)


def from_before(line, t):
    total = 0.0
    for j in range(t, len(line)):
        total = total + WEIGHTS[t + len(line) - j - 1] * line[j]
    return total


def main_kernel(plan, valve, state, adjoint, edge, in_state, in_adjoint, res, adj):
    instances, comps, beds, cells, _ = res.shape
    odd = is_odd()
    first = lax.axis_index("sec") == 0
    last = lax.axis_index("sec") == lax.axis_size("sec") - 1

    def cell_block(i, carry):
        t = i // beds
        b = lax.rem(i, beds)
        x = [state[t, c, b] for c in range(comps)]
        m = [adjoint[t, c, b] for c in range(comps)]
        y1, y2, _, q1, q2, temp = x
        b1 = BINDING_STRENGTH[0] * jnp.exp(HEAT_EXPONENT[0] * temp)
        b2 = BINDING_STRENGTH[1] * jnp.exp(HEAT_EXPONENT[1] * temp)
        over = 1.0 / (1.0 + b1 * y1 + b2 * y2)
        slope1 = b1 * over
        slope2 = b2 * over
        cover1 = slope1 * y1
        cover2 = slope2 * y2
        rate1 = KINETIC[0] * (CAPACITY[0] * cover1 - q1)
        rate2 = KINETIC[1] * (CAPACITY[1] * cover2 - q2)
        m1 = m[0] - m[3] - SORPTION_HEAT[0] * m[5]
        m2 = m[1] - m[4] - SORPTION_HEAT[1] * m[5]
        g1 = (KINETIC[0] * CAPACITY[0]) * m1
        g2 = (KINETIC[1] * CAPACITY[1]) * m2
        h = g1 * cover1 + g2 * cover2
        e1 = g1 - h
        e2 = g2 - h
        source = {0: rate1, 1: rate2, 5: -SORPTION_HEAT[0] * rate1 - SORPTION_HEAT[1] * rate2}
        pulled = {
            0: slope1 * e1,
            1: slope2 * e2,
            5: HEAT_EXPONENT[0] * cover1 * e1 + HEAT_EXPONENT[1] * cover2 * e2,
        }
        for k, c in enumerate(MOVING):
            from_x = edge[t, k, b][None]
            from_m = edge[t, len(MOVING) + k, b][None]
            below_x = jnp.where(first, 0.0, from_x)
            above_x = jnp.where(last, 0.0, from_x)
            below_m = jnp.where(first, 0.0, from_m)
            above_m = jnp.where(last, 0.0, from_m)
            r = transport(x[c], shifted(x[c], 1, below_x), shifted(x[c], -1, above_x))
            a = transport(m[c], shifted(m[c], -1, above_m), shifted(m[c], 1, below_m))
            res[t, c, b] = r + source[c] if c in source else r
            adj[t, c, b] = a + pulled[c] if c in pulled else a
        res[t, 3, b] = -rate1
        res[t, 4, b] = -rate2
        adj[t, 3, b] = -KINETIC[0] * m1
        adj[t, 4, b] = -KINETIC[1] * m2
        return carry

    lax.fori_loop(0, instances * beds, cell_block, 0)

    @pl.when(last)
    def _():
        def purge(i, carry):
            t = i // beds
            b = lax.rem(i, beds)
            s = lax.rem(b + plan[t, b], beds)
            gain = PURGE_GAIN * valve[t, b].astype(jnp.float32)
            end = pl.ds(cells - 1, 1)
            for c in range(3):
                res[t, c, b, end] += gain * (state[t, c, b, end] - state[t, c, s, end])
                flow = gain * adjoint[t, c, b, end]
                adj[t, c, b, end] += flow
                adj[t, c, s, end] -= flow
            return carry

        lax.fori_loop(0, instances * beds, purge, 0)

    sign = jnp.where(odd, -1.0, 1.0)
    at = [jnp.where(odd, instances - 1 - t, t) for t in range(instances)]

    def time_block(i, carry):
        c = i // beds
        b = lax.rem(i, beds)
        for own, near, out, factor in ((state, in_state, res, sign), (adjoint, in_adjoint, adj, -sign)):
            line = [own[at[t], c, b] for t in range(instances)]
            line += [near[at[t], c, b] for t in range(instances)]
            for t in range(instances):
                total = 0.0
                for k in range(1, REACH + 1):
                    diff = line[t + k]
                    if t - k >= 0:
                        diff = diff - line[t - k]
                    total = total + WEIGHTS[k - 1] * diff
                out[at[t], c, b] += factor * total
        return carry

    lax.fori_loop(0, comps * beds, time_block, 0)


def finish_kernel(scale, low, part, *rest):
    came, (out, whole, sem) = rest[:-4], rest[-3:]
    instances, size, beds, _, _ = whole.shape
    ways = [(ref, b) for ref in came for b in range(ref.shape[2])]
    extra = len(ways) - beds

    def moved(c):
        return pltpu.make_async_copy(whole.at[:, pl.ds(c, 1)], out.at[:, pl.ds(low + c, 1)], sem.at[c])

    def finish(sign, at):
        def component(c, carry):
            for b in range(beds):
                both = ways[b : b + 1] + (ways[b + extra : b + extra + 1] if b >= beds - extra else [])
                line = [sum(ref[at[t], c, place] for ref, place in both) for t in range(instances)]
                for t in range(instances):
                    whole[at[t], c, b] = part[at[t], low + c, b] - sign * from_before(line, t)
            moved(c).start()
            return carry

        lax.fori_loop(0, size, component, 0)

    odd = is_odd()

    @pl.when(odd)
    def _():
        finish(-scale, list(reversed(range(instances))))

    @pl.when(jnp.logical_not(odd))
    def _():
        finish(scale, list(range(instances)))

    for c in range(size):
        moved(c).wait()


VMEM = pl.BlockSpec(memory_space=pltpu.VMEM)
SMEM = pl.BlockSpec(memory_space=pltpu.SMEM)
ANY = pl.BlockSpec(memory_space=pl.ANY)
SMALL = pl.CostEstimate(flops=1000, bytes_accessed=1000, transcendentals=0)


def params(mib):
    return pltpu.CompilerParams(vmem_limit_bytes=mib * 2**20)


def local(state, adjoint, plan, valve):
    count = lax.axis_size("tm")
    sections = lax.axis_size("sec")
    instances, comps, beds, _, width = state.shape
    block = jax.ShapeDtypeStruct(state.shape, state.dtype)
    cells = jax.ShapeDtypeStruct((instances, 2 * len(MOVING), beds, width), state.dtype)
    across = [(i, (i + 1) % count if i % 2 else (i - 1) % count) for i in range(count)]
    on_chip = [(i, i ^ 1) for i in range(count)]
    far_state = lax.ppermute(state, "tm", across)
    cut = comps - LAST
    via = [i for i in VIA if i < count]
    kept = beds - len(via)
    far_adjoint = [
        lax.ppermute(adjoint[:, :cut], "tm", across),
        lax.ppermute(adjoint[:, cut:, :kept], "tm", across),
        lax.ppermute(adjoint[:, cut:, kept:], "tm", [pair for pair in across if pair != SPARED]),
    ]

    def near_transfers():
        in_state = lax.ppermute(state, "tm", on_chip)
        in_adjoint = lax.ppermute(adjoint, "tm", on_chip)
        edge = pl.pallas_call(
            pick_kernel,
            out_shape=cells,
            in_specs=[VMEM, VMEM],
            out_specs=VMEM,
            compiler_params=params(16),
            cost_estimate=SMALL,
            name="pick",
        )(state, adjoint)
        return lax.ppermute(edge, "sec", [(i, i ^ 1) for i in range(sections)]), in_state, in_adjoint

    def nothing():
        return jnp.zeros(cells.shape, cells.dtype), state, adjoint

    near = lax.cond(lax.axis_index("tm") % 2 >= 0, near_transfers, nothing)
    beds_of = [adjoint[:, cut:, kept + n : kept + n + 1] for n in range(len(via))]
    half_way = [lax.ppermute(x, "tm", [(SPARED[0], i)]) for x, i in zip(beds_of, via)]
    far_adjoint += [lax.ppermute(x, "tm", [(i, SPARED[1])]) for x, i in zip(half_way, via)]
    res, adj = pl.pallas_call(
        main_kernel,
        out_shape=(block, block),
        in_specs=[SMEM] * 2 + [VMEM] * 5,
        out_specs=(VMEM, VMEM),
        compiler_params=params(24),
        cost_estimate=SMALL,
        name="local_part",
    )(plan, valve, state, adjoint, *near)

    def finish(name, scale, low, part, came, before):
        size = came[0].shape[1]
        return pl.pallas_call(
            functools.partial(finish_kernel, scale, low),
            out_shape=block,
            in_specs=[VMEM] * (1 + len(came)) + [ANY],
            out_specs=ANY,
            scratch_shapes=[
                pltpu.VMEM((instances, size) + state.shape[2:], state.dtype),
                pltpu.SemaphoreType.DMA((size,)),
            ],
            input_output_aliases={1 + len(came): 0} if before.shape == block.shape else {},
            compiler_params=params(16),
            cost_estimate=SMALL,
            name=name,
        )(part, *came, before)

    residual = finish("finish_residual", 1.0, 0, res, [far_state], plan)
    begun = finish("finish_adjoint", -1.0, 0, adj, far_adjoint[:1], residual[0, 0, 0, :8])
    return residual, finish("finish_last", -1.0, cut, adj, far_adjoint[1:], begun)


def solution(mesh):
    spec = P("tm", None, None, "sec", None)
    return jax.shard_map(
        local,
        mesh=mesh,
        in_specs=(spec, spec, P("tm", None), P("tm", None)),
        out_specs=(spec, spec),
        check_vma=False,
    )
```

```python
import functools

import jax
import jax.numpy as jnp
from jax import lax
from jax.experimental import pallas as pl
from jax.experimental.pallas import tpu as pltpu
from jax.sharding import PartitionSpec as P

STENCIL = (0.8, -0.2, 4.0 / 105.0, -1.0 / 280.0)
TIME_SCALE = 4.0
FLOW_VELOCITY = 1.0
AXIAL_DISPERSION = 0.3
RADIAL_SPREADING = 0.2
BINDING_STRENGTH = (1.5, 0.6)
HEAT_EXPONENT = (0.5, 0.3)
KINETIC = (1.2, 0.7)
CAPACITY = (2.0, 1.0)
SORPTION_HEAT = (0.4, 0.25)
PURGE_GAIN = 1.5

REACH = len(STENCIL)
WEIGHTS = tuple(TIME_SCALE * c for c in STENCIL)
MOVING = (0, 1, 2, 5)
CENTRE = FLOW_VELOCITY + 2.0 * AXIAL_DISPERSION + 2.0 * RADIAL_SPREADING
UPWIND = FLOW_VELOCITY + AXIAL_DISPERSION
LAST = 1


def is_odd():
    return lax.rem(lax.axis_index("tm"), 2) == 1


def shifted(x, step, edge):
    cells = x.shape[0]
    row = lax.broadcasted_iota(jnp.int32, x.shape, 0)
    if step > 0:
        return jnp.where(row == 0, edge, pltpu.roll(x, 1, 0))
    return jnp.where(row == cells - 1, edge, pltpu.roll(x, cells - 1, 0))


def radial_pair(x):
    width = x.shape[1]
    lane = lax.broadcasted_iota(jnp.int32, x.shape, 1)
    lower = jnp.where(lane == 0, 0.0, pltpu.roll(x, 1, 1))
    upper = jnp.where(lane == width - 1, 0.0, pltpu.roll(x, width - 1, 1))
    return lower + upper


def transport(x, near, far):
    return CENTRE * x - UPWIND * near - AXIAL_DISPERSION * far - RADIAL_SPREADING * radial_pair(x)


def pick_kernel(state, adjoint, edge):
    instances, _, beds, cells, _ = state.shape
    first = lax.axis_index("sec") == 0

    def step(t, carry):
        for n, x in enumerate((state, adjoint)):
            for k, c in enumerate(MOVING):
                for b in range(beds):
                    row = jnp.where(first, x[t, c, b, cells - 1 :], x[t, c, b, :1])
                    edge[t, n * len(MOVING) + k, b : b + 1] = row
        return carry

    lax.fori_loop(0, instances, step, 0)


def from_before(line, t):
    total = 0.0
    for j in range(t, len(line)):
        total = total + WEIGHTS[t + len(line) - j - 1] * line[j]
    return total


def main_kernel(plan, valve, state, adjoint, edge, in_state, in_adjoint, res, adj, done):
    instances, comps, beds, cells, _ = res.shape
    done[...] = jnp.zeros_like(done)
    odd = is_odd()
    first = lax.axis_index("sec") == 0
    last = lax.axis_index("sec") == lax.axis_size("sec") - 1

    def cell_block(i, carry):
        t = i // beds
        b = lax.rem(i, beds)
        x = [state[t, c, b] for c in range(comps)]
        m = [adjoint[t, c, b] for c in range(comps)]
        y1, y2, _, q1, q2, temp = x
        b1 = BINDING_STRENGTH[0] * jnp.exp(HEAT_EXPONENT[0] * temp)
        b2 = BINDING_STRENGTH[1] * jnp.exp(HEAT_EXPONENT[1] * temp)
        over = 1.0 / (1.0 + b1 * y1 + b2 * y2)
        slope1 = b1 * over
        slope2 = b2 * over
        cover1 = slope1 * y1
        cover2 = slope2 * y2
        rate1 = KINETIC[0] * (CAPACITY[0] * cover1 - q1)
        rate2 = KINETIC[1] * (CAPACITY[1] * cover2 - q2)
        m1 = m[0] - m[3] - SORPTION_HEAT[0] * m[5]
        m2 = m[1] - m[4] - SORPTION_HEAT[1] * m[5]
        g1 = (KINETIC[0] * CAPACITY[0]) * m1
        g2 = (KINETIC[1] * CAPACITY[1]) * m2
        h = g1 * cover1 + g2 * cover2
        e1 = g1 - h
        e2 = g2 - h
        source = {0: rate1, 1: rate2, 5: -SORPTION_HEAT[0] * rate1 - SORPTION_HEAT[1] * rate2}
        pulled = {
            0: slope1 * e1,
            1: slope2 * e2,
            5: HEAT_EXPONENT[0] * cover1 * e1 + HEAT_EXPONENT[1] * cover2 * e2,
        }
        for k, c in enumerate(MOVING):
            from_x = edge[t, k, b][None]
            from_m = edge[t, len(MOVING) + k, b][None]
            below_x = jnp.where(first, 0.0, from_x)
            above_x = jnp.where(last, 0.0, from_x)
            below_m = jnp.where(first, 0.0, from_m)
            above_m = jnp.where(last, 0.0, from_m)
            r = transport(x[c], shifted(x[c], 1, below_x), shifted(x[c], -1, above_x))
            a = transport(m[c], shifted(m[c], -1, above_m), shifted(m[c], 1, below_m))
            res[t, c, b] = r + source[c] if c in source else r
            adj[t, c, b] = a + pulled[c] if c in pulled else a
        res[t, 3, b] = -rate1
        res[t, 4, b] = -rate2
        adj[t, 3, b] = -KINETIC[0] * m1
        adj[t, 4, b] = -KINETIC[1] * m2
        return carry

    lax.fori_loop(0, instances * beds, cell_block, 0)

    @pl.when(last)
    def _():
        def purge(i, carry):
            t = i // beds
            b = lax.rem(i, beds)
            s = lax.rem(b + plan[t, b], beds)
            gain = PURGE_GAIN * valve[t, b].astype(jnp.float32)
            end = pl.ds(cells - 1, 1)
            for c in range(3):
                res[t, c, b, end] += gain * (state[t, c, b, end] - state[t, c, s, end])
                flow = gain * adjoint[t, c, b, end]
                adj[t, c, b, end] += flow
                adj[t, c, s, end] -= flow
            return carry

        lax.fori_loop(0, instances * beds, purge, 0)

    sign = jnp.where(odd, -1.0, 1.0)
    at = [jnp.where(odd, instances - 1 - t, t) for t in range(instances)]

    def time_block(i, carry):
        c = i // beds
        b = lax.rem(i, beds)
        for own, near, out, factor in ((state, in_state, res, sign), (adjoint, in_adjoint, adj, -sign)):
            line = [own[at[t], c, b] for t in range(instances)]
            line += [near[at[t], c, b] for t in range(instances)]
            for t in range(instances):
                total = 0.0
                for k in range(1, REACH + 1):
                    diff = line[t + k]
                    if t - k >= 0:
                        diff = diff - line[t - k]
                    total = total + WEIGHTS[k - 1] * diff
                out[at[t], c, b] += factor * total
        return carry

    lax.fori_loop(0, comps * beds, time_block, 0)


def after_kernel(passed, before, out):
    del passed, before, out


def finish_kernel(scale, low, part, came, before, out, whole, sem):
    del before
    instances, size, beds, _, _ = came.shape

    def moved(c):
        return pltpu.make_async_copy(whole.at[:, pl.ds(c, 1)], out.at[:, pl.ds(low + c, 1)], sem.at[c])

    def finish(sign, at):
        def component(c, carry):
            for b in range(beds):
                line = [came[at[t], c, b] for t in range(instances)]
                for t in range(instances):
                    whole[at[t], c, b] = part[at[t], low + c, b] - sign * from_before(line, t)
            moved(c).start()
            return carry

        lax.fori_loop(0, size, component, 0)

    odd = is_odd()

    @pl.when(odd)
    def _():
        finish(-scale, list(reversed(range(instances))))

    @pl.when(jnp.logical_not(odd))
    def _():
        finish(scale, list(range(instances)))

    for c in range(size):
        moved(c).wait()


VMEM = pl.BlockSpec(memory_space=pltpu.VMEM)
SMEM = pl.BlockSpec(memory_space=pltpu.SMEM)
ANY = pl.BlockSpec(memory_space=pl.ANY)
SMALL = pl.CostEstimate(flops=1000, bytes_accessed=1000, transcendentals=0)


def params(mib):
    return pltpu.CompilerParams(vmem_limit_bytes=mib * 2**20)


def hops(count):
    first = {0: -4, 1: 1, 2: -1, 3: 4}
    second = {0: 3, 1: 0, 2: 0, 3: -3}
    return [[(i, (i + hop[i % 4]) % count) for i in range(count)] for hop in (first, second)]


def local(state, adjoint, plan, valve):
    count = lax.axis_size("tm")
    sections = lax.axis_size("sec")
    instances, comps, beds, _, width = state.shape
    block = jax.ShapeDtypeStruct(state.shape, state.dtype)
    cells = jax.ShapeDtypeStruct((instances, 2 * len(MOVING), beds, width), state.dtype)
    first, second = hops(count)
    on_chip = [(i, i ^ 1) for i in range(count)]
    passed_state = lax.ppermute(state, "tm", first)
    passed_adjoint = lax.ppermute(adjoint, "tm", first)

    def after(passed, before, name):
        return pl.pallas_call(
            after_kernel,
            out_shape=block,
            in_specs=[ANY, ANY],
            out_specs=ANY,
            input_output_aliases={0: 0},
            compiler_params=params(1),
            cost_estimate=SMALL,
            name=name,
        )(passed, before)

    def near_transfers():
        in_state = lax.ppermute(state, "tm", on_chip)
        in_adjoint = lax.ppermute(adjoint, "tm", on_chip)
        edge = pl.pallas_call(
            pick_kernel,
            out_shape=cells,
            in_specs=[VMEM, VMEM],
            out_specs=VMEM,
            compiler_params=params(16),
            cost_estimate=SMALL,
            name="pick",
        )(state, adjoint)
        return lax.ppermute(edge, "sec", [(i, i ^ 1) for i in range(sections)]), in_state, in_adjoint

    def nothing():
        return jnp.zeros(cells.shape, cells.dtype), state, adjoint

    near = lax.cond(lax.axis_index("tm") % 2 >= 0, near_transfers, nothing)
    far_state = lax.ppermute(after(passed_state, near[0], "state_after"), "tm", second)
    res, adj, done = pl.pallas_call(
        main_kernel,
        out_shape=(block, block, jax.ShapeDtypeStruct((8, 128), state.dtype)),
        in_specs=[SMEM] * 2 + [VMEM] * 5,
        out_specs=(VMEM, VMEM, VMEM),
        compiler_params=params(24),
        cost_estimate=SMALL,
        name="local_part",
    )(plan, valve, state, adjoint, *near)

    passed_adjoint = after(passed_adjoint, done, "adjoint_after")
    cut = comps - LAST
    far_adjoint = [lax.ppermute(x, "tm", second) for x in (passed_adjoint[:, :cut], passed_adjoint[:, cut:])]

    def finish(name, scale, low, part, came, before):
        return pl.pallas_call(
            functools.partial(finish_kernel, scale, low),
            out_shape=block,
            in_specs=[VMEM, VMEM, ANY],
            out_specs=ANY,
            scratch_shapes=[pltpu.VMEM(came.shape, came.dtype), pltpu.SemaphoreType.DMA((came.shape[1],))],
            input_output_aliases={2: 0} if before.shape == block.shape else {},
            compiler_params=params(16),
            cost_estimate=SMALL,
            name=name,
        )(part, came, before)

    residual = finish("finish_residual", 1.0, 0, res, far_state, plan)
    begun = finish("finish_adjoint", -1.0, 0, adj, far_adjoint[0], residual[0, 0, 0, :8])
    return residual, finish("finish_last", -1.0, cut, adj, far_adjoint[1], begun)


def solution(mesh):
    spec = P("tm", None, None, "sec", None)
    return jax.shard_map(
        local,
        mesh=mesh,
        in_specs=(spec, spec, P("tm", None), P("tm", None)),
        out_specs=(spec, spec),
        check_vma=False,
    )
```

```python
import functools

import jax
import jax.numpy as jnp
from jax import lax
from jax.experimental import pallas as pl
from jax.experimental.pallas import tpu as pltpu
from jax.sharding import PartitionSpec as P

STENCIL = (0.8, -0.2, 4.0 / 105.0, -1.0 / 280.0)
TIME_SCALE = 4.0
FLOW_VELOCITY = 1.0
AXIAL_DISPERSION = 0.3
RADIAL_SPREADING = 0.2
BINDING_STRENGTH = (1.5, 0.6)
HEAT_EXPONENT = (0.5, 0.3)
KINETIC = (1.2, 0.7)
CAPACITY = (2.0, 1.0)
SORPTION_HEAT = (0.4, 0.25)
PURGE_GAIN = 1.5

REACH = len(STENCIL)
WEIGHTS = tuple(TIME_SCALE * c for c in STENCIL)
MOVING = (0, 1, 2, 5)
CENTRE = FLOW_VELOCITY + 2.0 * AXIAL_DISPERSION + 2.0 * RADIAL_SPREADING
UPWIND = FLOW_VELOCITY + AXIAL_DISPERSION
LAST = 1
SPARED = (2, 1)
VIA = (9,)


def is_odd():
    return lax.rem(lax.axis_index("tm"), 2) == 1


def shifted(x, step, edge):
    cells = x.shape[0]
    row = lax.broadcasted_iota(jnp.int32, x.shape, 0)
    if step > 0:
        return jnp.where(row == 0, edge, pltpu.roll(x, 1, 0))
    return jnp.where(row == cells - 1, edge, pltpu.roll(x, cells - 1, 0))


def radial_pair(x):
    width = x.shape[1]
    lane = lax.broadcasted_iota(jnp.int32, x.shape, 1)
    lower = jnp.where(lane == 0, 0.0, pltpu.roll(x, 1, 1))
    upper = jnp.where(lane == width - 1, 0.0, pltpu.roll(x, width - 1, 1))
    return lower + upper


def transport(x, near, far):
    return CENTRE * x - UPWIND * near - AXIAL_DISPERSION * far - RADIAL_SPREADING * radial_pair(x)


def pick_kernel(state, adjoint, edge):
    instances, _, beds, cells, _ = state.shape
    first = lax.axis_index("sec") == 0

    def step(t, carry):
        for n, x in enumerate((state, adjoint)):
            for k, c in enumerate(MOVING):
                for b in range(beds):
                    row = jnp.where(first, x[t, c, b, cells - 1 :], x[t, c, b, :1])
                    edge[t, n * len(MOVING) + k, b : b + 1] = row
        return carry

    lax.fori_loop(0, instances, step, 0)


def from_before(line, t):
    total = 0.0
    for j in range(t, len(line)):
        total = total + WEIGHTS[t + len(line) - j - 1] * line[j]
    return total


def main_kernel(plan, valve, state, adjoint, edge, in_state, in_adjoint, res, adj):
    instances, comps, beds, cells, _ = res.shape
    odd = is_odd()
    first = lax.axis_index("sec") == 0
    last = lax.axis_index("sec") == lax.axis_size("sec") - 1

    def cell_block(i, carry):
        t = i // beds
        b = lax.rem(i, beds)
        x = [state[t, c, b] for c in range(comps)]
        m = [adjoint[t, c, b] for c in range(comps)]
        y1, y2, _, q1, q2, temp = x
        b1 = BINDING_STRENGTH[0] * jnp.exp(HEAT_EXPONENT[0] * temp)
        b2 = BINDING_STRENGTH[1] * jnp.exp(HEAT_EXPONENT[1] * temp)
        over = 1.0 / (1.0 + b1 * y1 + b2 * y2)
        slope1 = b1 * over
        slope2 = b2 * over
        cover1 = slope1 * y1
        cover2 = slope2 * y2
        rate1 = KINETIC[0] * (CAPACITY[0] * cover1 - q1)
        rate2 = KINETIC[1] * (CAPACITY[1] * cover2 - q2)
        m1 = m[0] - m[3] - SORPTION_HEAT[0] * m[5]
        m2 = m[1] - m[4] - SORPTION_HEAT[1] * m[5]
        g1 = (KINETIC[0] * CAPACITY[0]) * m1
        g2 = (KINETIC[1] * CAPACITY[1]) * m2
        h = g1 * cover1 + g2 * cover2
        e1 = g1 - h
        e2 = g2 - h
        source = {0: rate1, 1: rate2, 5: -SORPTION_HEAT[0] * rate1 - SORPTION_HEAT[1] * rate2}
        pulled = {
            0: slope1 * e1,
            1: slope2 * e2,
            5: HEAT_EXPONENT[0] * cover1 * e1 + HEAT_EXPONENT[1] * cover2 * e2,
        }
        for k, c in enumerate(MOVING):
            from_x = edge[t, k, b][None]
            from_m = edge[t, len(MOVING) + k, b][None]
            below_x = jnp.where(first, 0.0, from_x)
            above_x = jnp.where(last, 0.0, from_x)
            below_m = jnp.where(first, 0.0, from_m)
            above_m = jnp.where(last, 0.0, from_m)
            r = transport(x[c], shifted(x[c], 1, below_x), shifted(x[c], -1, above_x))
            a = transport(m[c], shifted(m[c], -1, above_m), shifted(m[c], 1, below_m))
            res[t, c, b] = r + source[c] if c in source else r
            adj[t, c, b] = a + pulled[c] if c in pulled else a
        res[t, 3, b] = -rate1
        res[t, 4, b] = -rate2
        adj[t, 3, b] = -KINETIC[0] * m1
        adj[t, 4, b] = -KINETIC[1] * m2
        return carry

    lax.fori_loop(0, instances * beds, cell_block, 0)

    @pl.when(last)
    def _():
        def purge(i, carry):
            t = i // beds
            b = lax.rem(i, beds)
            s = lax.rem(b + plan[t, b], beds)
            gain = PURGE_GAIN * valve[t, b].astype(jnp.float32)
            end = pl.ds(cells - 1, 1)
            for c in range(3):
                res[t, c, b, end] += gain * (state[t, c, b, end] - state[t, c, s, end])
                flow = gain * adjoint[t, c, b, end]
                adj[t, c, b, end] += flow
                adj[t, c, s, end] -= flow
            return carry

        lax.fori_loop(0, instances * beds, purge, 0)

    sign = jnp.where(odd, -1.0, 1.0)
    at = [jnp.where(odd, instances - 1 - t, t) for t in range(instances)]

    def time_block(i, carry):
        c = i // beds
        b = lax.rem(i, beds)
        for own, near, out, factor in ((state, in_state, res, sign), (adjoint, in_adjoint, adj, -sign)):
            line = [own[at[t], c, b] for t in range(instances)]
            line += [near[at[t], c, b] for t in range(instances)]
            for t in range(instances):
                total = 0.0
                for k in range(1, REACH + 1):
                    diff = line[t + k]
                    if t - k >= 0:
                        diff = diff - line[t - k]
                    total = total + WEIGHTS[k - 1] * diff
                out[at[t], c, b] += factor * total
        return carry

    lax.fori_loop(0, comps * beds, time_block, 0)


def finish_kernel(scale, low, part, *rest):
    came, (out, whole, sem) = rest[:-4], rest[-3:]
    instances, size, beds, _, _ = whole.shape
    ways = [(ref, b) for ref in came for b in range(ref.shape[2])]
    extra = len(ways) - beds

    def moved(c, b):
        return pltpu.make_async_copy(
            whole.at[:, pl.ds(c, 1), pl.ds(b, 1)], out.at[:, pl.ds(low + c, 1), pl.ds(b, 1)], sem.at[c, b]
        )

    def finish(sign, at):
        def component(c, carry):
            for b in range(beds):
                both = ways[b : b + 1] + (ways[b + extra : b + extra + 1] if b >= beds - extra else [])
                line = [sum(ref[at[t], c, place] for ref, place in both) for t in range(instances)]
                for t in range(instances):
                    whole[at[t], c, b] = part[at[t], low + c, b] - sign * from_before(line, t)
                moved(c, b).start()
            return carry

        lax.fori_loop(0, size, component, 0)

    odd = is_odd()

    @pl.when(odd)
    def _():
        finish(-scale, list(reversed(range(instances))))

    @pl.when(jnp.logical_not(odd))
    def _():
        finish(scale, list(range(instances)))

    for c in range(size):
        for b in range(beds):
            moved(c, b).wait()


VMEM = pl.BlockSpec(memory_space=pltpu.VMEM)
SMEM = pl.BlockSpec(memory_space=pltpu.SMEM)
ANY = pl.BlockSpec(memory_space=pl.ANY)
SMALL = pl.CostEstimate(flops=1000, bytes_accessed=1000, transcendentals=0)


def params(mib):
    return pltpu.CompilerParams(vmem_limit_bytes=mib * 2**20)


def local(state, adjoint, plan, valve):
    count = lax.axis_size("tm")
    sections = lax.axis_size("sec")
    instances, comps, beds, _, width = state.shape
    block = jax.ShapeDtypeStruct(state.shape, state.dtype)
    cells = jax.ShapeDtypeStruct((instances, 2 * len(MOVING), beds, width), state.dtype)
    across = [(i, (i + 1) % count if i % 2 else (i - 1) % count) for i in range(count)]
    on_chip = [(i, i ^ 1) for i in range(count)]
    far_state = lax.ppermute(state, "tm", across)
    cut = comps - LAST
    via = [i for i in VIA if i < count]
    kept = beds - len(via)
    far_adjoint = [
        lax.ppermute(adjoint[:, :cut], "tm", across),
        lax.ppermute(adjoint[:, cut:, :kept], "tm", across),
        lax.ppermute(adjoint[:, cut:, kept:], "tm", [pair for pair in across if pair != SPARED]),
    ]

    def near_transfers():
        in_state = lax.ppermute(state, "tm", on_chip)
        in_adjoint = lax.ppermute(adjoint, "tm", on_chip)
        edge = pl.pallas_call(
            pick_kernel,
            out_shape=cells,
            in_specs=[VMEM, VMEM],
            out_specs=VMEM,
            compiler_params=params(16),
            cost_estimate=SMALL,
            name="pick",
        )(state, adjoint)
        return lax.ppermute(edge, "sec", [(i, i ^ 1) for i in range(sections)]), in_state, in_adjoint

    def nothing():
        return jnp.zeros(cells.shape, cells.dtype), state, adjoint

    near = lax.cond(lax.axis_index("tm") % 2 >= 0, near_transfers, nothing)
    beds_of = [adjoint[:, cut:, kept + n : kept + n + 1] for n in range(len(via))]
    half_way = [lax.ppermute(x, "tm", [(SPARED[0], i)]) for x, i in zip(beds_of, via)]
    far_adjoint += [lax.ppermute(x, "tm", [(i, SPARED[1])]) for x, i in zip(half_way, via)]
    res, adj = pl.pallas_call(
        main_kernel,
        out_shape=(block, block),
        in_specs=[SMEM] * 2 + [VMEM] * 5,
        out_specs=(VMEM, VMEM),
        compiler_params=params(24),
        cost_estimate=SMALL,
        name="local_part",
    )(plan, valve, state, adjoint, *near)

    def finish(name, scale, low, part, came, before):
        size = came[0].shape[1]
        return pl.pallas_call(
            functools.partial(finish_kernel, scale, low),
            out_shape=block,
            in_specs=[VMEM] * (1 + len(came)) + [ANY],
            out_specs=ANY,
            scratch_shapes=[
                pltpu.VMEM((instances, size) + state.shape[2:], state.dtype),
                pltpu.SemaphoreType.DMA((size, beds)),
            ],
            input_output_aliases={1 + len(came): 0} if before.shape == block.shape else {},
            compiler_params=params(16),
            cost_estimate=SMALL,
            name=name,
        )(part, *came, before)

    residual = finish("finish_residual", 1.0, 0, res, [far_state], plan)
    begun = finish("finish_adjoint", -1.0, 0, adj, far_adjoint[:1], residual[0, 0, 0, :8])
    return residual, finish("finish_last", -1.0, cut, adj, far_adjoint[1:], begun)


def solution(mesh):
    spec = P("tm", None, None, "sec", None)
    return jax.shard_map(
        local,
        mesh=mesh,
        in_specs=(spec, spec, P("tm", None), P("tm", None)),
        out_specs=(spec, spec),
        check_vma=False,
    )
```

```python
import functools

import jax
import jax.numpy as jnp
from jax import lax
from jax.experimental import pallas as pl
from jax.experimental.pallas import tpu as pltpu
from jax.sharding import PartitionSpec as P

STENCIL = (0.8, -0.2, 4.0 / 105.0, -1.0 / 280.0)
TIME_SCALE = 4.0
FLOW_VELOCITY = 1.0
AXIAL_DISPERSION = 0.3
RADIAL_SPREADING = 0.2
BINDING_STRENGTH = (1.5, 0.6)
HEAT_EXPONENT = (0.5, 0.3)
KINETIC = (1.2, 0.7)
CAPACITY = (2.0, 1.0)
SORPTION_HEAT = (0.4, 0.25)
PURGE_GAIN = 1.5

REACH = len(STENCIL)
WEIGHTS = tuple(TIME_SCALE * c for c in STENCIL)
MOVING = (0, 1, 2, 5)
CENTRE = FLOW_VELOCITY + 2.0 * AXIAL_DISPERSION + 2.0 * RADIAL_SPREADING
UPWIND = FLOW_VELOCITY + AXIAL_DISPERSION
LAST = 1
SPARED = (2, 1)
VIA = (9,)


def is_odd():
    return lax.rem(lax.axis_index("tm"), 2) == 1


def shifted(x, step, edge):
    cells = x.shape[0]
    row = lax.broadcasted_iota(jnp.int32, x.shape, 0)
    if step > 0:
        return jnp.where(row == 0, edge, pltpu.roll(x, 1, 0))
    return jnp.where(row == cells - 1, edge, pltpu.roll(x, cells - 1, 0))


def radial_pair(x):
    width = x.shape[1]
    lane = lax.broadcasted_iota(jnp.int32, x.shape, 1)
    lower = jnp.where(lane == 0, 0.0, pltpu.roll(x, 1, 1))
    upper = jnp.where(lane == width - 1, 0.0, pltpu.roll(x, width - 1, 1))
    return lower + upper


def transport(x, near, far):
    return CENTRE * x - UPWIND * near - AXIAL_DISPERSION * far - RADIAL_SPREADING * radial_pair(x)


def pick_kernel(state, adjoint, edge):
    instances, _, beds, cells, _ = state.shape
    first = lax.axis_index("sec") == 0

    def step(t, carry):
        for n, x in enumerate((state, adjoint)):
            for k, c in enumerate(MOVING):
                for b in range(beds):
                    row = jnp.where(first, x[t, c, b, cells - 1 :], x[t, c, b, :1])
                    edge[t, n * len(MOVING) + k, b : b + 1] = row
        return carry

    lax.fori_loop(0, instances, step, 0)


def from_before(line, t):
    total = 0.0
    for j in range(t, len(line)):
        total = total + WEIGHTS[t + len(line) - j - 1] * line[j]
    return total


def main_kernel(plan, valve, state, adjoint, edge, in_state, in_adjoint, res, adj):
    instances, comps, beds, cells, _ = res.shape
    odd = is_odd()
    first = lax.axis_index("sec") == 0
    last = lax.axis_index("sec") == lax.axis_size("sec") - 1

    def cell_block(i, carry):
        t = i // beds
        b = lax.rem(i, beds)
        x = [state[t, c, b] for c in range(comps)]
        m = [adjoint[t, c, b] for c in range(comps)]
        y1, y2, _, q1, q2, temp = x
        b1 = BINDING_STRENGTH[0] * jnp.exp(HEAT_EXPONENT[0] * temp)
        b2 = BINDING_STRENGTH[1] * jnp.exp(HEAT_EXPONENT[1] * temp)
        over = 1.0 / (1.0 + b1 * y1 + b2 * y2)
        slope1 = b1 * over
        slope2 = b2 * over
        cover1 = slope1 * y1
        cover2 = slope2 * y2
        rate1 = KINETIC[0] * (CAPACITY[0] * cover1 - q1)
        rate2 = KINETIC[1] * (CAPACITY[1] * cover2 - q2)
        m1 = m[0] - m[3] - SORPTION_HEAT[0] * m[5]
        m2 = m[1] - m[4] - SORPTION_HEAT[1] * m[5]
        g1 = (KINETIC[0] * CAPACITY[0]) * m1
        g2 = (KINETIC[1] * CAPACITY[1]) * m2
        h = g1 * cover1 + g2 * cover2
        e1 = g1 - h
        e2 = g2 - h
        source = {0: rate1, 1: rate2, 5: -SORPTION_HEAT[0] * rate1 - SORPTION_HEAT[1] * rate2}
        pulled = {
            0: slope1 * e1,
            1: slope2 * e2,
            5: HEAT_EXPONENT[0] * cover1 * e1 + HEAT_EXPONENT[1] * cover2 * e2,
        }
        for k, c in enumerate(MOVING):
            from_x = edge[t, k, b][None]
            from_m = edge[t, len(MOVING) + k, b][None]
            below_x = jnp.where(first, 0.0, from_x)
            above_x = jnp.where(last, 0.0, from_x)
            below_m = jnp.where(first, 0.0, from_m)
            above_m = jnp.where(last, 0.0, from_m)
            r = transport(x[c], shifted(x[c], 1, below_x), shifted(x[c], -1, above_x))
            a = transport(m[c], shifted(m[c], -1, above_m), shifted(m[c], 1, below_m))
            res[t, c, b] = r + source[c] if c in source else r
            adj[t, c, b] = a + pulled[c] if c in pulled else a
        res[t, 3, b] = -rate1
        res[t, 4, b] = -rate2
        adj[t, 3, b] = -KINETIC[0] * m1
        adj[t, 4, b] = -KINETIC[1] * m2
        return carry

    lax.fori_loop(0, instances * beds, cell_block, 0)

    @pl.when(last)
    def _():
        def purge(i, carry):
            t = i // beds
            b = lax.rem(i, beds)
            s = lax.rem(b + plan[t, b], beds)
            gain = PURGE_GAIN * valve[t, b].astype(jnp.float32)
            end = pl.ds(cells - 1, 1)
            for c in range(3):
                res[t, c, b, end] += gain * (state[t, c, b, end] - state[t, c, s, end])
                flow = gain * adjoint[t, c, b, end]
                adj[t, c, b, end] += flow
                adj[t, c, s, end] -= flow
            return carry

        lax.fori_loop(0, instances * beds, purge, 0)

    sign = jnp.where(odd, -1.0, 1.0)
    at = [jnp.where(odd, instances - 1 - t, t) for t in range(instances)]

    def time_block(i, carry):
        c = i // beds
        b = lax.rem(i, beds)
        for own, near, out, factor in ((state, in_state, res, sign), (adjoint, in_adjoint, adj, -sign)):
            line = [own[at[t], c, b] for t in range(instances)]
            line += [near[at[t], c, b] for t in range(instances)]
            for t in range(instances):
                total = 0.0
                for k in range(1, REACH + 1):
                    diff = line[t + k]
                    if t - k >= 0:
                        diff = diff - line[t - k]
                    total = total + WEIGHTS[k - 1] * diff
                out[at[t], c, b] += factor * total
        return carry

    lax.fori_loop(0, comps * beds, time_block, 0)


def finish_kernel(scale, low, part, *rest):
    came, (out, whole, sem) = rest[:-4], rest[-3:]
    instances, size, beds, _, _ = whole.shape
    ways = [(ref, b) for ref in came for b in range(ref.shape[2])]
    extra = len(ways) - beds

    def moved(c):
        return pltpu.make_async_copy(whole.at[:, pl.ds(c, 1)], out.at[:, pl.ds(low + c, 1)], sem.at[c])

    def finish(sign, at):
        def component(c, carry):
            for b in range(beds):
                both = ways[b : b + 1] + (ways[b + extra : b + extra + 1] if b >= beds - extra else [])
                line = [sum(ref[at[t], c, place] for ref, place in both) for t in range(instances)]
                for t in range(instances):
                    whole[at[t], c, b] = part[at[t], low + c, b] - sign * from_before(line, t)
            moved(c).start()
            return carry

        lax.fori_loop(0, size, component, 0)

    odd = is_odd()

    @pl.when(odd)
    def _():
        finish(-scale, list(reversed(range(instances))))

    @pl.when(jnp.logical_not(odd))
    def _():
        finish(scale, list(range(instances)))

    for c in range(size):
        moved(c).wait()


VMEM = pl.BlockSpec(memory_space=pltpu.VMEM)
SMEM = pl.BlockSpec(memory_space=pltpu.SMEM)
ANY = pl.BlockSpec(memory_space=pl.ANY)
SMALL = pl.CostEstimate(flops=1000, bytes_accessed=1000, transcendentals=0)


def params(mib):
    return pltpu.CompilerParams(vmem_limit_bytes=mib * 2**20)


def local(state, adjoint, plan, valve):
    count = lax.axis_size("tm")
    sections = lax.axis_size("sec")
    instances, comps, beds, _, width = state.shape
    block = jax.ShapeDtypeStruct(state.shape, state.dtype)
    cells = jax.ShapeDtypeStruct((instances, 2 * len(MOVING), beds, width), state.dtype)
    across = [(i, (i + 1) % count if i % 2 else (i - 1) % count) for i in range(count)]
    on_chip = [(i, i ^ 1) for i in range(count)]
    in_state = lax.ppermute(state, "tm", on_chip)
    far_state = lax.ppermute(state, "tm", across)
    cut = comps - LAST
    via = [i for i in VIA if i < count]
    kept = beds - len(via)
    far_adjoint = [
        lax.ppermute(adjoint[:, :cut], "tm", across),
        lax.ppermute(adjoint[:, cut:, :kept], "tm", across),
        lax.ppermute(adjoint[:, cut:, kept:], "tm", [pair for pair in across if pair != SPARED]),
    ]

    def near_transfers():
        in_adjoint = lax.ppermute(adjoint, "tm", on_chip)
        edge = pl.pallas_call(
            pick_kernel,
            out_shape=cells,
            in_specs=[VMEM, VMEM],
            out_specs=VMEM,
            compiler_params=params(16),
            cost_estimate=SMALL,
            name="pick",
        )(state, adjoint)
        return lax.ppermute(edge, "sec", [(i, i ^ 1) for i in range(sections)]), in_adjoint

    def nothing():
        return jnp.zeros(cells.shape, cells.dtype), adjoint

    edge, in_adjoint = lax.cond(lax.axis_index("tm") % 2 >= 0, near_transfers, nothing)
    beds_of = [adjoint[:, cut:, kept + n : kept + n + 1] for n in range(len(via))]
    half_way = [lax.ppermute(x, "tm", [(SPARED[0], i)]) for x, i in zip(beds_of, via)]
    far_adjoint += [lax.ppermute(x, "tm", [(i, SPARED[1])]) for x, i in zip(half_way, via)]
    res, adj = pl.pallas_call(
        main_kernel,
        out_shape=(block, block),
        in_specs=[SMEM] * 2 + [VMEM] * 5,
        out_specs=(VMEM, VMEM),
        compiler_params=params(24),
        cost_estimate=SMALL,
        name="local_part",
    )(plan, valve, state, adjoint, edge, in_state, in_adjoint)

    def finish(name, scale, low, part, came, before):
        size = came[0].shape[1]
        return pl.pallas_call(
            functools.partial(finish_kernel, scale, low),
            out_shape=block,
            in_specs=[VMEM] * (1 + len(came)) + [ANY],
            out_specs=ANY,
            scratch_shapes=[
                pltpu.VMEM((instances, size) + state.shape[2:], state.dtype),
                pltpu.SemaphoreType.DMA((size,)),
            ],
            input_output_aliases={1 + len(came): 0} if before.shape == block.shape else {},
            compiler_params=params(16),
            cost_estimate=SMALL,
            name=name,
        )(part, *came, before)

    residual = finish("finish_residual", 1.0, 0, res, [far_state], plan)
    begun = finish("finish_adjoint", -1.0, 0, adj, far_adjoint[:1], residual[0, 0, 0, :8])
    return residual, finish("finish_last", -1.0, cut, adj, far_adjoint[1:], begun)


def solution(mesh):
    spec = P("tm", None, None, "sec", None)
    return jax.shard_map(
        local,
        mesh=mesh,
        in_specs=(spec, spec, P("tm", None), P("tm", None)),
        out_specs=(spec, spec),
        check_vma=False,
    )
```

```python
import functools

import jax
import jax.numpy as jnp
from jax import lax
from jax.experimental import pallas as pl
from jax.experimental.pallas import tpu as pltpu
from jax.sharding import PartitionSpec as P

STENCIL = (0.8, -0.2, 4.0 / 105.0, -1.0 / 280.0)
TIME_SCALE = 4.0
FLOW_VELOCITY = 1.0
AXIAL_DISPERSION = 0.3
RADIAL_SPREADING = 0.2
BINDING_STRENGTH = (1.5, 0.6)
HEAT_EXPONENT = (0.5, 0.3)
KINETIC = (1.2, 0.7)
CAPACITY = (2.0, 1.0)
SORPTION_HEAT = (0.4, 0.25)
PURGE_GAIN = 1.5

REACH = len(STENCIL)
WEIGHTS = tuple(TIME_SCALE * c for c in STENCIL)
MOVING = (0, 1, 2, 5)
CENTRE = FLOW_VELOCITY + 2.0 * AXIAL_DISPERSION + 2.0 * RADIAL_SPREADING
UPWIND = FLOW_VELOCITY + AXIAL_DISPERSION
SPARED = ((2, 0), (1, 0))
VIA = (9, 13)
SHARE = 3


def is_odd():
    return lax.rem(lax.axis_index("tm"), 2) == 1


def shifted(x, step, edge):
    cells = x.shape[0]
    row = lax.broadcasted_iota(jnp.int32, x.shape, 0)
    if step > 0:
        return jnp.where(row == 0, edge, pltpu.roll(x, 1, 0))
    return jnp.where(row == cells - 1, edge, pltpu.roll(x, cells - 1, 0))


def radial_pair(x):
    width = x.shape[1]
    lane = lax.broadcasted_iota(jnp.int32, x.shape, 1)
    lower = jnp.where(lane == 0, 0.0, pltpu.roll(x, 1, 1))
    upper = jnp.where(lane == width - 1, 0.0, pltpu.roll(x, width - 1, 1))
    return lower + upper


def transport(x, near, far):
    return CENTRE * x - UPWIND * near - AXIAL_DISPERSION * far - RADIAL_SPREADING * radial_pair(x)


def pick_kernel(state, adjoint, edge):
    instances, _, beds, cells, _ = state.shape
    first = lax.axis_index("sec") == 0

    def step(t, carry):
        for n, x in enumerate((state, adjoint)):
            for k, c in enumerate(MOVING):
                for b in range(beds):
                    row = jnp.where(first, x[t, c, b, cells - 1 :], x[t, c, b, :1])
                    edge[t, n * len(MOVING) + k, b : b + 1] = row
        return carry

    lax.fori_loop(0, instances, step, 0)


def from_before(line, t):
    total = 0.0
    for j in range(t, len(line)):
        total = total + WEIGHTS[t + len(line) - j - 1] * line[j]
    return total


def main_kernel(plan, valve, state, adjoint, edge, in_state, in_adjoint, res, adj):
    instances, comps, beds, cells, _ = res.shape
    odd = is_odd()
    first = lax.axis_index("sec") == 0
    last = lax.axis_index("sec") == lax.axis_size("sec") - 1

    def cell_block(i, carry):
        t = i // beds
        b = lax.rem(i, beds)
        x = [state[t, c, b] for c in range(comps)]
        m = [adjoint[t, c, b] for c in range(comps)]
        y1, y2, _, q1, q2, temp = x
        b1 = BINDING_STRENGTH[0] * jnp.exp(HEAT_EXPONENT[0] * temp)
        b2 = BINDING_STRENGTH[1] * jnp.exp(HEAT_EXPONENT[1] * temp)
        over = 1.0 / (1.0 + b1 * y1 + b2 * y2)
        slope1 = b1 * over
        slope2 = b2 * over
        cover1 = slope1 * y1
        cover2 = slope2 * y2
        rate1 = KINETIC[0] * (CAPACITY[0] * cover1 - q1)
        rate2 = KINETIC[1] * (CAPACITY[1] * cover2 - q2)
        m1 = m[0] - m[3] - SORPTION_HEAT[0] * m[5]
        m2 = m[1] - m[4] - SORPTION_HEAT[1] * m[5]
        g1 = (KINETIC[0] * CAPACITY[0]) * m1
        g2 = (KINETIC[1] * CAPACITY[1]) * m2
        h = g1 * cover1 + g2 * cover2
        e1 = g1 - h
        e2 = g2 - h
        source = {0: rate1, 1: rate2, 5: -SORPTION_HEAT[0] * rate1 - SORPTION_HEAT[1] * rate2}
        pulled = {
            0: slope1 * e1,
            1: slope2 * e2,
            5: HEAT_EXPONENT[0] * cover1 * e1 + HEAT_EXPONENT[1] * cover2 * e2,
        }
        for k, c in enumerate(MOVING):
            from_x = edge[t, k, b][None]
            from_m = edge[t, len(MOVING) + k, b][None]
            below_x = jnp.where(first, 0.0, from_x)
            above_x = jnp.where(last, 0.0, from_x)
            below_m = jnp.where(first, 0.0, from_m)
            above_m = jnp.where(last, 0.0, from_m)
            r = transport(x[c], shifted(x[c], 1, below_x), shifted(x[c], -1, above_x))
            a = transport(m[c], shifted(m[c], -1, above_m), shifted(m[c], 1, below_m))
            res[t, c, b] = r + source[c] if c in source else r
            adj[t, c, b] = a + pulled[c] if c in pulled else a
        res[t, 3, b] = -rate1
        res[t, 4, b] = -rate2
        adj[t, 3, b] = -KINETIC[0] * m1
        adj[t, 4, b] = -KINETIC[1] * m2
        return carry

    lax.fori_loop(0, instances * beds, cell_block, 0)

    @pl.when(last)
    def _():
        def purge(i, carry):
            t = i // beds
            b = lax.rem(i, beds)
            s = lax.rem(b + plan[t, b], beds)
            gain = PURGE_GAIN * valve[t, b].astype(jnp.float32)
            end = pl.ds(cells - 1, 1)
            for c in range(3):
                res[t, c, b, end] += gain * (state[t, c, b, end] - state[t, c, s, end])
                flow = gain * adjoint[t, c, b, end]
                adj[t, c, b, end] += flow
                adj[t, c, s, end] -= flow
            return carry

        lax.fori_loop(0, instances * beds, purge, 0)

    sign = jnp.where(odd, -1.0, 1.0)
    at = [jnp.where(odd, instances - 1 - t, t) for t in range(instances)]

    def time_block(i, carry):
        c = i // beds
        b = lax.rem(i, beds)
        for own, near, out, factor in ((state, in_state, res, sign), (adjoint, in_adjoint, adj, -sign)):
            line = [own[at[t], c, b] for t in range(instances)]
            line += [near[at[t], c, b] for t in range(instances)]
            for t in range(instances):
                total = 0.0
                for k in range(1, REACH + 1):
                    diff = line[t + k]
                    if t - k >= 0:
                        diff = diff - line[t - k]
                    total = total + WEIGHTS[k - 1] * diff
                out[at[t], c, b] += factor * total
        return carry

    lax.fori_loop(0, comps * beds, time_block, 0)


def finish_kernel(scale, low, starts, part, *rest):
    came, (out, whole, sem) = rest[: len(starts) or 1], rest[-3:]
    instances, size, beds, _, _ = whole.shape

    def moved(c):
        return pltpu.make_async_copy(whole.at[:, pl.ds(c, 1)], out.at[:, pl.ds(low + c, 1)], sem.at[c])

    def arrived(t, c, b):
        if not starts:
            return came[0][t, c, b]
        n = t * beds + b
        return sum(run[n - start] for run, start in zip(came, starts) if start <= n < start + run.shape[0])

    def finish(sign, at):
        def component(c, carry):
            for b in range(beds):
                line = [arrived(at[t], c, b) for t in range(instances)]
                for t in range(instances):
                    whole[at[t], c, b] = part[at[t], low + c, b] - sign * from_before(line, t)
            moved(c).start()
            return carry

        lax.fori_loop(0, size, component, 0)

    odd = is_odd()

    @pl.when(odd)
    def _():
        finish(-scale, list(reversed(range(instances))))

    @pl.when(jnp.logical_not(odd))
    def _():
        finish(scale, list(range(instances)))

    for c in range(size):
        moved(c).wait()


VMEM = pl.BlockSpec(memory_space=pltpu.VMEM)
SMEM = pl.BlockSpec(memory_space=pltpu.SMEM)
ANY = pl.BlockSpec(memory_space=pl.ANY)
SMALL = pl.CostEstimate(flops=1000, bytes_accessed=1000, transcendentals=0)


def params(mib):
    return pltpu.CompilerParams(vmem_limit_bytes=mib * 2**20)


def local(state, adjoint, plan, valve):
    count = lax.axis_size("tm")
    sections = lax.axis_size("sec")
    instances, comps, beds, _, width = state.shape
    block = jax.ShapeDtypeStruct(state.shape, state.dtype)
    cells = jax.ShapeDtypeStruct((instances, 2 * len(MOVING), beds, width), state.dtype)
    across = [(i, (i + 1) % count if i % 2 else (i - 1) % count) for i in range(count)]
    on_chip = [(i, i ^ 1) for i in range(count)]
    far_state = lax.ppermute(state, "tm", across)
    cut = comps - 1
    far_adjoint = lax.ppermute(adjoint[:, :cut], "tm", across)

    last = adjoint[:, cut].reshape((instances * beds,) + state.shape[3:])
    via = [i for i in VIA if i < count]
    kept = instances * beds - SHARE * len(via)
    starts = [0, kept] + [kept + SHARE * n for n in range(len(via))]

    def over_both(x, pairs):
        return lax.ppermute(x, ("tm", "sec"), [(i * sections + j, k * sections + l) for (i, j), (k, l) in pairs])

    everywhere = [((i, j), (k, j)) for i, k in across for j in range(sections)]
    runs = [
        lax.ppermute(last[:kept], "tm", across),
        over_both(last[kept:], [pair for pair in everywhere if pair != SPARED]),
    ]

    def near_transfers():
        in_state = lax.ppermute(state, "tm", on_chip)
        in_adjoint = lax.ppermute(adjoint, "tm", on_chip)
        edge = pl.pallas_call(
            pick_kernel,
            out_shape=cells,
            in_specs=[VMEM, VMEM],
            out_specs=VMEM,
            compiler_params=params(16),
            cost_estimate=SMALL,
            name="pick",
        )(state, adjoint)
        return lax.ppermute(edge, "sec", [(i, i ^ 1) for i in range(sections)]), in_state, in_adjoint

    def nothing():
        return jnp.zeros(cells.shape, cells.dtype), state, adjoint

    near = lax.cond(lax.axis_index("tm") % 2 >= 0, near_transfers, nothing)
    half_way = [
        over_both(last[start : start + SHARE], [(SPARED[0], (i, 0))]) for start, i in zip(starts[2:], via)
    ]
    runs += [over_both(x, [((i, 0), SPARED[1])]) for x, i in zip(half_way, via)]
    res, adj = pl.pallas_call(
        main_kernel,
        out_shape=(block, block),
        in_specs=[SMEM] * 2 + [VMEM] * 5,
        out_specs=(VMEM, VMEM),
        compiler_params=params(24),
        cost_estimate=SMALL,
        name="local_part",
    )(plan, valve, state, adjoint, *near)

    def finish(name, scale, low, size, part, came, before, starts=(), begun=False):
        return pl.pallas_call(
            functools.partial(finish_kernel, scale, low, starts),
            out_shape=block,
            in_specs=[VMEM] * (1 + len(came)) + [ANY] * len(before),
            out_specs=ANY,
            scratch_shapes=[
                pltpu.VMEM((instances, size) + state.shape[2:], state.dtype),
                pltpu.SemaphoreType.DMA((size,)),
            ],
            input_output_aliases={1 + len(came): 0} if begun else {},
            compiler_params=params(16),
            cost_estimate=SMALL,
            name=name,
        )(part, *came, *before)

    residual = finish("finish_residual", 1.0, 0, comps, res, [far_state], runs[2:])
    begun = finish("finish_adjoint", -1.0, 0, cut, adj, [far_adjoint], [residual[0, 0, 0, :8]])
    return residual, finish("finish_last", -1.0, cut, 1, adj, runs, [begun], starts, True)


def solution(mesh):
    spec = P("tm", None, None, "sec", None)
    return jax.shard_map(
        local,
        mesh=mesh,
        in_specs=(spec, spec, P("tm", None), P("tm", None)),
        out_specs=(spec, spec),
        check_vma=False,
    )
```

```python
import functools

import jax
import jax.numpy as jnp
from jax import lax
from jax.experimental import pallas as pl
from jax.experimental.pallas import tpu as pltpu
from jax.sharding import PartitionSpec as P

STENCIL = (0.8, -0.2, 4.0 / 105.0, -1.0 / 280.0)
TIME_SCALE = 4.0
FLOW_VELOCITY = 1.0
AXIAL_DISPERSION = 0.3
RADIAL_SPREADING = 0.2
BINDING_STRENGTH = (1.5, 0.6)
HEAT_EXPONENT = (0.5, 0.3)
KINETIC = (1.2, 0.7)
CAPACITY = (2.0, 1.0)
SORPTION_HEAT = (0.4, 0.25)
PURGE_GAIN = 1.5

REACH = len(STENCIL)
WEIGHTS = tuple(TIME_SCALE * c for c in STENCIL)
MOVING = (0, 1, 2, 5)
CENTRE = FLOW_VELOCITY + 2.0 * AXIAL_DISPERSION + 2.0 * RADIAL_SPREADING
UPWIND = FLOW_VELOCITY + AXIAL_DISPERSION
LAST = 2
SPARED = ((2, 0), (1, 0))
VIA = (5, 9, 13)
SHARE = 2


def is_odd():
    return lax.rem(lax.axis_index("tm"), 2) == 1


def shifted(x, step, edge):
    cells = x.shape[0]
    row = lax.broadcasted_iota(jnp.int32, x.shape, 0)
    if step > 0:
        return jnp.where(row == 0, edge, pltpu.roll(x, 1, 0))
    return jnp.where(row == cells - 1, edge, pltpu.roll(x, cells - 1, 0))


def radial_pair(x):
    width = x.shape[1]
    lane = lax.broadcasted_iota(jnp.int32, x.shape, 1)
    lower = jnp.where(lane == 0, 0.0, pltpu.roll(x, 1, 1))
    upper = jnp.where(lane == width - 1, 0.0, pltpu.roll(x, width - 1, 1))
    return lower + upper


def transport(x, near, far):
    return CENTRE * x - UPWIND * near - AXIAL_DISPERSION * far - RADIAL_SPREADING * radial_pair(x)


def pick_kernel(state, adjoint, edge):
    instances, _, beds, cells, _ = state.shape
    first = lax.axis_index("sec") == 0

    def step(t, carry):
        for n, x in enumerate((state, adjoint)):
            for k, c in enumerate(MOVING):
                for b in range(beds):
                    row = jnp.where(first, x[t, c, b, cells - 1 :], x[t, c, b, :1])
                    edge[t, n * len(MOVING) + k, b : b + 1] = row
        return carry

    lax.fori_loop(0, instances, step, 0)


def from_before(line, t):
    total = 0.0
    for j in range(t, len(line)):
        total = total + WEIGHTS[t + len(line) - j - 1] * line[j]
    return total


def main_kernel(plan, valve, state, adjoint, edge, in_state, in_adjoint, res, adj):
    instances, comps, beds, cells, _ = res.shape
    odd = is_odd()
    first = lax.axis_index("sec") == 0
    last = lax.axis_index("sec") == lax.axis_size("sec") - 1

    def cell_block(i, carry):
        t = i // beds
        b = lax.rem(i, beds)
        x = [state[t, c, b] for c in range(comps)]
        m = [adjoint[t, c, b] for c in range(comps)]
        y1, y2, _, q1, q2, temp = x
        b1 = BINDING_STRENGTH[0] * jnp.exp(HEAT_EXPONENT[0] * temp)
        b2 = BINDING_STRENGTH[1] * jnp.exp(HEAT_EXPONENT[1] * temp)
        over = 1.0 / (1.0 + b1 * y1 + b2 * y2)
        slope1 = b1 * over
        slope2 = b2 * over
        cover1 = slope1 * y1
        cover2 = slope2 * y2
        rate1 = KINETIC[0] * (CAPACITY[0] * cover1 - q1)
        rate2 = KINETIC[1] * (CAPACITY[1] * cover2 - q2)
        m1 = m[0] - m[3] - SORPTION_HEAT[0] * m[5]
        m2 = m[1] - m[4] - SORPTION_HEAT[1] * m[5]
        g1 = (KINETIC[0] * CAPACITY[0]) * m1
        g2 = (KINETIC[1] * CAPACITY[1]) * m2
        h = g1 * cover1 + g2 * cover2
        e1 = g1 - h
        e2 = g2 - h
        source = {0: rate1, 1: rate2, 5: -SORPTION_HEAT[0] * rate1 - SORPTION_HEAT[1] * rate2}
        pulled = {
            0: slope1 * e1,
            1: slope2 * e2,
            5: HEAT_EXPONENT[0] * cover1 * e1 + HEAT_EXPONENT[1] * cover2 * e2,
        }
        for k, c in enumerate(MOVING):
            from_x = edge[t, k, b][None]
            from_m = edge[t, len(MOVING) + k, b][None]
            below_x = jnp.where(first, 0.0, from_x)
            above_x = jnp.where(last, 0.0, from_x)
            below_m = jnp.where(first, 0.0, from_m)
            above_m = jnp.where(last, 0.0, from_m)
            r = transport(x[c], shifted(x[c], 1, below_x), shifted(x[c], -1, above_x))
            a = transport(m[c], shifted(m[c], -1, above_m), shifted(m[c], 1, below_m))
            res[t, c, b] = r + source[c] if c in source else r
            adj[t, c, b] = a + pulled[c] if c in pulled else a
        res[t, 3, b] = -rate1
        res[t, 4, b] = -rate2
        adj[t, 3, b] = -KINETIC[0] * m1
        adj[t, 4, b] = -KINETIC[1] * m2
        return carry

    lax.fori_loop(0, instances * beds, cell_block, 0)

    @pl.when(last)
    def _():
        def purge(i, carry):
            t = i // beds
            b = lax.rem(i, beds)
            s = lax.rem(b + plan[t, b], beds)
            gain = PURGE_GAIN * valve[t, b].astype(jnp.float32)
            end = pl.ds(cells - 1, 1)
            for c in range(3):
                res[t, c, b, end] += gain * (state[t, c, b, end] - state[t, c, s, end])
                flow = gain * adjoint[t, c, b, end]
                adj[t, c, b, end] += flow
                adj[t, c, s, end] -= flow
            return carry

        lax.fori_loop(0, instances * beds, purge, 0)

    sign = jnp.where(odd, -1.0, 1.0)
    at = [jnp.where(odd, instances - 1 - t, t) for t in range(instances)]

    def time_block(i, carry):
        c = i // beds
        b = lax.rem(i, beds)
        for own, near, out, factor in ((state, in_state, res, sign), (adjoint, in_adjoint, adj, -sign)):
            line = [own[at[t], c, b] for t in range(instances)]
            line += [near[at[t], c, b] for t in range(instances)]
            for t in range(instances):
                total = 0.0
                for k in range(1, REACH + 1):
                    diff = line[t + k]
                    if t - k >= 0:
                        diff = diff - line[t - k]
                    total = total + WEIGHTS[k - 1] * diff
                out[at[t], c, b] += factor * total
        return carry

    lax.fori_loop(0, comps * beds, time_block, 0)


def finish_kernel(scale, low, starts, part, *rest):
    came, (out, whole, sem) = rest[: len(starts) or 1], rest[-3:]
    instances, size, beds, _, _ = whole.shape

    def moved(c):
        return pltpu.make_async_copy(whole.at[:, pl.ds(c, 1)], out.at[:, pl.ds(low + c, 1)], sem.at[c])

    def arrived(t, c, b):
        if not starts:
            return came[0][t, c, b]
        n = (t * size + c) * beds + b
        return sum(run[n - start] for run, start in zip(came, starts) if start <= n < start + run.shape[0])

    def finish(sign, at):
        def component(c, carry):
            for b in range(beds):
                line = [arrived(at[t], c, b) for t in range(instances)]
                for t in range(instances):
                    whole[at[t], c, b] = part[at[t], low + c, b] - sign * from_before(line, t)
            moved(c).start()
            return carry

        if starts:
            for c in range(size):
                component(c, 0)
        else:
            lax.fori_loop(0, size, component, 0)

    odd = is_odd()

    @pl.when(odd)
    def _():
        finish(-scale, list(reversed(range(instances))))

    @pl.when(jnp.logical_not(odd))
    def _():
        finish(scale, list(range(instances)))

    for c in range(size):
        moved(c).wait()


VMEM = pl.BlockSpec(memory_space=pltpu.VMEM)
SMEM = pl.BlockSpec(memory_space=pltpu.SMEM)
ANY = pl.BlockSpec(memory_space=pl.ANY)
SMALL = pl.CostEstimate(flops=1000, bytes_accessed=1000, transcendentals=0)


def params(mib):
    return pltpu.CompilerParams(vmem_limit_bytes=mib * 2**20)


def local(state, adjoint, plan, valve):
    count = lax.axis_size("tm")
    sections = lax.axis_size("sec")
    instances, comps, beds, _, width = state.shape
    block = jax.ShapeDtypeStruct(state.shape, state.dtype)
    cells = jax.ShapeDtypeStruct((instances, 2 * len(MOVING), beds, width), state.dtype)
    across = [(i, (i + 1) % count if i % 2 else (i - 1) % count) for i in range(count)]
    on_chip = [(i, i ^ 1) for i in range(count)]
    far_state = lax.ppermute(state, "tm", across)
    cut = comps - LAST
    far_adjoint = lax.ppermute(adjoint[:, :cut], "tm", across)

    last = adjoint[:, cut:].reshape((instances * LAST * beds,) + state.shape[3:])
    via = [i for i in VIA if i < count]
    kept = instances * LAST * beds - SHARE * len(via)
    starts = [0, kept] + [kept + SHARE * n for n in range(len(via))]

    def over_both(x, pairs):
        return lax.ppermute(x, ("tm", "sec"), [(i * sections + j, k * sections + l) for (i, j), (k, l) in pairs])

    everywhere = [((i, j), (k, j)) for i, k in across for j in range(sections)]
    runs = [
        lax.ppermute(last[:kept], "tm", across),
        over_both(last[kept:], [pair for pair in everywhere if pair != SPARED]),
    ]

    def near_transfers():
        in_state = lax.ppermute(state, "tm", on_chip)
        in_adjoint = lax.ppermute(adjoint, "tm", on_chip)
        edge = pl.pallas_call(
            pick_kernel,
            out_shape=cells,
            in_specs=[VMEM, VMEM],
            out_specs=VMEM,
            compiler_params=params(16),
            cost_estimate=SMALL,
            name="pick",
        )(state, adjoint)
        return lax.ppermute(edge, "sec", [(i, i ^ 1) for i in range(sections)]), in_state, in_adjoint

    def nothing():
        return jnp.zeros(cells.shape, cells.dtype), state, adjoint

    near = lax.cond(lax.axis_index("tm") % 2 >= 0, near_transfers, nothing)
    half_way = [
        over_both(last[start : start + SHARE], [(SPARED[0], (i, 0))]) for start, i in zip(starts[2:], via)
    ]
    runs += [over_both(x, [((i, 0), SPARED[1])]) for x, i in zip(half_way, via)]
    res, adj = pl.pallas_call(
        main_kernel,
        out_shape=(block, block),
        in_specs=[SMEM] * 2 + [VMEM] * 5,
        out_specs=(VMEM, VMEM),
        compiler_params=params(24),
        cost_estimate=SMALL,
        name="local_part",
    )(plan, valve, state, adjoint, *near)

    def finish(name, scale, low, size, part, came, before, starts=(), begun=False):
        return pl.pallas_call(
            functools.partial(finish_kernel, scale, low, starts),
            out_shape=block,
            in_specs=[VMEM] * (1 + len(came)) + [ANY] * len(before),
            out_specs=ANY,
            scratch_shapes=[
                pltpu.VMEM((instances, size) + state.shape[2:], state.dtype),
                pltpu.SemaphoreType.DMA((size,)),
            ],
            input_output_aliases={1 + len(came): 0} if begun else {},
            compiler_params=params(16),
            cost_estimate=SMALL,
            name=name,
        )(part, *came, *before)

    residual = finish("finish_residual", 1.0, 0, comps, res, [far_state], runs[2:])
    begun = finish("finish_adjoint", -1.0, 0, cut, adj, [far_adjoint], [residual[0, 0, 0, :8]])
    return residual, finish("finish_last", -1.0, cut, LAST, adj, runs, [begun], starts, True)


def solution(mesh):
    spec = P("tm", None, None, "sec", None)
    return jax.shard_map(
        local,
        mesh=mesh,
        in_specs=(spec, spec, P("tm", None), P("tm", None)),
        out_specs=(spec, spec),
        check_vma=False,
    )
```

```python
import functools

import jax
import jax.numpy as jnp
from jax import lax
from jax.experimental import pallas as pl
from jax.experimental.pallas import tpu as pltpu
from jax.sharding import PartitionSpec as P

STENCIL = (0.8, -0.2, 4.0 / 105.0, -1.0 / 280.0)
TIME_SCALE = 4.0
FLOW_VELOCITY = 1.0
AXIAL_DISPERSION = 0.3
RADIAL_SPREADING = 0.2
BINDING_STRENGTH = (1.5, 0.6)
HEAT_EXPONENT = (0.5, 0.3)
KINETIC = (1.2, 0.7)
CAPACITY = (2.0, 1.0)
SORPTION_HEAT = (0.4, 0.25)
PURGE_GAIN = 1.5

REACH = len(STENCIL)
WEIGHTS = tuple(TIME_SCALE * c for c in STENCIL)
MOVING = (0, 1, 2, 5)
CENTRE = FLOW_VELOCITY + 2.0 * AXIAL_DISPERSION + 2.0 * RADIAL_SPREADING
UPWIND = FLOW_VELOCITY + AXIAL_DISPERSION
LAST = 2
SPARED = ((2, 0), (1, 0))
VIA = (5, 9, 13)
SHARE = 3


def is_odd():
    return lax.rem(lax.axis_index("tm"), 2) == 1


def shifted(x, step, edge):
    cells = x.shape[0]
    row = lax.broadcasted_iota(jnp.int32, x.shape, 0)
    if step > 0:
        return jnp.where(row == 0, edge, pltpu.roll(x, 1, 0))
    return jnp.where(row == cells - 1, edge, pltpu.roll(x, cells - 1, 0))


def radial_pair(x):
    width = x.shape[1]
    lane = lax.broadcasted_iota(jnp.int32, x.shape, 1)
    lower = jnp.where(lane == 0, 0.0, pltpu.roll(x, 1, 1))
    upper = jnp.where(lane == width - 1, 0.0, pltpu.roll(x, width - 1, 1))
    return lower + upper


def transport(x, near, far):
    return CENTRE * x - UPWIND * near - AXIAL_DISPERSION * far - RADIAL_SPREADING * radial_pair(x)


def pick_kernel(state, adjoint, edge):
    instances, _, beds, cells, _ = state.shape
    first = lax.axis_index("sec") == 0

    def step(t, carry):
        for n, x in enumerate((state, adjoint)):
            for k, c in enumerate(MOVING):
                for b in range(beds):
                    row = jnp.where(first, x[t, c, b, cells - 1 :], x[t, c, b, :1])
                    edge[t, n * len(MOVING) + k, b : b + 1] = row
        return carry

    lax.fori_loop(0, instances, step, 0)


def from_before(line, t):
    total = 0.0
    for j in range(t, len(line)):
        total = total + WEIGHTS[t + len(line) - j - 1] * line[j]
    return total


def main_kernel(plan, valve, state, adjoint, edge, in_state, in_adjoint, res, adj):
    instances, comps, beds, cells, _ = res.shape
    odd = is_odd()
    first = lax.axis_index("sec") == 0
    last = lax.axis_index("sec") == lax.axis_size("sec") - 1

    def cell_block(i, carry):
        t = i // beds
        b = lax.rem(i, beds)
        x = [state[t, c, b] for c in range(comps)]
        m = [adjoint[t, c, b] for c in range(comps)]
        y1, y2, _, q1, q2, temp = x
        b1 = BINDING_STRENGTH[0] * jnp.exp(HEAT_EXPONENT[0] * temp)
        b2 = BINDING_STRENGTH[1] * jnp.exp(HEAT_EXPONENT[1] * temp)
        over = 1.0 / (1.0 + b1 * y1 + b2 * y2)
        slope1 = b1 * over
        slope2 = b2 * over
        cover1 = slope1 * y1
        cover2 = slope2 * y2
        rate1 = KINETIC[0] * (CAPACITY[0] * cover1 - q1)
        rate2 = KINETIC[1] * (CAPACITY[1] * cover2 - q2)
        m1 = m[0] - m[3] - SORPTION_HEAT[0] * m[5]
        m2 = m[1] - m[4] - SORPTION_HEAT[1] * m[5]
        g1 = (KINETIC[0] * CAPACITY[0]) * m1
        g2 = (KINETIC[1] * CAPACITY[1]) * m2
        h = g1 * cover1 + g2 * cover2
        e1 = g1 - h
        e2 = g2 - h
        source = {0: rate1, 1: rate2, 5: -SORPTION_HEAT[0] * rate1 - SORPTION_HEAT[1] * rate2}
        pulled = {
            0: slope1 * e1,
            1: slope2 * e2,
            5: HEAT_EXPONENT[0] * cover1 * e1 + HEAT_EXPONENT[1] * cover2 * e2,
        }
        for k, c in enumerate(MOVING):
            from_x = edge[t, k, b][None]
            from_m = edge[t, len(MOVING) + k, b][None]
            below_x = jnp.where(first, 0.0, from_x)
            above_x = jnp.where(last, 0.0, from_x)
            below_m = jnp.where(first, 0.0, from_m)
            above_m = jnp.where(last, 0.0, from_m)
            r = transport(x[c], shifted(x[c], 1, below_x), shifted(x[c], -1, above_x))
            a = transport(m[c], shifted(m[c], -1, above_m), shifted(m[c], 1, below_m))
            res[t, c, b] = r + source[c] if c in source else r
            adj[t, c, b] = a + pulled[c] if c in pulled else a
        res[t, 3, b] = -rate1
        res[t, 4, b] = -rate2
        adj[t, 3, b] = -KINETIC[0] * m1
        adj[t, 4, b] = -KINETIC[1] * m2
        return carry

    lax.fori_loop(0, instances * beds, cell_block, 0)

    @pl.when(last)
    def _():
        def purge(i, carry):
            t = i // beds
            b = lax.rem(i, beds)
            s = lax.rem(b + plan[t, b], beds)
            gain = PURGE_GAIN * valve[t, b].astype(jnp.float32)
            end = pl.ds(cells - 1, 1)
            for c in range(3):
                res[t, c, b, end] += gain * (state[t, c, b, end] - state[t, c, s, end])
                flow = gain * adjoint[t, c, b, end]
                adj[t, c, b, end] += flow
                adj[t, c, s, end] -= flow
            return carry

        lax.fori_loop(0, instances * beds, purge, 0)

    sign = jnp.where(odd, -1.0, 1.0)
    at = [jnp.where(odd, instances - 1 - t, t) for t in range(instances)]

    def time_block(i, carry):
        c = i // beds
        b = lax.rem(i, beds)
        for own, near, out, factor in ((state, in_state, res, sign), (adjoint, in_adjoint, adj, -sign)):
            line = [own[at[t], c, b] for t in range(instances)]
            line += [near[at[t], c, b] for t in range(instances)]
            for t in range(instances):
                total = 0.0
                for k in range(1, REACH + 1):
                    diff = line[t + k]
                    if t - k >= 0:
                        diff = diff - line[t - k]
                    total = total + WEIGHTS[k - 1] * diff
                out[at[t], c, b] += factor * total
        return carry

    lax.fori_loop(0, comps * beds, time_block, 0)


def finish_kernel(scale, low, starts, part, *rest):
    came, (out, whole, sem) = rest[: len(starts) or 1], rest[-3:]
    instances, size, beds, _, _ = whole.shape

    def moved(c):
        return pltpu.make_async_copy(whole.at[:, pl.ds(c, 1)], out.at[:, pl.ds(low + c, 1)], sem.at[c])

    def arrived(t, c, b):
        if not starts:
            return came[0][t, c, b]
        n = (t * size + c) * beds + b
        return sum(run[n - start] for run, start in zip(came, starts) if start <= n < start + run.shape[0])

    def finish(sign, at):
        def component(c, carry):
            for b in range(beds):
                line = [arrived(at[t], c, b) for t in range(instances)]
                for t in range(instances):
                    whole[at[t], c, b] = part[at[t], low + c, b] - sign * from_before(line, t)
            moved(c).start()
            return carry

        if starts:
            for c in range(size):
                component(c, 0)
        else:
            lax.fori_loop(0, size, component, 0)

    odd = is_odd()

    @pl.when(odd)
    def _():
        finish(-scale, list(reversed(range(instances))))

    @pl.when(jnp.logical_not(odd))
    def _():
        finish(scale, list(range(instances)))

    for c in range(size):
        moved(c).wait()


VMEM = pl.BlockSpec(memory_space=pltpu.VMEM)
SMEM = pl.BlockSpec(memory_space=pltpu.SMEM)
ANY = pl.BlockSpec(memory_space=pl.ANY)
SMALL = pl.CostEstimate(flops=1000, bytes_accessed=1000, transcendentals=0)


def params(mib):
    return pltpu.CompilerParams(vmem_limit_bytes=mib * 2**20)


def local(state, adjoint, plan, valve):
    count = lax.axis_size("tm")
    sections = lax.axis_size("sec")
    instances, comps, beds, _, width = state.shape
    block = jax.ShapeDtypeStruct(state.shape, state.dtype)
    cells = jax.ShapeDtypeStruct((instances, 2 * len(MOVING), beds, width), state.dtype)
    across = [(i, (i + 1) % count if i % 2 else (i - 1) % count) for i in range(count)]
    on_chip = [(i, i ^ 1) for i in range(count)]
    far_state = lax.ppermute(state, "tm", across)
    cut = comps - LAST
    far_adjoint = lax.ppermute(adjoint[:, :cut], "tm", across)

    last = adjoint[:, cut:].reshape((instances * LAST * beds,) + state.shape[3:])
    via = [i for i in VIA if i < count]
    kept = instances * LAST * beds - SHARE * len(via)
    starts = [0, kept] + [kept + SHARE * n for n in range(len(via))]

    def over_both(x, pairs):
        return lax.ppermute(x, ("tm", "sec"), [(i * sections + j, k * sections + l) for (i, j), (k, l) in pairs])

    everywhere = [((i, j), (k, j)) for i, k in across for j in range(sections)]
    runs = [
        lax.ppermute(last[:kept], "tm", across),
        over_both(last[kept:], [pair for pair in everywhere if pair != SPARED]),
    ]

    def near_transfers():
        in_state = lax.ppermute(state, "tm", on_chip)
        in_adjoint = lax.ppermute(adjoint, "tm", on_chip)
        edge = pl.pallas_call(
            pick_kernel,
            out_shape=cells,
            in_specs=[VMEM, VMEM],
            out_specs=VMEM,
            compiler_params=params(16),
            cost_estimate=SMALL,
            name="pick",
        )(state, adjoint)
        return lax.ppermute(edge, "sec", [(i, i ^ 1) for i in range(sections)]), in_state, in_adjoint

    def nothing():
        return jnp.zeros(cells.shape, cells.dtype), state, adjoint

    near = lax.cond(lax.axis_index("tm") % 2 >= 0, near_transfers, nothing)
    half_way = [
        over_both(last[start : start + SHARE], [(SPARED[0], (i, 0))]) for start, i in zip(starts[2:], via)
    ]
    runs += [over_both(x, [((i, 0), SPARED[1])]) for x, i in zip(half_way, via)]
    res, adj = pl.pallas_call(
        main_kernel,
        out_shape=(block, block),
        in_specs=[SMEM] * 2 + [VMEM] * 5,
        out_specs=(VMEM, VMEM),
        compiler_params=params(24),
        cost_estimate=SMALL,
        name="local_part",
    )(plan, valve, state, adjoint, *near)

    def finish(name, scale, low, size, part, came, before, starts=(), begun=False):
        return pl.pallas_call(
            functools.partial(finish_kernel, scale, low, starts),
            out_shape=block,
            in_specs=[VMEM] * (1 + len(came)) + [ANY] * len(before),
            out_specs=ANY,
            scratch_shapes=[
                pltpu.VMEM((instances, size) + state.shape[2:], state.dtype),
                pltpu.SemaphoreType.DMA((size,)),
            ],
            input_output_aliases={1 + len(came): 0} if begun else {},
            compiler_params=params(16),
            cost_estimate=SMALL,
            name=name,
        )(part, *came, *before)

    residual = finish("finish_residual", 1.0, 0, comps, res, [far_state], runs[2:])
    begun = finish("finish_adjoint", -1.0, 0, cut, adj, [far_adjoint], [residual[0, 0, 0, :8]])
    return residual, finish("finish_last", -1.0, cut, LAST, adj, runs, [begun], starts, True)


def solution(mesh):
    spec = P("tm", None, None, "sec", None)
    return jax.shard_map(
        local,
        mesh=mesh,
        in_specs=(spec, spec, P("tm", None), P("tm", None)),
        out_specs=(spec, spec),
        check_vma=False,
    )
```

```python
import functools

import jax
import jax.numpy as jnp
from jax import lax
from jax.experimental import pallas as pl
from jax.experimental.pallas import tpu as pltpu
from jax.sharding import PartitionSpec as P

STENCIL = (0.8, -0.2, 4.0 / 105.0, -1.0 / 280.0)
TIME_SCALE = 4.0
FLOW_VELOCITY = 1.0
AXIAL_DISPERSION = 0.3
RADIAL_SPREADING = 0.2
BINDING_STRENGTH = (1.5, 0.6)
HEAT_EXPONENT = (0.5, 0.3)
KINETIC = (1.2, 0.7)
CAPACITY = (2.0, 1.0)
SORPTION_HEAT = (0.4, 0.25)
PURGE_GAIN = 1.5

REACH = len(STENCIL)
WEIGHTS = tuple(TIME_SCALE * c for c in STENCIL)
MOVING = (0, 1, 2, 5)
CENTRE = FLOW_VELOCITY + 2.0 * AXIAL_DISPERSION + 2.0 * RADIAL_SPREADING
UPWIND = FLOW_VELOCITY + AXIAL_DISPERSION
SPARED = ((2, 0), (1, 0))
VIA = (9, 13)
SHARE = 3


def is_odd():
    return lax.rem(lax.axis_index("tm"), 2) == 1


def shifted(x, step, edge):
    cells = x.shape[0]
    row = lax.broadcasted_iota(jnp.int32, x.shape, 0)
    if step > 0:
        return jnp.where(row == 0, edge, pltpu.roll(x, 1, 0))
    return jnp.where(row == cells - 1, edge, pltpu.roll(x, cells - 1, 0))


def radial_pair(x):
    width = x.shape[1]
    lane = lax.broadcasted_iota(jnp.int32, x.shape, 1)
    lower = jnp.where(lane == 0, 0.0, pltpu.roll(x, 1, 1))
    upper = jnp.where(lane == width - 1, 0.0, pltpu.roll(x, width - 1, 1))
    return lower + upper


def transport(x, near, far):
    return CENTRE * x - UPWIND * near - AXIAL_DISPERSION * far - RADIAL_SPREADING * radial_pair(x)


def pick_kernel(state, adjoint, edge):
    instances, _, beds, cells, _ = state.shape
    first = lax.axis_index("sec") == 0

    def step(t, carry):
        for n, x in enumerate((state, adjoint)):
            for k, c in enumerate(MOVING):
                for b in range(beds):
                    row = jnp.where(first, x[t, c, b, cells - 1 :], x[t, c, b, :1])
                    edge[t, n * len(MOVING) + k, b : b + 1] = row
        return carry

    lax.fori_loop(0, instances, step, 0)


def from_before(line, t):
    total = 0.0
    count = len(line)
    for j in range(t, count):
        total = total + WEIGHTS[t + count - j - 1] * line[j]
    return total


def main_kernel(plan, valve, state, adjoint, edge, in_state, in_adjoint, res, adj):
    instances, comps, beds, cells, _ = res.shape
    odd = is_odd()
    first = lax.axis_index("sec") == 0
    last = lax.axis_index("sec") == lax.axis_size("sec") - 1

    def cell_block(i, carry):
        t = i // beds
        b = lax.rem(i, beds)
        x = [state[t, c, b] for c in range(comps)]
        m = [adjoint[t, c, b] for c in range(comps)]
        y1, y2, _, q1, q2, temp = x
        b1 = BINDING_STRENGTH[0] * jnp.exp(HEAT_EXPONENT[0] * temp)
        b2 = BINDING_STRENGTH[1] * jnp.exp(HEAT_EXPONENT[1] * temp)
        over = 1.0 / (1.0 + b1 * y1 + b2 * y2)
        slope1 = b1 * over
        slope2 = b2 * over
        cover1 = slope1 * y1
        cover2 = slope2 * y2
        rate1 = KINETIC[0] * (CAPACITY[0] * cover1 - q1)
        rate2 = KINETIC[1] * (CAPACITY[1] * cover2 - q2)
        m1 = m[0] - m[3] - SORPTION_HEAT[0] * m[5]
        m2 = m[1] - m[4] - SORPTION_HEAT[1] * m[5]
        g1 = (KINETIC[0] * CAPACITY[0]) * m1
        g2 = (KINETIC[1] * CAPACITY[1]) * m2
        h = g1 * cover1 + g2 * cover2
        e1 = g1 - h
        e2 = g2 - h
        source = {0: rate1, 1: rate2, 5: -SORPTION_HEAT[0] * rate1 - SORPTION_HEAT[1] * rate2}
        pulled = {
            0: slope1 * e1,
            1: slope2 * e2,
            5: HEAT_EXPONENT[0] * cover1 * e1 + HEAT_EXPONENT[1] * cover2 * e2,
        }
        for k, c in enumerate(MOVING):
            from_x = edge[t, k, b][None]
            from_m = edge[t, len(MOVING) + k, b][None]
            below_x = jnp.where(first, 0.0, from_x)
            above_x = jnp.where(last, 0.0, from_x)
            below_m = jnp.where(first, 0.0, from_m)
            above_m = jnp.where(last, 0.0, from_m)
            r = transport(x[c], shifted(x[c], 1, below_x), shifted(x[c], -1, above_x))
            a = transport(m[c], shifted(m[c], -1, above_m), shifted(m[c], 1, below_m))
            res[t, c, b] = r + source[c] if c in source else r
            adj[t, c, b] = a + pulled[c] if c in pulled else a
        res[t, 3, b] = -rate1
        res[t, 4, b] = -rate2
        adj[t, 3, b] = -KINETIC[0] * m1
        adj[t, 4, b] = -KINETIC[1] * m2
        return carry

    lax.fori_loop(0, instances * beds, cell_block, 0)

    @pl.when(last)
    def _():
        def purge(i, carry):
            t = i // beds
            b = lax.rem(i, beds)
            s = lax.rem(b + plan[t, b], beds)
            gain = PURGE_GAIN * valve[t, b].astype(jnp.float32)
            end = pl.ds(cells - 1, 1)
            for c in range(3):
                res[t, c, b, end] += gain * (state[t, c, b, end] - state[t, c, s, end])
                flow = gain * adjoint[t, c, b, end]
                adj[t, c, b, end] += flow
                adj[t, c, s, end] -= flow
            return carry

        lax.fori_loop(0, instances * beds, purge, 0)

    sign = jnp.where(odd, -1.0, 1.0)
    at = [jnp.where(odd, instances - 1 - t, t) for t in range(instances)]

    def time_block(i, carry):
        c = i // beds
        b = lax.rem(i, beds)
        for own, near, out, factor in ((state, in_state, res, sign), (adjoint, in_adjoint, adj, -sign)):
            line = [own[at[t], c, b] for t in range(instances)]
            line += [near[at[t], c, b] for t in range(instances)]
            for t in range(instances):
                total = 0.0
                for k in range(1, REACH + 1):
                    diff = line[t + k]
                    if t - k >= 0:
                        diff = diff - line[t - k]
                    total = total + WEIGHTS[k - 1] * diff
                out[at[t], c, b] += factor * total
        return carry

    lax.fori_loop(0, comps * beds, time_block, 0)


def finish_kernel(scale, low, part, came, *rest):
    out, token, whole, sem = rest[-4:]
    token[...] = jnp.zeros_like(token)
    instances, size, beds, _, _ = whole.shape

    def moved(c):
        return pltpu.make_async_copy(whole.at[:, pl.ds(c, 1)], out.at[:, pl.ds(low + c, 1)], sem.at[c])

    def finish(sign, at):
        def component(c, carry):
            for b in range(beds):
                line = [came[at[t], c, b] for t in range(instances)]
                for t in range(instances):
                    whole[at[t], c, b] = part[at[t], low + c, b] - sign * from_before(line, t)
            moved(c).start()
            return carry

        lax.fori_loop(0, size, component, 0)

    odd = is_odd()

    @pl.when(odd)
    def _():
        finish(-scale, list(reversed(range(instances))))

    @pl.when(jnp.logical_not(odd))
    def _():
        finish(scale, list(range(instances)))

    for c in range(size):
        moved(c).wait()


def after_kernel(came, before, out):
    del came, before, out


VMEM = pl.BlockSpec(memory_space=pltpu.VMEM)
SMEM = pl.BlockSpec(memory_space=pltpu.SMEM)
ANY = pl.BlockSpec(memory_space=pl.ANY)
SMALL = pl.CostEstimate(flops=1000, bytes_accessed=1000, transcendentals=0)


def params(mib):
    return pltpu.CompilerParams(vmem_limit_bytes=mib * 2**20)


def local(state, adjoint, plan, valve):
    count = lax.axis_size("tm")
    sections = lax.axis_size("sec")
    instances, comps, beds, _, width = state.shape
    block = jax.ShapeDtypeStruct(state.shape, state.dtype)
    cells = jax.ShapeDtypeStruct((instances, 2 * len(MOVING), beds, width), state.dtype)
    across = [(i, (i + 1) % count if i % 2 else (i - 1) % count) for i in range(count)]
    on_chip = [(i, i ^ 1) for i in range(count)]
    far_state = lax.ppermute(state, "tm", across)
    cut = comps - 1
    far_adjoint = lax.ppermute(adjoint[:, :cut], "tm", across)

    last = adjoint[:, cut].reshape((instances * beds,) + state.shape[3:])
    via = [i for i in VIA if i < count]
    kept = instances * beds - SHARE * len(via)
    starts = [0, kept] + [kept + SHARE * n for n in range(len(via))]

    def over_both(x, pairs):
        return lax.ppermute(x, ("tm", "sec"), [(i * sections + j, k * sections + l) for (i, j), (k, l) in pairs])

    everywhere = [((i, j), (k, j)) for i, k in across for j in range(sections)]
    runs = [
        lax.ppermute(last[:kept], "tm", across),
        over_both(last[kept:], [pair for pair in everywhere if pair != SPARED]),
    ]

    def near_transfers():
        in_state = lax.ppermute(state, "tm", on_chip)
        in_adjoint = lax.ppermute(adjoint, "tm", on_chip)
        edge = pl.pallas_call(
            pick_kernel,
            out_shape=cells,
            in_specs=[VMEM, VMEM],
            out_specs=VMEM,
            compiler_params=params(16),
            cost_estimate=SMALL,
            name="pick",
        )(state, adjoint)
        return lax.ppermute(edge, "sec", [(i, i ^ 1) for i in range(sections)]), in_state, in_adjoint

    def nothing():
        return jnp.zeros(cells.shape, cells.dtype), state, adjoint

    near = lax.cond(lax.axis_index("tm") % 2 >= 0, near_transfers, nothing)
    half_way = [
        over_both(last[start : start + SHARE], [(SPARED[0], (i, 0))]) for start, i in zip(starts[2:], via)
    ]
    runs += [over_both(x, [((i, 0), SPARED[1])]) for x, i in zip(half_way, via)]
    res, adj = pl.pallas_call(
        main_kernel,
        out_shape=(block, block),
        in_specs=[SMEM] * 2 + [VMEM] * 5,
        out_specs=(VMEM, VMEM),
        compiler_params=params(24),
        cost_estimate=SMALL,
        name="local_part",
    )(plan, valve, state, adjoint, *near)

    def finish(name, scale, low, size, part, came, before):
        return pl.pallas_call(
            functools.partial(finish_kernel, scale, low),
            out_shape=(block, jax.ShapeDtypeStruct((8, 128), state.dtype)),
            in_specs=[VMEM] * 2 + [ANY] * len(before),
            out_specs=(ANY, VMEM),
            scratch_shapes=[
                pltpu.VMEM((instances, size) + state.shape[2:], state.dtype),
                pltpu.SemaphoreType.DMA((size,)),
            ],
            compiler_params=params(16),
            cost_estimate=SMALL,
            name=name,
        )(part, came, *before)

    residual, token = finish("finish_residual", 1.0, 0, comps, res, far_state, runs[2:])
    begun, token = finish("finish_adjoint", -1.0, 0, cut, adj, far_adjoint, [token])

    def after(came, name):
        return pl.pallas_call(
            after_kernel,
            out_shape=jax.ShapeDtypeStruct(came.shape, came.dtype),
            in_specs=[ANY, ANY],
            out_specs=ANY,
            input_output_aliases={0: 0},
            compiler_params=params(1),
            cost_estimate=SMALL,
            name=name,
        )(came, token)

    runs = [after(runs[0], "first_after"), after(runs[1], "second_after")] + runs[2:]
    odd = lax.axis_index("tm") % 2 == 1
    came = jnp.concatenate([runs[0], runs[1] + jnp.concatenate(runs[2:])]).reshape((instances,) + state.shape[2:])
    line = jnp.where(odd, came[::-1], came)
    reach = jnp.stack([from_before(line, t) for t in range(instances)])
    final = adj[:, cut] + jnp.where(odd, -reach[::-1], reach)
    return residual, lax.dynamic_update_slice(begun, final[:, None], (0, cut, 0, 0, 0))


def solution(mesh):
    spec = P("tm", None, None, "sec", None)
    return jax.shard_map(
        local,
        mesh=mesh,
        in_specs=(spec, spec, P("tm", None), P("tm", None)),
        out_specs=(spec, spec),
        check_vma=False,
    )
```

```python
import functools

import jax
import jax.numpy as jnp
from jax import lax
from jax.experimental import pallas as pl
from jax.experimental.pallas import tpu as pltpu
from jax.sharding import PartitionSpec as P

STENCIL = (0.8, -0.2, 4.0 / 105.0, -1.0 / 280.0)
TIME_SCALE = 4.0
FLOW_VELOCITY = 1.0
AXIAL_DISPERSION = 0.3
RADIAL_SPREADING = 0.2
BINDING_STRENGTH = (1.5, 0.6)
HEAT_EXPONENT = (0.5, 0.3)
KINETIC = (1.2, 0.7)
CAPACITY = (2.0, 1.0)
SORPTION_HEAT = (0.4, 0.25)
PURGE_GAIN = 1.5

REACH = len(STENCIL)
WEIGHTS = tuple(TIME_SCALE * c for c in STENCIL)
MOVING = (0, 1, 2, 5)
CENTRE = FLOW_VELOCITY + 2.0 * AXIAL_DISPERSION + 2.0 * RADIAL_SPREADING
UPWIND = FLOW_VELOCITY + AXIAL_DISPERSION
SPARED = ((2, 0), (1, 0))
VIA = (5, 9, 13)
SHARE = 2


def is_odd():
    return lax.rem(lax.axis_index("tm"), 2) == 1


def shifted(x, step, edge):
    cells = x.shape[0]
    row = lax.broadcasted_iota(jnp.int32, x.shape, 0)
    if step > 0:
        return jnp.where(row == 0, edge, pltpu.roll(x, 1, 0))
    return jnp.where(row == cells - 1, edge, pltpu.roll(x, cells - 1, 0))


def radial_pair(x):
    width = x.shape[1]
    lane = lax.broadcasted_iota(jnp.int32, x.shape, 1)
    lower = jnp.where(lane == 0, 0.0, pltpu.roll(x, 1, 1))
    upper = jnp.where(lane == width - 1, 0.0, pltpu.roll(x, width - 1, 1))
    return lower + upper


def transport(x, near, far):
    return CENTRE * x - UPWIND * near - AXIAL_DISPERSION * far - RADIAL_SPREADING * radial_pair(x)


def pick_kernel(state, adjoint, edge):
    instances, _, beds, cells, _ = state.shape
    first = lax.axis_index("sec") == 0

    def step(t, carry):
        for n, x in enumerate((state, adjoint)):
            for k, c in enumerate(MOVING):
                for b in range(beds):
                    row = jnp.where(first, x[t, c, b, cells - 1 :], x[t, c, b, :1])
                    edge[t, n * len(MOVING) + k, b : b + 1] = row
        return carry

    lax.fori_loop(0, instances, step, 0)


def from_before(line, t):
    total = 0.0
    for j in range(t, len(line)):
        total = total + WEIGHTS[t + len(line) - j - 1] * line[j]
    return total


def main_kernel(plan, valve, state, adjoint, edge, in_state, in_adjoint, res, adj):
    instances, comps, beds, cells, _ = res.shape
    odd = is_odd()
    first = lax.axis_index("sec") == 0
    last = lax.axis_index("sec") == lax.axis_size("sec") - 1

    def cell_block(i, carry):
        t = i // beds
        b = lax.rem(i, beds)
        x = [state[t, c, b] for c in range(comps)]
        m = [adjoint[t, c, b] for c in range(comps)]
        y1, y2, _, q1, q2, temp = x
        b1 = BINDING_STRENGTH[0] * jnp.exp(HEAT_EXPONENT[0] * temp)
        b2 = BINDING_STRENGTH[1] * jnp.exp(HEAT_EXPONENT[1] * temp)
        over = 1.0 / (1.0 + b1 * y1 + b2 * y2)
        slope1 = b1 * over
        slope2 = b2 * over
        cover1 = slope1 * y1
        cover2 = slope2 * y2
        rate1 = KINETIC[0] * (CAPACITY[0] * cover1 - q1)
        rate2 = KINETIC[1] * (CAPACITY[1] * cover2 - q2)
        m1 = m[0] - m[3] - SORPTION_HEAT[0] * m[5]
        m2 = m[1] - m[4] - SORPTION_HEAT[1] * m[5]
        g1 = (KINETIC[0] * CAPACITY[0]) * m1
        g2 = (KINETIC[1] * CAPACITY[1]) * m2
        h = g1 * cover1 + g2 * cover2
        e1 = g1 - h
        e2 = g2 - h
        source = {0: rate1, 1: rate2, 5: -SORPTION_HEAT[0] * rate1 - SORPTION_HEAT[1] * rate2}
        pulled = {
            0: slope1 * e1,
            1: slope2 * e2,
            5: HEAT_EXPONENT[0] * cover1 * e1 + HEAT_EXPONENT[1] * cover2 * e2,
        }
        for k, c in enumerate(MOVING):
            from_x = edge[t, k, b][None]
            from_m = edge[t, len(MOVING) + k, b][None]
            below_x = jnp.where(first, 0.0, from_x)
            above_x = jnp.where(last, 0.0, from_x)
            below_m = jnp.where(first, 0.0, from_m)
            above_m = jnp.where(last, 0.0, from_m)
            r = transport(x[c], shifted(x[c], 1, below_x), shifted(x[c], -1, above_x))
            a = transport(m[c], shifted(m[c], -1, above_m), shifted(m[c], 1, below_m))
            res[t, c, b] = r + source[c] if c in source else r
            adj[t, c, b] = a + pulled[c] if c in pulled else a
        res[t, 3, b] = -rate1
        res[t, 4, b] = -rate2
        adj[t, 3, b] = -KINETIC[0] * m1
        adj[t, 4, b] = -KINETIC[1] * m2
        return carry

    lax.fori_loop(0, instances * beds, cell_block, 0)

    @pl.when(last)
    def _():
        def purge(i, carry):
            t = i // beds
            b = lax.rem(i, beds)
            s = lax.rem(b + plan[t, b], beds)
            gain = PURGE_GAIN * valve[t, b].astype(jnp.float32)
            end = pl.ds(cells - 1, 1)
            for c in range(3):
                res[t, c, b, end] += gain * (state[t, c, b, end] - state[t, c, s, end])
                flow = gain * adjoint[t, c, b, end]
                adj[t, c, b, end] += flow
                adj[t, c, s, end] -= flow
            return carry

        lax.fori_loop(0, instances * beds, purge, 0)

    sign = jnp.where(odd, -1.0, 1.0)
    at = [jnp.where(odd, instances - 1 - t, t) for t in range(instances)]

    def time_block(i, carry):
        c = i // beds
        b = lax.rem(i, beds)
        for own, near, out, factor in ((state, in_state, res, sign), (adjoint, in_adjoint, adj, -sign)):
            line = [own[at[t], c, b] for t in range(instances)]
            line += [near[at[t], c, b] for t in range(instances)]
            for t in range(instances):
                total = 0.0
                for k in range(1, REACH + 1):
                    diff = line[t + k]
                    if t - k >= 0:
                        diff = diff - line[t - k]
                    total = total + WEIGHTS[k - 1] * diff
                out[at[t], c, b] += factor * total
        return carry

    lax.fori_loop(0, comps * beds, time_block, 0)


def finish_kernel(scale, low, starts, part, *rest):
    came, (out, whole, sem) = rest[: len(starts) or 1], rest[-3:]
    instances, size, beds, _, _ = whole.shape

    def moved(c):
        return pltpu.make_async_copy(whole.at[:, pl.ds(c, 1)], out.at[:, pl.ds(low + c, 1)], sem.at[c])

    def arrived(t, c, b):
        if not starts:
            return came[0][t, c, b]
        n = t * beds + b
        return sum(run[n - start] for run, start in zip(came, starts) if start <= n < start + run.shape[0])

    def finish(sign, at):
        def component(c, carry):
            for b in range(beds):
                line = [arrived(at[t], c, b) for t in range(instances)]
                for t in range(instances):
                    whole[at[t], c, b] = part[at[t], low + c, b] - sign * from_before(line, t)
            moved(c).start()
            return carry

        lax.fori_loop(0, size, component, 0)

    odd = is_odd()

    @pl.when(odd)
    def _():
        finish(-scale, list(reversed(range(instances))))

    @pl.when(jnp.logical_not(odd))
    def _():
        finish(scale, list(range(instances)))

    for c in range(size):
        moved(c).wait()


VMEM = pl.BlockSpec(memory_space=pltpu.VMEM)
SMEM = pl.BlockSpec(memory_space=pltpu.SMEM)
ANY = pl.BlockSpec(memory_space=pl.ANY)
SMALL = pl.CostEstimate(flops=1000, bytes_accessed=1000, transcendentals=0)


def params(mib):
    return pltpu.CompilerParams(vmem_limit_bytes=mib * 2**20)


def local(state, adjoint, plan, valve):
    count = lax.axis_size("tm")
    sections = lax.axis_size("sec")
    instances, comps, beds, _, width = state.shape
    block = jax.ShapeDtypeStruct(state.shape, state.dtype)
    cells = jax.ShapeDtypeStruct((instances, 2 * len(MOVING), beds, width), state.dtype)
    across = [(i, (i + 1) % count if i % 2 else (i - 1) % count) for i in range(count)]
    on_chip = [(i, i ^ 1) for i in range(count)]
    far_state = lax.ppermute(state, "tm", across)
    cut = comps - 1
    far_adjoint = lax.ppermute(adjoint[:, :cut], "tm", across)

    last = adjoint[:, cut].reshape((instances * beds,) + state.shape[3:])
    via = [i for i in VIA if i < count]
    kept = instances * beds - SHARE * len(via)
    starts = [0, kept] + [kept + SHARE * n for n in range(len(via))]

    def over_both(x, pairs):
        return lax.ppermute(x, ("tm", "sec"), [(i * sections + j, k * sections + l) for (i, j), (k, l) in pairs])

    everywhere = [((i, j), (k, j)) for i, k in across for j in range(sections)]
    runs = [
        lax.ppermute(last[:kept], "tm", across),
        over_both(last[kept:], [pair for pair in everywhere if pair != SPARED]),
    ]

    def near_transfers():
        in_state = lax.ppermute(state, "tm", on_chip)
        in_adjoint = lax.ppermute(adjoint, "tm", on_chip)
        edge = pl.pallas_call(
            pick_kernel,
            out_shape=cells,
            in_specs=[VMEM, VMEM],
            out_specs=VMEM,
            compiler_params=params(16),
            cost_estimate=SMALL,
            name="pick",
        )(state, adjoint)
        return lax.ppermute(edge, "sec", [(i, i ^ 1) for i in range(sections)]), in_state, in_adjoint

    def nothing():
        return jnp.zeros(cells.shape, cells.dtype), state, adjoint

    near = lax.cond(lax.axis_index("tm") % 2 >= 0, near_transfers, nothing)
    half_way = [
        over_both(last[start : start + SHARE], [(SPARED[0], (i, 0))]) for start, i in zip(starts[2:], via)
    ]
    runs += [over_both(x, [((i, 0), SPARED[1])]) for x, i in zip(half_way, via)]
    res, adj = pl.pallas_call(
        main_kernel,
        out_shape=(block, block),
        in_specs=[SMEM] * 2 + [VMEM] * 5,
        out_specs=(VMEM, VMEM),
        compiler_params=params(24),
        cost_estimate=SMALL,
        name="local_part",
    )(plan, valve, state, adjoint, *near)

    def finish(name, scale, low, size, part, came, before, starts=(), begun=False):
        return pl.pallas_call(
            functools.partial(finish_kernel, scale, low, starts),
            out_shape=block,
            in_specs=[VMEM] * (1 + len(came)) + [ANY] * len(before),
            out_specs=ANY,
            scratch_shapes=[
                pltpu.VMEM((instances, size) + state.shape[2:], state.dtype),
                pltpu.SemaphoreType.DMA((size,)),
            ],
            input_output_aliases={1 + len(came): 0} if begun else {},
            compiler_params=params(16),
            cost_estimate=SMALL,
            name=name,
        )(part, *came, *before)

    residual = finish("finish_residual", 1.0, 0, comps, res, [far_state], runs[2:])
    begun = finish("finish_adjoint", -1.0, 0, cut, adj, [far_adjoint], [residual[0, 0, 0, :8]])
    return residual, finish("finish_last", -1.0, cut, 1, adj, runs, [begun], starts, True)


def solution(mesh):
    spec = P("tm", None, None, "sec", None)
    return jax.shard_map(
        local,
        mesh=mesh,
        in_specs=(spec, spec, P("tm", None), P("tm", None)),
        out_specs=(spec, spec),
        check_vma=False,
    )
```

```python
import functools

import jax
import jax.numpy as jnp
from jax import lax
from jax.experimental import pallas as pl
from jax.experimental.pallas import tpu as pltpu
from jax.sharding import PartitionSpec as P

STENCIL = (0.8, -0.2, 4.0 / 105.0, -1.0 / 280.0)
TIME_SCALE = 4.0
FLOW_VELOCITY = 1.0
AXIAL_DISPERSION = 0.3
RADIAL_SPREADING = 0.2
BINDING_STRENGTH = (1.5, 0.6)
HEAT_EXPONENT = (0.5, 0.3)
KINETIC = (1.2, 0.7)
CAPACITY = (2.0, 1.0)
SORPTION_HEAT = (0.4, 0.25)
PURGE_GAIN = 1.5

REACH = len(STENCIL)
WEIGHTS = tuple(TIME_SCALE * c for c in STENCIL)
MOVING = (0, 1, 2, 5)
CENTRE = FLOW_VELOCITY + 2.0 * AXIAL_DISPERSION + 2.0 * RADIAL_SPREADING
UPWIND = FLOW_VELOCITY + AXIAL_DISPERSION
SPARED = ((2, 0), (1, 0))
VIA = (9, 13)
SHARE = 3


def is_odd():
    return lax.rem(lax.axis_index("tm"), 2) == 1


def shifted(x, step, edge):
    cells = x.shape[0]
    row = lax.broadcasted_iota(jnp.int32, x.shape, 0)
    if step > 0:
        return jnp.where(row == 0, edge, pltpu.roll(x, 1, 0))
    return jnp.where(row == cells - 1, edge, pltpu.roll(x, cells - 1, 0))


def radial_pair(x):
    width = x.shape[1]
    lane = lax.broadcasted_iota(jnp.int32, x.shape, 1)
    lower = jnp.where(lane == 0, 0.0, pltpu.roll(x, 1, 1))
    upper = jnp.where(lane == width - 1, 0.0, pltpu.roll(x, width - 1, 1))
    return lower + upper


def transport(x, near, far):
    return CENTRE * x - UPWIND * near - AXIAL_DISPERSION * far - RADIAL_SPREADING * radial_pair(x)


def pick_kernel(state, adjoint, edge):
    instances, _, beds, cells, _ = state.shape
    first = lax.axis_index("sec") == 0

    def step(t, carry):
        for n, x in enumerate((state, adjoint)):
            for k, c in enumerate(MOVING):
                for b in range(beds):
                    row = jnp.where(first, x[t, c, b, cells - 1 :], x[t, c, b, :1])
                    edge[t, n * len(MOVING) + k, b : b + 1] = row
        return carry

    lax.fori_loop(0, instances, step, 0)


def from_before(line, t):
    total = 0.0
    for j in range(t, len(line)):
        total = total + WEIGHTS[t + len(line) - j - 1] * line[j]
    return total


def main_kernel(plan, valve, state, adjoint, edge, in_state, in_adjoint, res, adj):
    instances, comps, beds, cells, _ = res.shape
    odd = is_odd()
    first = lax.axis_index("sec") == 0
    last = lax.axis_index("sec") == lax.axis_size("sec") - 1

    def cell_block(i, carry):
        t = i // beds
        b = lax.rem(i, beds)
        x = [state[t, c, b] for c in range(comps)]
        m = [adjoint[t, c, b] for c in range(comps)]
        y1, y2, _, q1, q2, temp = x
        b1 = BINDING_STRENGTH[0] * jnp.exp(HEAT_EXPONENT[0] * temp)
        b2 = BINDING_STRENGTH[1] * jnp.exp(HEAT_EXPONENT[1] * temp)
        over = 1.0 / (1.0 + b1 * y1 + b2 * y2)
        slope1 = b1 * over
        slope2 = b2 * over
        cover1 = slope1 * y1
        cover2 = slope2 * y2
        rate1 = KINETIC[0] * (CAPACITY[0] * cover1 - q1)
        rate2 = KINETIC[1] * (CAPACITY[1] * cover2 - q2)
        m1 = m[0] - m[3] - SORPTION_HEAT[0] * m[5]
        m2 = m[1] - m[4] - SORPTION_HEAT[1] * m[5]
        g1 = (KINETIC[0] * CAPACITY[0]) * m1
        g2 = (KINETIC[1] * CAPACITY[1]) * m2
        h = g1 * cover1 + g2 * cover2
        e1 = g1 - h
        e2 = g2 - h
        source = {0: rate1, 1: rate2, 5: -SORPTION_HEAT[0] * rate1 - SORPTION_HEAT[1] * rate2}
        pulled = {
            0: slope1 * e1,
            1: slope2 * e2,
            5: HEAT_EXPONENT[0] * cover1 * e1 + HEAT_EXPONENT[1] * cover2 * e2,
        }
        for k, c in enumerate(MOVING):
            from_x = edge[t, k, b][None]
            from_m = edge[t, len(MOVING) + k, b][None]
            below_x = jnp.where(first, 0.0, from_x)
            above_x = jnp.where(last, 0.0, from_x)
            below_m = jnp.where(first, 0.0, from_m)
            above_m = jnp.where(last, 0.0, from_m)
            r = transport(x[c], shifted(x[c], 1, below_x), shifted(x[c], -1, above_x))
            a = transport(m[c], shifted(m[c], -1, above_m), shifted(m[c], 1, below_m))
            res[t, c, b] = r + source[c] if c in source else r
            adj[t, c, b] = a + pulled[c] if c in pulled else a
        res[t, 3, b] = -rate1
        res[t, 4, b] = -rate2
        adj[t, 3, b] = -KINETIC[0] * m1
        adj[t, 4, b] = -KINETIC[1] * m2
        return carry

    lax.fori_loop(0, instances * beds, cell_block, 0)

    @pl.when(last)
    def _():
        def purge(i, carry):
            t = i // beds
            b = lax.rem(i, beds)
            s = lax.rem(b + plan[t, b], beds)
            gain = PURGE_GAIN * valve[t, b].astype(jnp.float32)
            end = pl.ds(cells - 1, 1)
            for c in range(3):
                res[t, c, b, end] += gain * (state[t, c, b, end] - state[t, c, s, end])
                flow = gain * adjoint[t, c, b, end]
                adj[t, c, b, end] += flow
                adj[t, c, s, end] -= flow
            return carry

        lax.fori_loop(0, instances * beds, purge, 0)

    sign = jnp.where(odd, -1.0, 1.0)
    at = [jnp.where(odd, instances - 1 - t, t) for t in range(instances)]

    def time_block(i, carry):
        c = i // beds
        b = lax.rem(i, beds)
        for own, near, out, factor in ((state, in_state, res, sign), (adjoint, in_adjoint, adj, -sign)):
            line = [own[at[t], c, b] for t in range(instances)]
            line += [near[at[t], c, b] for t in range(instances)]
            for t in range(instances):
                total = 0.0
                for k in range(1, REACH + 1):
                    diff = line[t + k]
                    if t - k >= 0:
                        diff = diff - line[t - k]
                    total = total + WEIGHTS[k - 1] * diff
                out[at[t], c, b] += factor * total
        return carry

    lax.fori_loop(0, comps * beds, time_block, 0)


def finish_kernel(scale, low, starts, part, *rest):
    came, (out, whole, sem) = rest[: len(starts) or 1], rest[-3:]
    instances, size, beds, _, _ = whole.shape

    def moved(c):
        return pltpu.make_async_copy(whole.at[:, pl.ds(c, 1)], out.at[:, pl.ds(low + c, 1)], sem.at[c])

    def arrived(t, c, b):
        if not starts:
            return came[0][t, c, b]
        n = t * beds + b
        return sum(run[n - start] for run, start in zip(came, starts) if start <= n < start + run.shape[0])

    def finish(sign, at):
        def component(c, carry):
            for b in range(beds):
                line = [arrived(at[t], c, b) for t in range(instances)]
                for t in range(instances):
                    whole[at[t], c, b] = part[at[t], low + c, b] - sign * from_before(line, t)
            moved(c).start()
            return carry

        lax.fori_loop(0, size, component, 0)

    odd = is_odd()

    @pl.when(odd)
    def _():
        finish(-scale, list(reversed(range(instances))))

    @pl.when(jnp.logical_not(odd))
    def _():
        finish(scale, list(range(instances)))

    for c in range(size):
        moved(c).wait()


VMEM = pl.BlockSpec(memory_space=pltpu.VMEM)
SMEM = pl.BlockSpec(memory_space=pltpu.SMEM)
ANY = pl.BlockSpec(memory_space=pl.ANY)
SMALL = pl.CostEstimate(flops=1000, bytes_accessed=1000, transcendentals=0)


def params(mib):
    return pltpu.CompilerParams(vmem_limit_bytes=mib * 2**20)


def local(state, adjoint, plan, valve):
    count = lax.axis_size("tm")
    sections = lax.axis_size("sec")
    instances, comps, beds, _, width = state.shape
    block = jax.ShapeDtypeStruct(state.shape, state.dtype)
    cells = jax.ShapeDtypeStruct((instances, 2 * len(MOVING), beds, width), state.dtype)
    across = [(i, (i + 1) % count if i % 2 else (i - 1) % count) for i in range(count)]
    on_chip = [(i, i ^ 1) for i in range(count)]
    far_state = lax.ppermute(state, "tm", across)
    cut = comps - 2
    far_adjoint = lax.ppermute(adjoint[:, :cut], "tm", across)

    cut_up = adjoint[:, cut].reshape((instances * beds,) + state.shape[3:])
    via = [i for i in VIA if i < count]
    kept = instances * beds - SHARE * len(via)
    starts = [0, kept] + [kept + SHARE * n for n in range(len(via))]

    def over_both(x, pairs):
        return lax.ppermute(x, ("tm", "sec"), [(i * sections + j, k * sections + l) for (i, j), (k, l) in pairs])

    everywhere = [((i, j), (k, j)) for i, k in across for j in range(sections)]
    runs = [
        lax.ppermute(cut_up[:kept], "tm", across),
        over_both(cut_up[kept:], [pair for pair in everywhere if pair != SPARED]),
    ]

    far_last = lax.ppermute(adjoint[:, cut + 1 :], "tm", across)

    def near_transfers():
        in_state = lax.ppermute(state, "tm", on_chip)
        in_adjoint = lax.ppermute(adjoint, "tm", on_chip)
        edge = pl.pallas_call(
            pick_kernel,
            out_shape=cells,
            in_specs=[VMEM, VMEM],
            out_specs=VMEM,
            compiler_params=params(16),
            cost_estimate=SMALL,
            name="pick",
        )(state, adjoint)
        return lax.ppermute(edge, "sec", [(i, i ^ 1) for i in range(sections)]), in_state, in_adjoint

    def nothing():
        return jnp.zeros(cells.shape, cells.dtype), state, adjoint

    near = lax.cond(lax.axis_index("tm") % 2 >= 0, near_transfers, nothing)
    half_way = [
        over_both(cut_up[start : start + SHARE], [(SPARED[0], (i, 0))]) for start, i in zip(starts[2:], via)
    ]
    runs += [over_both(x, [((i, 0), SPARED[1])]) for x, i in zip(half_way, via)]
    res, adj = pl.pallas_call(
        main_kernel,
        out_shape=(block, block),
        in_specs=[SMEM] * 2 + [VMEM] * 5,
        out_specs=(VMEM, VMEM),
        compiler_params=params(24),
        cost_estimate=SMALL,
        name="local_part",
    )(plan, valve, state, adjoint, *near)

    def finish(name, scale, low, size, part, came, before, starts=(), begun=False):
        return pl.pallas_call(
            functools.partial(finish_kernel, scale, low, starts),
            out_shape=block,
            in_specs=[VMEM] * (1 + len(came)) + [ANY] * len(before),
            out_specs=ANY,
            scratch_shapes=[
                pltpu.VMEM((instances, size) + state.shape[2:], state.dtype),
                pltpu.SemaphoreType.DMA((size,)),
            ],
            input_output_aliases={1 + len(came): 0} if begun else {},
            compiler_params=params(16),
            cost_estimate=SMALL,
            name=name,
        )(part, *came, *before)

    residual = finish("finish_residual", 1.0, 0, comps, res, [far_state], runs[2:])
    begun = finish("finish_adjoint", -1.0, 0, cut, adj, [far_adjoint], [residual[0, 0, 0, :8]])
    begun = finish("finish_runs", -1.0, cut, 1, adj, runs, [begun], starts, True)
    return residual, finish("finish_last", -1.0, cut + 1, 1, adj, [far_last], [begun], (), True)


def solution(mesh):
    spec = P("tm", None, None, "sec", None)
    return jax.shard_map(
        local,
        mesh=mesh,
        in_specs=(spec, spec, P("tm", None), P("tm", None)),
        out_specs=(spec, spec),
        check_vma=False,
    )
```

```python
import functools

import jax
import jax.numpy as jnp
from jax import lax
from jax.experimental import pallas as pl
from jax.experimental.pallas import tpu as pltpu
from jax.sharding import PartitionSpec as P

STENCIL = (0.8, -0.2, 4.0 / 105.0, -1.0 / 280.0)
TIME_SCALE = 4.0
FLOW_VELOCITY = 1.0
AXIAL_DISPERSION = 0.3
RADIAL_SPREADING = 0.2
BINDING_STRENGTH = (1.5, 0.6)
HEAT_EXPONENT = (0.5, 0.3)
KINETIC = (1.2, 0.7)
CAPACITY = (2.0, 1.0)
SORPTION_HEAT = (0.4, 0.25)
PURGE_GAIN = 1.5

REACH = len(STENCIL)
WEIGHTS = tuple(TIME_SCALE * c for c in STENCIL)
MOVING = (0, 1, 2, 5)
CENTRE = FLOW_VELOCITY + 2.0 * AXIAL_DISPERSION + 2.0 * RADIAL_SPREADING
UPWIND = FLOW_VELOCITY + AXIAL_DISPERSION
SPARED = ((2, 0), (1, 0))
VIA = ((9, 0), (13, 0), (1, 1))
SHARE = 2


def is_odd():
    return lax.rem(lax.axis_index("tm"), 2) == 1


def shifted(x, step, edge):
    cells = x.shape[0]
    row = lax.broadcasted_iota(jnp.int32, x.shape, 0)
    if step > 0:
        return jnp.where(row == 0, edge, pltpu.roll(x, 1, 0))
    return jnp.where(row == cells - 1, edge, pltpu.roll(x, cells - 1, 0))


def radial_pair(x):
    width = x.shape[1]
    lane = lax.broadcasted_iota(jnp.int32, x.shape, 1)
    lower = jnp.where(lane == 0, 0.0, pltpu.roll(x, 1, 1))
    upper = jnp.where(lane == width - 1, 0.0, pltpu.roll(x, width - 1, 1))
    return lower + upper


def transport(x, near, far):
    return CENTRE * x - UPWIND * near - AXIAL_DISPERSION * far - RADIAL_SPREADING * radial_pair(x)


def pick_kernel(state, adjoint, edge):
    instances, _, beds, cells, _ = state.shape
    first = lax.axis_index("sec") == 0

    def step(t, carry):
        for n, x in enumerate((state, adjoint)):
            for k, c in enumerate(MOVING):
                for b in range(beds):
                    row = jnp.where(first, x[t, c, b, cells - 1 :], x[t, c, b, :1])
                    edge[t, n * len(MOVING) + k, b : b + 1] = row
        return carry

    lax.fori_loop(0, instances, step, 0)


def from_before(line, t):
    total = 0.0
    for j in range(t, len(line)):
        total = total + WEIGHTS[t + len(line) - j - 1] * line[j]
    return total


def main_kernel(plan, valve, state, adjoint, edge, in_state, in_adjoint, res, adj):
    instances, comps, beds, cells, _ = res.shape
    odd = is_odd()
    first = lax.axis_index("sec") == 0
    last = lax.axis_index("sec") == lax.axis_size("sec") - 1

    def cell_block(i, carry):
        t = i // beds
        b = lax.rem(i, beds)
        x = [state[t, c, b] for c in range(comps)]
        m = [adjoint[t, c, b] for c in range(comps)]
        y1, y2, _, q1, q2, temp = x
        b1 = BINDING_STRENGTH[0] * jnp.exp(HEAT_EXPONENT[0] * temp)
        b2 = BINDING_STRENGTH[1] * jnp.exp(HEAT_EXPONENT[1] * temp)
        over = 1.0 / (1.0 + b1 * y1 + b2 * y2)
        slope1 = b1 * over
        slope2 = b2 * over
        cover1 = slope1 * y1
        cover2 = slope2 * y2
        rate1 = KINETIC[0] * (CAPACITY[0] * cover1 - q1)
        rate2 = KINETIC[1] * (CAPACITY[1] * cover2 - q2)
        m1 = m[0] - m[3] - SORPTION_HEAT[0] * m[5]
        m2 = m[1] - m[4] - SORPTION_HEAT[1] * m[5]
        g1 = (KINETIC[0] * CAPACITY[0]) * m1
        g2 = (KINETIC[1] * CAPACITY[1]) * m2
        h = g1 * cover1 + g2 * cover2
        e1 = g1 - h
        e2 = g2 - h
        source = {0: rate1, 1: rate2, 5: -SORPTION_HEAT[0] * rate1 - SORPTION_HEAT[1] * rate2}
        pulled = {
            0: slope1 * e1,
            1: slope2 * e2,
            5: HEAT_EXPONENT[0] * cover1 * e1 + HEAT_EXPONENT[1] * cover2 * e2,
        }
        for k, c in enumerate(MOVING):
            from_x = edge[t, k, b][None]
            from_m = edge[t, len(MOVING) + k, b][None]
            below_x = jnp.where(first, 0.0, from_x)
            above_x = jnp.where(last, 0.0, from_x)
            below_m = jnp.where(first, 0.0, from_m)
            above_m = jnp.where(last, 0.0, from_m)
            r = transport(x[c], shifted(x[c], 1, below_x), shifted(x[c], -1, above_x))
            a = transport(m[c], shifted(m[c], -1, above_m), shifted(m[c], 1, below_m))
            res[t, c, b] = r + source[c] if c in source else r
            adj[t, c, b] = a + pulled[c] if c in pulled else a
        res[t, 3, b] = -rate1
        res[t, 4, b] = -rate2
        adj[t, 3, b] = -KINETIC[0] * m1
        adj[t, 4, b] = -KINETIC[1] * m2
        return carry

    lax.fori_loop(0, instances * beds, cell_block, 0)

    @pl.when(last)
    def _():
        def purge(i, carry):
            t = i // beds
            b = lax.rem(i, beds)
            s = lax.rem(b + plan[t, b], beds)
            gain = PURGE_GAIN * valve[t, b].astype(jnp.float32)
            end = pl.ds(cells - 1, 1)
            for c in range(3):
                res[t, c, b, end] += gain * (state[t, c, b, end] - state[t, c, s, end])
                flow = gain * adjoint[t, c, b, end]
                adj[t, c, b, end] += flow
                adj[t, c, s, end] -= flow
            return carry

        lax.fori_loop(0, instances * beds, purge, 0)

    sign = jnp.where(odd, -1.0, 1.0)
    at = [jnp.where(odd, instances - 1 - t, t) for t in range(instances)]

    def time_block(i, carry):
        c = i // beds
        b = lax.rem(i, beds)
        for own, near, out, factor in ((state, in_state, res, sign), (adjoint, in_adjoint, adj, -sign)):
            line = [own[at[t], c, b] for t in range(instances)]
            line += [near[at[t], c, b] for t in range(instances)]
            for t in range(instances):
                total = 0.0
                for k in range(1, REACH + 1):
                    diff = line[t + k]
                    if t - k >= 0:
                        diff = diff - line[t - k]
                    total = total + WEIGHTS[k - 1] * diff
                out[at[t], c, b] += factor * total
        return carry

    lax.fori_loop(0, comps * beds, time_block, 0)


def finish_kernel(scale, low, starts, part, *rest):
    came, (out, whole, sem) = rest[: len(starts) or 1], rest[-3:]
    instances, size, beds, _, _ = whole.shape

    def moved(c):
        return pltpu.make_async_copy(whole.at[:, pl.ds(c, 1)], out.at[:, pl.ds(low + c, 1)], sem.at[c])

    def arrived(t, c, b):
        if not starts:
            return came[0][t, c, b]
        n = t * beds + b
        return sum(run[n - start] for run, start in zip(came, starts) if start <= n < start + run.shape[0])

    def finish(sign, at):
        def component(c, carry):
            for b in range(beds):
                line = [arrived(at[t], c, b) for t in range(instances)]
                for t in range(instances):
                    whole[at[t], c, b] = part[at[t], low + c, b] - sign * from_before(line, t)
            moved(c).start()
            return carry

        lax.fori_loop(0, size, component, 0)

    odd = is_odd()

    @pl.when(odd)
    def _():
        finish(-scale, list(reversed(range(instances))))

    @pl.when(jnp.logical_not(odd))
    def _():
        finish(scale, list(range(instances)))

    for c in range(size):
        moved(c).wait()


VMEM = pl.BlockSpec(memory_space=pltpu.VMEM)
SMEM = pl.BlockSpec(memory_space=pltpu.SMEM)
ANY = pl.BlockSpec(memory_space=pl.ANY)
SMALL = pl.CostEstimate(flops=1000, bytes_accessed=1000, transcendentals=0)


def params(mib):
    return pltpu.CompilerParams(vmem_limit_bytes=mib * 2**20)


def local(state, adjoint, plan, valve):
    count = lax.axis_size("tm")
    sections = lax.axis_size("sec")
    instances, comps, beds, _, width = state.shape
    block = jax.ShapeDtypeStruct(state.shape, state.dtype)
    cells = jax.ShapeDtypeStruct((instances, 2 * len(MOVING), beds, width), state.dtype)
    across = [(i, (i + 1) % count if i % 2 else (i - 1) % count) for i in range(count)]
    on_chip = [(i, i ^ 1) for i in range(count)]
    far_state = lax.ppermute(state, "tm", across)
    cut = comps - 1
    far_adjoint = lax.ppermute(adjoint[:, :cut], "tm", across)

    last = adjoint[:, cut].reshape((instances * beds,) + state.shape[3:])
    via = [place for place in VIA if place[0] < count]
    kept = instances * beds - SHARE * len(via)
    starts = [0, kept] + [kept + SHARE * n for n in range(len(via))]

    def over_both(x, pairs):
        return lax.ppermute(x, ("tm", "sec"), [(i * sections + j, k * sections + l) for (i, j), (k, l) in pairs])

    everywhere = [((i, j), (k, j)) for i, k in across for j in range(sections)]
    runs = [
        lax.ppermute(last[:kept], "tm", across),
        over_both(last[kept:], [pair for pair in everywhere if pair != SPARED]),
    ]

    def near_transfers():
        in_state = lax.ppermute(state, "tm", on_chip)
        in_adjoint = lax.ppermute(adjoint, "tm", on_chip)
        edge = pl.pallas_call(
            pick_kernel,
            out_shape=cells,
            in_specs=[VMEM, VMEM],
            out_specs=VMEM,
            compiler_params=params(16),
            cost_estimate=SMALL,
            name="pick",
        )(state, adjoint)
        return lax.ppermute(edge, "sec", [(i, i ^ 1) for i in range(sections)]), in_state, in_adjoint

    def nothing():
        return jnp.zeros(cells.shape, cells.dtype), state, adjoint

    near = lax.cond(lax.axis_index("tm") % 2 >= 0, near_transfers, nothing)
    half_way = [
        over_both(last[start : start + SHARE], [(SPARED[0], place)]) for start, place in zip(starts[2:], via)
    ]
    runs += [over_both(x, [(place, SPARED[1])]) for x, place in zip(half_way, via)]
    res, adj = pl.pallas_call(
        main_kernel,
        out_shape=(block, block),
        in_specs=[SMEM] * 2 + [VMEM] * 5,
        out_specs=(VMEM, VMEM),
        compiler_params=params(24),
        cost_estimate=SMALL,
        name="local_part",
    )(plan, valve, state, adjoint, *near)

    def finish(name, scale, low, size, part, came, before, starts=(), begun=False):
        return pl.pallas_call(
            functools.partial(finish_kernel, scale, low, starts),
            out_shape=block,
            in_specs=[VMEM] * (1 + len(came)) + [ANY] * len(before),
            out_specs=ANY,
            scratch_shapes=[
                pltpu.VMEM((instances, size) + state.shape[2:], state.dtype),
                pltpu.SemaphoreType.DMA((size,)),
            ],
            input_output_aliases={1 + len(came): 0} if begun else {},
            compiler_params=params(16),
            cost_estimate=SMALL,
            name=name,
        )(part, *came, *before)

    residual = finish("finish_residual", 1.0, 0, comps, res, [far_state], runs[2:])
    begun = finish("finish_adjoint", -1.0, 0, cut, adj, [far_adjoint], [residual[0, 0, 0, :8]])
    return residual, finish("finish_last", -1.0, cut, 1, adj, runs, [begun], starts, True)


def solution(mesh):
    spec = P("tm", None, None, "sec", None)
    return jax.shard_map(
        local,
        mesh=mesh,
        in_specs=(spec, spec, P("tm", None), P("tm", None)),
        out_specs=(spec, spec),
        check_vma=False,
    )
```

```python
import functools

import jax
import jax.numpy as jnp
from jax import lax
from jax.experimental import pallas as pl
from jax.experimental.pallas import tpu as pltpu
from jax.sharding import PartitionSpec as P

STENCIL = (0.8, -0.2, 4.0 / 105.0, -1.0 / 280.0)
TIME_SCALE = 4.0
FLOW_VELOCITY = 1.0
AXIAL_DISPERSION = 0.3
RADIAL_SPREADING = 0.2
BINDING_STRENGTH = (1.5, 0.6)
HEAT_EXPONENT = (0.5, 0.3)
KINETIC = (1.2, 0.7)
CAPACITY = (2.0, 1.0)
SORPTION_HEAT = (0.4, 0.25)
PURGE_GAIN = 1.5

REACH = len(STENCIL)
WEIGHTS = tuple(TIME_SCALE * c for c in STENCIL)
MOVING = (0, 1, 2, 5)
CENTRE = FLOW_VELOCITY + 2.0 * AXIAL_DISPERSION + 2.0 * RADIAL_SPREADING
UPWIND = FLOW_VELOCITY + AXIAL_DISPERSION
SPARED = ((2, 0), (1, 0))
VIA = (5, 9, 13)
SHARE = 2


def is_odd():
    return lax.rem(lax.axis_index("tm"), 2) == 1


def shifted(x, step, edge):
    cells = x.shape[0]
    row = lax.broadcasted_iota(jnp.int32, x.shape, 0)
    if step > 0:
        return jnp.where(row == 0, edge, pltpu.roll(x, 1, 0))
    return jnp.where(row == cells - 1, edge, pltpu.roll(x, cells - 1, 0))


def radial_pair(x):
    width = x.shape[1]
    lane = lax.broadcasted_iota(jnp.int32, x.shape, 1)
    lower = jnp.where(lane == 0, 0.0, pltpu.roll(x, 1, 1))
    upper = jnp.where(lane == width - 1, 0.0, pltpu.roll(x, width - 1, 1))
    return lower + upper


def transport(x, near, far):
    return CENTRE * x - UPWIND * near - AXIAL_DISPERSION * far - RADIAL_SPREADING * radial_pair(x)


def pick_kernel(state, adjoint, edge):
    instances, _, beds, cells, _ = state.shape
    first = lax.axis_index("sec") == 0

    def step(t, carry):
        for n, x in enumerate((state, adjoint)):
            for k, c in enumerate(MOVING):
                for b in range(beds):
                    row = jnp.where(first, x[t, c, b, cells - 1 :], x[t, c, b, :1])
                    edge[t, n * len(MOVING) + k, b : b + 1] = row
        return carry

    lax.fori_loop(0, instances, step, 0)


def from_before(line, t):
    total = 0.0
    for j in range(t, len(line)):
        total = total + WEIGHTS[t + len(line) - j - 1] * line[j]
    return total


def main_kernel(plan, valve, state, adjoint, edge, in_state, in_adjoint, res, adj):
    instances, comps, beds, cells, _ = res.shape
    odd = is_odd()
    first = lax.axis_index("sec") == 0
    last = lax.axis_index("sec") == lax.axis_size("sec") - 1

    def cell_block(i, carry):
        t = i // beds
        b = lax.rem(i, beds)
        x = [state[t, c, b] for c in range(comps)]
        m = [adjoint[t, c, b] for c in range(comps)]
        y1, y2, _, q1, q2, temp = x
        b1 = BINDING_STRENGTH[0] * jnp.exp(HEAT_EXPONENT[0] * temp)
        b2 = BINDING_STRENGTH[1] * jnp.exp(HEAT_EXPONENT[1] * temp)
        over = 1.0 / (1.0 + b1 * y1 + b2 * y2)
        slope1 = b1 * over
        slope2 = b2 * over
        cover1 = slope1 * y1
        cover2 = slope2 * y2
        rate1 = KINETIC[0] * (CAPACITY[0] * cover1 - q1)
        rate2 = KINETIC[1] * (CAPACITY[1] * cover2 - q2)
        m1 = m[0] - m[3] - SORPTION_HEAT[0] * m[5]
        m2 = m[1] - m[4] - SORPTION_HEAT[1] * m[5]
        g1 = (KINETIC[0] * CAPACITY[0]) * m1
        g2 = (KINETIC[1] * CAPACITY[1]) * m2
        h = g1 * cover1 + g2 * cover2
        e1 = g1 - h
        e2 = g2 - h
        source = {0: rate1, 1: rate2, 5: -SORPTION_HEAT[0] * rate1 - SORPTION_HEAT[1] * rate2}
        pulled = {
            0: slope1 * e1,
            1: slope2 * e2,
            5: HEAT_EXPONENT[0] * cover1 * e1 + HEAT_EXPONENT[1] * cover2 * e2,
        }
        for k, c in enumerate(MOVING):
            from_x = edge[t, k, b][None]
            from_m = edge[t, len(MOVING) + k, b][None]
            below_x = jnp.where(first, 0.0, from_x)
            above_x = jnp.where(last, 0.0, from_x)
            below_m = jnp.where(first, 0.0, from_m)
            above_m = jnp.where(last, 0.0, from_m)
            r = transport(x[c], shifted(x[c], 1, below_x), shifted(x[c], -1, above_x))
            a = transport(m[c], shifted(m[c], -1, above_m), shifted(m[c], 1, below_m))
            res[t, c, b] = r + source[c] if c in source else r
            adj[t, c, b] = a + pulled[c] if c in pulled else a
        res[t, 3, b] = -rate1
        res[t, 4, b] = -rate2
        adj[t, 3, b] = -KINETIC[0] * m1
        adj[t, 4, b] = -KINETIC[1] * m2
        return carry

    lax.fori_loop(0, instances * beds, cell_block, 0)

    @pl.when(last)
    def _():
        def purge(i, carry):
            t = i // beds
            b = lax.rem(i, beds)
            s = lax.rem(b + plan[t, b], beds)
            gain = PURGE_GAIN * valve[t, b].astype(jnp.float32)
            end = pl.ds(cells - 1, 1)
            for c in range(3):
                res[t, c, b, end] += gain * (state[t, c, b, end] - state[t, c, s, end])
                flow = gain * adjoint[t, c, b, end]
                adj[t, c, b, end] += flow
                adj[t, c, s, end] -= flow
            return carry

        lax.fori_loop(0, instances * beds, purge, 0)

    sign = jnp.where(odd, -1.0, 1.0)
    at = [jnp.where(odd, instances - 1 - t, t) for t in range(instances)]

    def time_block(i, carry):
        c = i // beds
        b = lax.rem(i, beds)
        for own, near, out, factor in ((state, in_state, res, sign), (adjoint, in_adjoint, adj, -sign)):
            line = [own[at[t], c, b] for t in range(instances)]
            line += [near[at[t], c, b] for t in range(instances)]
            for t in range(instances):
                total = 0.0
                for k in range(1, REACH + 1):
                    diff = line[t + k]
                    if t - k >= 0:
                        diff = diff - line[t - k]
                    total = total + WEIGHTS[k - 1] * diff
                out[at[t], c, b] += factor * total
        return carry

    lax.fori_loop(0, comps * beds, time_block, 0)


def finish_kernel(scale, low, starts, part, *rest):
    came, (out, whole, sem) = rest[: len(starts) or 1], rest[-3:]
    instances, size, beds, _, _ = whole.shape

    def moved(c):
        return pltpu.make_async_copy(whole.at[:, pl.ds(c, 1)], out.at[:, pl.ds(low + c, 1)], sem.at[c])

    def arrived(t, c, b):
        if not starts:
            return came[0][t, c, b]
        n = t * beds + b
        return sum(run[n - start] for run, start in zip(came, starts) if start <= n < start + run.shape[0])

    def finish(sign, at):
        def component(c, carry):
            for b in range(beds):
                line = [arrived(at[t], c, b) for t in range(instances)]
                for t in range(instances):
                    whole[at[t], c, b] = part[at[t], low + c, b] - sign * from_before(line, t)
            moved(c).start()
            return carry

        lax.fori_loop(0, size, component, 0)

    odd = is_odd()

    @pl.when(odd)
    def _():
        finish(-scale, list(reversed(range(instances))))

    @pl.when(jnp.logical_not(odd))
    def _():
        finish(scale, list(range(instances)))

    for c in range(size):
        moved(c).wait()


VMEM = pl.BlockSpec(memory_space=pltpu.VMEM)
SMEM = pl.BlockSpec(memory_space=pltpu.SMEM)
ANY = pl.BlockSpec(memory_space=pl.ANY)
SMALL = pl.CostEstimate(flops=1000, bytes_accessed=1000, transcendentals=0)


def params(mib):
    return pltpu.CompilerParams(vmem_limit_bytes=mib * 2**20)


def local(state, adjoint, plan, valve):
    count = lax.axis_size("tm")
    sections = lax.axis_size("sec")
    instances, comps, beds, _, width = state.shape
    block = jax.ShapeDtypeStruct(state.shape, state.dtype)
    cells = jax.ShapeDtypeStruct((instances, 2 * len(MOVING), beds, width), state.dtype)
    across = [(i, (i + 1) % count if i % 2 else (i - 1) % count) for i in range(count)]
    on_chip = [(i, i ^ 1) for i in range(count)]
    far_state = lax.ppermute(state, "tm", across)
    cut = comps - 2
    far_adjoint = lax.ppermute(adjoint[:, :cut], "tm", across)

    cut_up = adjoint[:, cut].reshape((instances * beds,) + state.shape[3:])
    via = [i for i in VIA if i < count]
    kept = instances * beds - SHARE * len(via)
    starts = [0, kept] + [kept + SHARE * n for n in range(len(via))]

    def over_both(x, pairs):
        return lax.ppermute(x, ("tm", "sec"), [(i * sections + j, k * sections + l) for (i, j), (k, l) in pairs])

    everywhere = [((i, j), (k, j)) for i, k in across for j in range(sections)]
    runs = [
        lax.ppermute(cut_up[:kept], "tm", across),
        over_both(cut_up[kept:], [pair for pair in everywhere if pair != SPARED]),
    ]

    far_last = lax.ppermute(adjoint[:, cut + 1 :], "tm", across)

    def near_transfers():
        in_state = lax.ppermute(state, "tm", on_chip)
        in_adjoint = lax.ppermute(adjoint, "tm", on_chip)
        edge = pl.pallas_call(
            pick_kernel,
            out_shape=cells,
            in_specs=[VMEM, VMEM],
            out_specs=VMEM,
            compiler_params=params(16),
            cost_estimate=SMALL,
            name="pick",
        )(state, adjoint)
        return lax.ppermute(edge, "sec", [(i, i ^ 1) for i in range(sections)]), in_state, in_adjoint

    def nothing():
        return jnp.zeros(cells.shape, cells.dtype), state, adjoint

    near = lax.cond(lax.axis_index("tm") % 2 >= 0, near_transfers, nothing)
    half_way = [
        over_both(cut_up[start : start + SHARE], [(SPARED[0], (i, 0))]) for start, i in zip(starts[2:], via)
    ]
    runs += [over_both(x, [((i, 0), SPARED[1])]) for x, i in zip(half_way, via)]
    res, adj = pl.pallas_call(
        main_kernel,
        out_shape=(block, block),
        in_specs=[SMEM] * 2 + [VMEM] * 5,
        out_specs=(VMEM, VMEM),
        compiler_params=params(24),
        cost_estimate=SMALL,
        name="local_part",
    )(plan, valve, state, adjoint, *near)

    def finish(name, scale, low, size, part, came, before, starts=(), begun=False):
        return pl.pallas_call(
            functools.partial(finish_kernel, scale, low, starts),
            out_shape=block,
            in_specs=[VMEM] * (1 + len(came)) + [ANY] * len(before),
            out_specs=ANY,
            scratch_shapes=[
                pltpu.VMEM((instances, size) + state.shape[2:], state.dtype),
                pltpu.SemaphoreType.DMA((size,)),
            ],
            input_output_aliases={1 + len(came): 0} if begun else {},
            compiler_params=params(16),
            cost_estimate=SMALL,
            name=name,
        )(part, *came, *before)

    residual = finish("finish_residual", 1.0, 0, comps, res, [far_state], runs[2:])
    begun = finish("finish_adjoint", -1.0, 0, cut, adj, [far_adjoint], [residual[0, 0, 0, :8]])
    begun = finish("finish_runs", -1.0, cut, 1, adj, runs, [begun], starts, True)
    return residual, finish("finish_last", -1.0, cut + 1, 1, adj, [far_last], [begun], (), True)


def solution(mesh):
    spec = P("tm", None, None, "sec", None)
    return jax.shard_map(
        local,
        mesh=mesh,
        in_specs=(spec, spec, P("tm", None), P("tm", None)),
        out_specs=(spec, spec),
        check_vma=False,
    )
```

```python
import functools

import jax
import jax.numpy as jnp
from jax import lax
from jax.experimental import pallas as pl
from jax.experimental.pallas import tpu as pltpu
from jax.sharding import PartitionSpec as P

STENCIL = (0.8, -0.2, 4.0 / 105.0, -1.0 / 280.0)
TIME_SCALE = 4.0
FLOW_VELOCITY = 1.0
AXIAL_DISPERSION = 0.3
RADIAL_SPREADING = 0.2
BINDING_STRENGTH = (1.5, 0.6)
HEAT_EXPONENT = (0.5, 0.3)
KINETIC = (1.2, 0.7)
CAPACITY = (2.0, 1.0)
SORPTION_HEAT = (0.4, 0.25)
PURGE_GAIN = 1.5

REACH = len(STENCIL)
WEIGHTS = tuple(TIME_SCALE * c for c in STENCIL)
MOVING = (0, 1, 2, 5)
CENTRE = FLOW_VELOCITY + 2.0 * AXIAL_DISPERSION + 2.0 * RADIAL_SPREADING
UPWIND = FLOW_VELOCITY + AXIAL_DISPERSION
SPARED = ((2, 0), (1, 0))
VIA = (5, 13)
SHARE = 3


def is_odd():
    return lax.rem(lax.axis_index("tm"), 2) == 1


def shifted(x, step, edge):
    cells = x.shape[0]
    row = lax.broadcasted_iota(jnp.int32, x.shape, 0)
    if step > 0:
        return jnp.where(row == 0, edge, pltpu.roll(x, 1, 0))
    return jnp.where(row == cells - 1, edge, pltpu.roll(x, cells - 1, 0))


def radial_pair(x):
    width = x.shape[1]
    lane = lax.broadcasted_iota(jnp.int32, x.shape, 1)
    lower = jnp.where(lane == 0, 0.0, pltpu.roll(x, 1, 1))
    upper = jnp.where(lane == width - 1, 0.0, pltpu.roll(x, width - 1, 1))
    return lower + upper


def transport(x, near, far):
    return CENTRE * x - UPWIND * near - AXIAL_DISPERSION * far - RADIAL_SPREADING * radial_pair(x)


def pick_kernel(state, adjoint, edge):
    instances, _, beds, cells, _ = state.shape
    first = lax.axis_index("sec") == 0

    def step(t, carry):
        for n, x in enumerate((state, adjoint)):
            for k, c in enumerate(MOVING):
                for b in range(beds):
                    row = jnp.where(first, x[t, c, b, cells - 1 :], x[t, c, b, :1])
                    edge[t, n * len(MOVING) + k, b : b + 1] = row
        return carry

    lax.fori_loop(0, instances, step, 0)


def from_before(line, t):
    total = 0.0
    for j in range(t, len(line)):
        total = total + WEIGHTS[t + len(line) - j - 1] * line[j]
    return total


def main_kernel(plan, valve, state, adjoint, edge, in_state, in_adjoint, res, adj):
    instances, comps, beds, cells, _ = res.shape
    odd = is_odd()
    first = lax.axis_index("sec") == 0
    last = lax.axis_index("sec") == lax.axis_size("sec") - 1

    def cell_block(i, carry):
        t = i // beds
        b = lax.rem(i, beds)
        x = [state[t, c, b] for c in range(comps)]
        m = [adjoint[t, c, b] for c in range(comps)]
        y1, y2, _, q1, q2, temp = x
        b1 = BINDING_STRENGTH[0] * jnp.exp(HEAT_EXPONENT[0] * temp)
        b2 = BINDING_STRENGTH[1] * jnp.exp(HEAT_EXPONENT[1] * temp)
        over = 1.0 / (1.0 + b1 * y1 + b2 * y2)
        slope1 = b1 * over
        slope2 = b2 * over
        cover1 = slope1 * y1
        cover2 = slope2 * y2
        rate1 = KINETIC[0] * (CAPACITY[0] * cover1 - q1)
        rate2 = KINETIC[1] * (CAPACITY[1] * cover2 - q2)
        m1 = m[0] - m[3] - SORPTION_HEAT[0] * m[5]
        m2 = m[1] - m[4] - SORPTION_HEAT[1] * m[5]
        g1 = (KINETIC[0] * CAPACITY[0]) * m1
        g2 = (KINETIC[1] * CAPACITY[1]) * m2
        h = g1 * cover1 + g2 * cover2
        e1 = g1 - h
        e2 = g2 - h
        source = {0: rate1, 1: rate2, 5: -SORPTION_HEAT[0] * rate1 - SORPTION_HEAT[1] * rate2}
        pulled = {
            0: slope1 * e1,
            1: slope2 * e2,
            5: HEAT_EXPONENT[0] * cover1 * e1 + HEAT_EXPONENT[1] * cover2 * e2,
        }
        for k, c in enumerate(MOVING):
            from_x = edge[t, k, b][None]
            from_m = edge[t, len(MOVING) + k, b][None]
            below_x = jnp.where(first, 0.0, from_x)
            above_x = jnp.where(last, 0.0, from_x)
            below_m = jnp.where(first, 0.0, from_m)
            above_m = jnp.where(last, 0.0, from_m)
            r = transport(x[c], shifted(x[c], 1, below_x), shifted(x[c], -1, above_x))
            a = transport(m[c], shifted(m[c], -1, above_m), shifted(m[c], 1, below_m))
            res[t, c, b] = r + source[c] if c in source else r
            adj[t, c, b] = a + pulled[c] if c in pulled else a
        res[t, 3, b] = -rate1
        res[t, 4, b] = -rate2
        adj[t, 3, b] = -KINETIC[0] * m1
        adj[t, 4, b] = -KINETIC[1] * m2
        return carry

    lax.fori_loop(0, instances * beds, cell_block, 0)

    @pl.when(last)
    def _():
        def purge(i, carry):
            t = i // beds
            b = lax.rem(i, beds)
            s = lax.rem(b + plan[t, b], beds)
            gain = PURGE_GAIN * valve[t, b].astype(jnp.float32)
            end = pl.ds(cells - 1, 1)
            for c in range(3):
                res[t, c, b, end] += gain * (state[t, c, b, end] - state[t, c, s, end])
                flow = gain * adjoint[t, c, b, end]
                adj[t, c, b, end] += flow
                adj[t, c, s, end] -= flow
            return carry

        lax.fori_loop(0, instances * beds, purge, 0)

    sign = jnp.where(odd, -1.0, 1.0)
    at = [jnp.where(odd, instances - 1 - t, t) for t in range(instances)]

    def time_block(i, carry):
        c = i // beds
        b = lax.rem(i, beds)
        for own, near, out, factor in ((state, in_state, res, sign), (adjoint, in_adjoint, adj, -sign)):
            line = [own[at[t], c, b] for t in range(instances)]
            line += [near[at[t], c, b] for t in range(instances)]
            for t in range(instances):
                total = 0.0
                for k in range(1, REACH + 1):
                    diff = line[t + k]
                    if t - k >= 0:
                        diff = diff - line[t - k]
                    total = total + WEIGHTS[k - 1] * diff
                out[at[t], c, b] += factor * total
        return carry

    lax.fori_loop(0, comps * beds, time_block, 0)


def finish_kernel(scale, low, starts, part, *rest):
    came, (out, whole, sem) = rest[: len(starts) or 1], rest[-3:]
    instances, size, beds, _, _ = whole.shape

    def moved(c):
        return pltpu.make_async_copy(whole.at[:, pl.ds(c, 1)], out.at[:, pl.ds(low + c, 1)], sem.at[c])

    def arrived(t, c, b):
        if not starts:
            return came[0][t, c, b]
        n = t * beds + b
        return sum(run[n - start] for run, start in zip(came, starts) if start <= n < start + run.shape[0])

    def finish(sign, at):
        def component(c, carry):
            for b in range(beds):
                line = [arrived(at[t], c, b) for t in range(instances)]
                for t in range(instances):
                    whole[at[t], c, b] = part[at[t], low + c, b] - sign * from_before(line, t)
            moved(c).start()
            return carry

        lax.fori_loop(0, size, component, 0)

    odd = is_odd()

    @pl.when(odd)
    def _():
        finish(-scale, list(reversed(range(instances))))

    @pl.when(jnp.logical_not(odd))
    def _():
        finish(scale, list(range(instances)))

    for c in range(size):
        moved(c).wait()


VMEM = pl.BlockSpec(memory_space=pltpu.VMEM)
SMEM = pl.BlockSpec(memory_space=pltpu.SMEM)
ANY = pl.BlockSpec(memory_space=pl.ANY)
SMALL = pl.CostEstimate(flops=1000, bytes_accessed=1000, transcendentals=0)


def params(mib):
    return pltpu.CompilerParams(vmem_limit_bytes=mib * 2**20)


def local(state, adjoint, plan, valve):
    count = lax.axis_size("tm")
    sections = lax.axis_size("sec")
    instances, comps, beds, _, width = state.shape
    block = jax.ShapeDtypeStruct(state.shape, state.dtype)
    cells = jax.ShapeDtypeStruct((instances, 2 * len(MOVING), beds, width), state.dtype)
    across = [(i, (i + 1) % count if i % 2 else (i - 1) % count) for i in range(count)]
    on_chip = [(i, i ^ 1) for i in range(count)]
    far_state = lax.ppermute(state, "tm", across)
    cut = comps - 1
    far_adjoint = lax.ppermute(adjoint[:, :cut], "tm", across)

    last = adjoint[:, cut].reshape((instances * beds,) + state.shape[3:])
    via = [i for i in VIA if i < count]
    kept = instances * beds - SHARE * len(via)
    starts = [0, kept] + [kept + SHARE * n for n in range(len(via))]

    def over_both(x, pairs):
        return lax.ppermute(x, ("tm", "sec"), [(i * sections + j, k * sections + l) for (i, j), (k, l) in pairs])

    everywhere = [((i, j), (k, j)) for i, k in across for j in range(sections)]
    runs = [
        lax.ppermute(last[:kept], "tm", across),
        over_both(last[kept:], [pair for pair in everywhere if pair != SPARED]),
    ]

    def near_transfers():
        in_state = lax.ppermute(state, "tm", on_chip)
        in_adjoint = lax.ppermute(adjoint, "tm", on_chip)
        edge = pl.pallas_call(
            pick_kernel,
            out_shape=cells,
            in_specs=[VMEM, VMEM],
            out_specs=VMEM,
            compiler_params=params(16),
            cost_estimate=SMALL,
            name="pick",
        )(state, adjoint)
        return lax.ppermute(edge, "sec", [(i, i ^ 1) for i in range(sections)]), in_state, in_adjoint

    def nothing():
        return jnp.zeros(cells.shape, cells.dtype), state, adjoint

    near = lax.cond(lax.axis_index("tm") % 2 >= 0, near_transfers, nothing)
    half_way = [
        over_both(last[start : start + SHARE], [(SPARED[0], (i, 0))]) for start, i in zip(starts[2:], via)
    ]
    runs += [over_both(x, [((i, 0), SPARED[1])]) for x, i in zip(half_way, via)]
    res, adj = pl.pallas_call(
        main_kernel,
        out_shape=(block, block),
        in_specs=[SMEM] * 2 + [VMEM] * 5,
        out_specs=(VMEM, VMEM),
        compiler_params=params(24),
        cost_estimate=SMALL,
        name="local_part",
    )(plan, valve, state, adjoint, *near)

    def finish(name, scale, low, size, part, came, before, starts=(), begun=False):
        return pl.pallas_call(
            functools.partial(finish_kernel, scale, low, starts),
            out_shape=block,
            in_specs=[VMEM] * (1 + len(came)) + [ANY] * len(before),
            out_specs=ANY,
            scratch_shapes=[
                pltpu.VMEM((instances, size) + state.shape[2:], state.dtype),
                pltpu.SemaphoreType.DMA((size,)),
            ],
            input_output_aliases={1 + len(came): 0} if begun else {},
            compiler_params=params(16),
            cost_estimate=SMALL,
            name=name,
        )(part, *came, *before)

    residual = finish("finish_residual", 1.0, 0, comps, res, [far_state], runs[2:])
    begun = finish("finish_adjoint", -1.0, 0, cut, adj, [far_adjoint], [residual[0, 0, 0, :8]])
    return residual, finish("finish_last", -1.0, cut, 1, adj, runs, [begun], starts, True)


def solution(mesh):
    spec = P("tm", None, None, "sec", None)
    return jax.shard_map(
        local,
        mesh=mesh,
        in_specs=(spec, spec, P("tm", None), P("tm", None)),
        out_specs=(spec, spec),
        check_vma=False,
    )
```

```python
import functools

import jax
import jax.numpy as jnp
from jax import lax
from jax.experimental import pallas as pl
from jax.experimental.pallas import tpu as pltpu
from jax.sharding import PartitionSpec as P

STENCIL = (0.8, -0.2, 4.0 / 105.0, -1.0 / 280.0)
TIME_SCALE = 4.0
FLOW_VELOCITY = 1.0
AXIAL_DISPERSION = 0.3
RADIAL_SPREADING = 0.2
BINDING_STRENGTH = (1.5, 0.6)
HEAT_EXPONENT = (0.5, 0.3)
KINETIC = (1.2, 0.7)
CAPACITY = (2.0, 1.0)
SORPTION_HEAT = (0.4, 0.25)
PURGE_GAIN = 1.5

REACH = len(STENCIL)
WEIGHTS = tuple(TIME_SCALE * c for c in STENCIL)
MOVING = (0, 1, 2, 5)
CENTRE = FLOW_VELOCITY + 2.0 * AXIAL_DISPERSION + 2.0 * RADIAL_SPREADING
UPWIND = FLOW_VELOCITY + AXIAL_DISPERSION
SPARED = ((2, 0), (1, 0))
VIA = (9, 13)
SHARE = 3


def is_odd():
    return lax.rem(lax.axis_index("tm"), 2) == 1


def shifted(x, step, edge):
    cells = x.shape[0]
    row = lax.broadcasted_iota(jnp.int32, x.shape, 0)
    if step > 0:
        return jnp.where(row == 0, edge, pltpu.roll(x, 1, 0))
    return jnp.where(row == cells - 1, edge, pltpu.roll(x, cells - 1, 0))


def radial_pair(x):
    width = x.shape[1]
    lane = lax.broadcasted_iota(jnp.int32, x.shape, 1)
    lower = jnp.where(lane == 0, 0.0, pltpu.roll(x, 1, 1))
    upper = jnp.where(lane == width - 1, 0.0, pltpu.roll(x, width - 1, 1))
    return lower + upper


def transport(x, near, far):
    return CENTRE * x - UPWIND * near - AXIAL_DISPERSION * far - RADIAL_SPREADING * radial_pair(x)


def pick_kernel(state, adjoint, edge):
    instances, _, beds, cells, _ = state.shape
    first = lax.axis_index("sec") == 0

    def step(t, carry):
        for n, x in enumerate((state, adjoint)):
            for k, c in enumerate(MOVING):
                for b in range(beds):
                    row = jnp.where(first, x[t, c, b, cells - 1 :], x[t, c, b, :1])
                    edge[t, n * len(MOVING) + k, b : b + 1] = row
        return carry

    lax.fori_loop(0, instances, step, 0)


def from_before(line, t):
    total = 0.0
    for j in range(t, len(line)):
        total = total + WEIGHTS[t + len(line) - j - 1] * line[j]
    return total


def main_kernel(plan, valve, state, adjoint, edge, in_state, in_adjoint, res, adj):
    instances, comps, beds, cells, _ = res.shape
    odd = is_odd()
    first = lax.axis_index("sec") == 0
    last = lax.axis_index("sec") == lax.axis_size("sec") - 1

    def cell_block(i, carry):
        t = i // beds
        b = lax.rem(i, beds)
        x = [state[t, c, b] for c in range(comps)]
        m = [adjoint[t, c, b] for c in range(comps)]
        y1, y2, _, q1, q2, temp = x
        b1 = BINDING_STRENGTH[0] * jnp.exp(HEAT_EXPONENT[0] * temp)
        b2 = BINDING_STRENGTH[1] * jnp.exp(HEAT_EXPONENT[1] * temp)
        over = 1.0 / (1.0 + b1 * y1 + b2 * y2)
        slope1 = b1 * over
        slope2 = b2 * over
        cover1 = slope1 * y1
        cover2 = slope2 * y2
        rate1 = KINETIC[0] * (CAPACITY[0] * cover1 - q1)
        rate2 = KINETIC[1] * (CAPACITY[1] * cover2 - q2)
        m1 = m[0] - m[3] - SORPTION_HEAT[0] * m[5]
        m2 = m[1] - m[4] - SORPTION_HEAT[1] * m[5]
        g1 = (KINETIC[0] * CAPACITY[0]) * m1
        g2 = (KINETIC[1] * CAPACITY[1]) * m2
        h = g1 * cover1 + g2 * cover2
        e1 = g1 - h
        e2 = g2 - h
        source = {0: rate1, 1: rate2, 5: -SORPTION_HEAT[0] * rate1 - SORPTION_HEAT[1] * rate2}
        pulled = {
            0: slope1 * e1,
            1: slope2 * e2,
            5: HEAT_EXPONENT[0] * cover1 * e1 + HEAT_EXPONENT[1] * cover2 * e2,
        }
        for k, c in enumerate(MOVING):
            from_x = edge[t, k, b][None]
            from_m = edge[t, len(MOVING) + k, b][None]
            below_x = jnp.where(first, 0.0, from_x)
            above_x = jnp.where(last, 0.0, from_x)
            below_m = jnp.where(first, 0.0, from_m)
            above_m = jnp.where(last, 0.0, from_m)
            r = transport(x[c], shifted(x[c], 1, below_x), shifted(x[c], -1, above_x))
            a = transport(m[c], shifted(m[c], -1, above_m), shifted(m[c], 1, below_m))
            res[t, c, b] = r + source[c] if c in source else r
            adj[t, c, b] = a + pulled[c] if c in pulled else a
        res[t, 3, b] = -rate1
        res[t, 4, b] = -rate2
        adj[t, 3, b] = -KINETIC[0] * m1
        adj[t, 4, b] = -KINETIC[1] * m2
        return carry

    lax.fori_loop(0, instances * beds, cell_block, 0)

    @pl.when(last)
    def _():
        def purge(i, carry):
            t = i // beds
            b = lax.rem(i, beds)
            s = lax.rem(b + plan[t, b], beds)
            gain = PURGE_GAIN * valve[t, b].astype(jnp.float32)
            end = pl.ds(cells - 1, 1)
            for c in range(3):
                res[t, c, b, end] += gain * (state[t, c, b, end] - state[t, c, s, end])
                flow = gain * adjoint[t, c, b, end]
                adj[t, c, b, end] += flow
                adj[t, c, s, end] -= flow
            return carry

        lax.fori_loop(0, instances * beds, purge, 0)

    sign = jnp.where(odd, -1.0, 1.0)
    at = [jnp.where(odd, instances - 1 - t, t) for t in range(instances)]

    def time_block(i, carry):
        c = i // beds
        b = lax.rem(i, beds)
        for own, near, out, factor in ((state, in_state, res, sign), (adjoint, in_adjoint, adj, -sign)):
            line = [own[at[t], c, b] for t in range(instances)]
            line += [near[at[t], c, b] for t in range(instances)]
            for t in range(instances):
                total = 0.0
                for k in range(1, REACH + 1):
                    diff = line[t + k]
                    if t - k >= 0:
                        diff = diff - line[t - k]
                    total = total + WEIGHTS[k - 1] * diff
                out[at[t], c, b] += factor * total
        return carry

    lax.fori_loop(0, comps * beds, time_block, 0)


def finish_kernel(scale, low, starts, part, *rest):
    came, (out, whole, sem) = rest[: len(starts) or 1], rest[-3:]
    instances, size, beds, _, _ = whole.shape

    def moved(t, c):
        return pltpu.make_async_copy(
            whole.at[pl.ds(t, 1), pl.ds(c, 1)], out.at[pl.ds(t, 1), pl.ds(low + c, 1)], sem.at[t, c]
        )

    def arrived(t, c, b):
        if not starts:
            return came[0][t, c, b]
        n = t * beds + b
        return sum(run[n - start] for run, start in zip(came, starts) if start <= n < start + run.shape[0])

    def finish(sign, at):
        def component(c, carry):
            for b in range(beds):
                line = [arrived(at[t], c, b) for t in range(instances)]
                for t in range(instances):
                    whole[at[t], c, b] = part[at[t], low + c, b] - sign * from_before(line, t)
            for t in range(instances):
                moved(t, c).start()
            return carry

        lax.fori_loop(0, size, component, 0)

    odd = is_odd()

    @pl.when(odd)
    def _():
        finish(-scale, list(reversed(range(instances))))

    @pl.when(jnp.logical_not(odd))
    def _():
        finish(scale, list(range(instances)))

    for c in range(size):
        for t in range(instances):
            moved(t, c).wait()


VMEM = pl.BlockSpec(memory_space=pltpu.VMEM)
SMEM = pl.BlockSpec(memory_space=pltpu.SMEM)
ANY = pl.BlockSpec(memory_space=pl.ANY)
SMALL = pl.CostEstimate(flops=1000, bytes_accessed=1000, transcendentals=0)


def params(mib):
    return pltpu.CompilerParams(vmem_limit_bytes=mib * 2**20)


def local(state, adjoint, plan, valve):
    count = lax.axis_size("tm")
    sections = lax.axis_size("sec")
    instances, comps, beds, _, width = state.shape
    block = jax.ShapeDtypeStruct(state.shape, state.dtype)
    cells = jax.ShapeDtypeStruct((instances, 2 * len(MOVING), beds, width), state.dtype)
    across = [(i, (i + 1) % count if i % 2 else (i - 1) % count) for i in range(count)]
    on_chip = [(i, i ^ 1) for i in range(count)]
    far_state = lax.ppermute(state, "tm", across)
    cut = comps - 1
    far_adjoint = lax.ppermute(adjoint[:, :cut], "tm", across)

    last = adjoint[:, cut].reshape((instances * beds,) + state.shape[3:])
    via = [i for i in VIA if i < count]
    kept = instances * beds - SHARE * len(via)
    starts = [0, kept] + [kept + SHARE * n for n in range(len(via))]

    def over_both(x, pairs):
        return lax.ppermute(x, ("tm", "sec"), [(i * sections + j, k * sections + l) for (i, j), (k, l) in pairs])

    everywhere = [((i, j), (k, j)) for i, k in across for j in range(sections)]
    runs = [
        lax.ppermute(last[:kept], "tm", across),
        over_both(last[kept:], [pair for pair in everywhere if pair != SPARED]),
    ]

    def near_transfers():
        in_state = lax.ppermute(state, "tm", on_chip)
        in_adjoint = lax.ppermute(adjoint, "tm", on_chip)
        edge = pl.pallas_call(
            pick_kernel,
            out_shape=cells,
            in_specs=[VMEM, VMEM],
            out_specs=VMEM,
            compiler_params=params(16),
            cost_estimate=SMALL,
            name="pick",
        )(state, adjoint)
        return lax.ppermute(edge, "sec", [(i, i ^ 1) for i in range(sections)]), in_state, in_adjoint

    def nothing():
        return jnp.zeros(cells.shape, cells.dtype), state, adjoint

    near = lax.cond(lax.axis_index("tm") % 2 >= 0, near_transfers, nothing)
    half_way = [
        over_both(last[start : start + SHARE], [(SPARED[0], (i, 0))]) for start, i in zip(starts[2:], via)
    ]
    runs += [over_both(x, [((i, 0), SPARED[1])]) for x, i in zip(half_way, via)]
    res, adj = pl.pallas_call(
        main_kernel,
        out_shape=(block, block),
        in_specs=[SMEM] * 2 + [VMEM] * 5,
        out_specs=(VMEM, VMEM),
        compiler_params=params(24),
        cost_estimate=SMALL,
        name="local_part",
    )(plan, valve, state, adjoint, *near)

    def finish(name, scale, low, size, part, came, before, starts=(), begun=False):
        return pl.pallas_call(
            functools.partial(finish_kernel, scale, low, starts),
            out_shape=block,
            in_specs=[VMEM] * (1 + len(came)) + [ANY] * len(before),
            out_specs=ANY,
            scratch_shapes=[
                pltpu.VMEM((instances, size) + state.shape[2:], state.dtype),
                pltpu.SemaphoreType.DMA((instances, size)),
            ],
            input_output_aliases={1 + len(came): 0} if begun else {},
            compiler_params=params(16),
            cost_estimate=SMALL,
            name=name,
        )(part, *came, *before)

    residual = finish("finish_residual", 1.0, 0, comps, res, [far_state], runs[2:])
    begun = finish("finish_adjoint", -1.0, 0, cut, adj, [far_adjoint], [residual[0, 0, 0, :8]])
    return residual, finish("finish_last", -1.0, cut, 1, adj, runs, [begun], starts, True)


def solution(mesh):
    spec = P("tm", None, None, "sec", None)
    return jax.shard_map(
        local,
        mesh=mesh,
        in_specs=(spec, spec, P("tm", None), P("tm", None)),
        out_specs=(spec, spec),
        check_vma=False,
    )
```

```python
import functools

import jax
import jax.numpy as jnp
from jax import lax
from jax.experimental import pallas as pl
from jax.experimental.pallas import tpu as pltpu
from jax.sharding import PartitionSpec as P

STENCIL = (0.8, -0.2, 4.0 / 105.0, -1.0 / 280.0)
TIME_SCALE = 4.0
FLOW_VELOCITY = 1.0
AXIAL_DISPERSION = 0.3
RADIAL_SPREADING = 0.2
BINDING_STRENGTH = (1.5, 0.6)
HEAT_EXPONENT = (0.5, 0.3)
KINETIC = (1.2, 0.7)
CAPACITY = (2.0, 1.0)
SORPTION_HEAT = (0.4, 0.25)
PURGE_GAIN = 1.5

REACH = len(STENCIL)
WEIGHTS = tuple(TIME_SCALE * c for c in STENCIL)
MOVING = (0, 1, 2, 5)
CENTRE = FLOW_VELOCITY + 2.0 * AXIAL_DISPERSION + 2.0 * RADIAL_SPREADING
UPWIND = FLOW_VELOCITY + AXIAL_DISPERSION
SPARED = ((2, 0), (1, 0))
VIA = (9, 13)
SHARE = 3


def is_odd():
    return lax.rem(lax.axis_index("tm"), 2) == 1


def shifted(x, step, edge):
    cells = x.shape[0]
    row = lax.broadcasted_iota(jnp.int32, x.shape, 0)
    if step > 0:
        return jnp.where(row == 0, edge, pltpu.roll(x, 1, 0))
    return jnp.where(row == cells - 1, edge, pltpu.roll(x, cells - 1, 0))


def radial_pair(x):
    width = x.shape[1]
    lane = lax.broadcasted_iota(jnp.int32, x.shape, 1)
    lower = jnp.where(lane == 0, 0.0, pltpu.roll(x, 1, 1))
    upper = jnp.where(lane == width - 1, 0.0, pltpu.roll(x, width - 1, 1))
    return lower + upper


def transport(x, near, far):
    return CENTRE * x - UPWIND * near - AXIAL_DISPERSION * far - RADIAL_SPREADING * radial_pair(x)


def pick_kernel(state, adjoint, edge):
    instances, _, beds, cells, _ = state.shape
    first = lax.axis_index("sec") == 0

    def step(t, carry):
        for n, x in enumerate((state, adjoint)):
            for k, c in enumerate(MOVING):
                for b in range(beds):
                    row = jnp.where(first, x[t, c, b, cells - 1 :], x[t, c, b, :1])
                    edge[t, n * len(MOVING) + k, b : b + 1] = row
        return carry

    lax.fori_loop(0, instances, step, 0)


def from_before(line, t):
    total = 0.0
    for j in range(t, len(line)):
        total = total + WEIGHTS[t + len(line) - j - 1] * line[j]
    return total


def main_kernel(plan, valve, state, adjoint, edge, in_state, in_adjoint, res, adj):
    instances, comps, beds, cells, _ = res.shape
    odd = is_odd()
    first = lax.axis_index("sec") == 0
    last = lax.axis_index("sec") == lax.axis_size("sec") - 1

    def cell_block(i, carry):
        t = i // beds
        b = lax.rem(i, beds)
        x = [state[t, c, b] for c in range(comps)]
        m = [adjoint[t, c, b] for c in range(comps)]
        y1, y2, _, q1, q2, temp = x
        b1 = BINDING_STRENGTH[0] * jnp.exp(HEAT_EXPONENT[0] * temp)
        b2 = BINDING_STRENGTH[1] * jnp.exp(HEAT_EXPONENT[1] * temp)
        over = 1.0 / (1.0 + b1 * y1 + b2 * y2)
        slope1 = b1 * over
        slope2 = b2 * over
        cover1 = slope1 * y1
        cover2 = slope2 * y2
        rate1 = KINETIC[0] * (CAPACITY[0] * cover1 - q1)
        rate2 = KINETIC[1] * (CAPACITY[1] * cover2 - q2)
        m1 = m[0] - m[3] - SORPTION_HEAT[0] * m[5]
        m2 = m[1] - m[4] - SORPTION_HEAT[1] * m[5]
        g1 = (KINETIC[0] * CAPACITY[0]) * m1
        g2 = (KINETIC[1] * CAPACITY[1]) * m2
        h = g1 * cover1 + g2 * cover2
        e1 = g1 - h
        e2 = g2 - h
        source = {0: rate1, 1: rate2, 5: -SORPTION_HEAT[0] * rate1 - SORPTION_HEAT[1] * rate2}
        pulled = {
            0: slope1 * e1,
            1: slope2 * e2,
            5: HEAT_EXPONENT[0] * cover1 * e1 + HEAT_EXPONENT[1] * cover2 * e2,
        }
        for k, c in enumerate(MOVING):
            from_x = edge[t, k, b][None]
            from_m = edge[t, len(MOVING) + k, b][None]
            below_x = jnp.where(first, 0.0, from_x)
            above_x = jnp.where(last, 0.0, from_x)
            below_m = jnp.where(first, 0.0, from_m)
            above_m = jnp.where(last, 0.0, from_m)
            r = transport(x[c], shifted(x[c], 1, below_x), shifted(x[c], -1, above_x))
            a = transport(m[c], shifted(m[c], -1, above_m), shifted(m[c], 1, below_m))
            res[t, c, b] = r + source[c] if c in source else r
            adj[t, c, b] = a + pulled[c] if c in pulled else a
        res[t, 3, b] = -rate1
        res[t, 4, b] = -rate2
        adj[t, 3, b] = -KINETIC[0] * m1
        adj[t, 4, b] = -KINETIC[1] * m2
        return carry

    lax.fori_loop(0, instances * beds, cell_block, 0)

    @pl.when(last)
    def _():
        def purge(i, carry):
            t = i // beds
            b = lax.rem(i, beds)
            s = lax.rem(b + plan[t, b], beds)
            gain = PURGE_GAIN * valve[t, b].astype(jnp.float32)
            end = pl.ds(cells - 1, 1)
            for c in range(3):
                res[t, c, b, end] += gain * (state[t, c, b, end] - state[t, c, s, end])
                flow = gain * adjoint[t, c, b, end]
                adj[t, c, b, end] += flow
                adj[t, c, s, end] -= flow
            return carry

        lax.fori_loop(0, instances * beds, purge, 0)

    sign = jnp.where(odd, -1.0, 1.0)
    at = [jnp.where(odd, instances - 1 - t, t) for t in range(instances)]

    def time_block(i, carry):
        c = i // beds
        b = lax.rem(i, beds)
        for own, near, out, factor in ((state, in_state, res, sign), (adjoint, in_adjoint, adj, -sign)):
            line = [own[at[t], c, b] for t in range(instances)]
            line += [near[at[t], c, b] for t in range(instances)]
            for t in range(instances):
                total = 0.0
                for k in range(1, REACH + 1):
                    diff = line[t + k]
                    if t - k >= 0:
                        diff = diff - line[t - k]
                    total = total + WEIGHTS[k - 1] * diff
                out[at[t], c, b] += factor * total
        return carry

    lax.fori_loop(0, comps * beds, time_block, 0)


def finish_kernel(scale, low, starts, part, *rest):
    came, (out, whole, sem) = rest[: len(starts) or 1], rest[-3:]
    instances, size, beds, _, _ = whole.shape

    def arrived(t, c, b):
        if not starts:
            return came[0][t, c, b]
        n = t * beds + b
        return sum(run[n - start] for run, start in zip(came, starts) if start <= n < start + run.shape[0])

    def finish(sign, at):
        def component(c, carry):
            for b in range(beds):
                line = [arrived(at[t], c, b) for t in range(instances)]
                for t in range(instances):
                    whole[at[t], c, b] = part[at[t], low + c, b] - sign * from_before(line, t)
            return carry

        lax.fori_loop(0, size, component, 0)

    odd = is_odd()

    @pl.when(odd)
    def _():
        finish(-scale, list(reversed(range(instances))))

    @pl.when(jnp.logical_not(odd))
    def _():
        finish(scale, list(range(instances)))

    copy = pltpu.make_async_copy(whole, out.at[:, pl.ds(low, size)], sem)
    copy.start()
    copy.wait()


VMEM = pl.BlockSpec(memory_space=pltpu.VMEM)
SMEM = pl.BlockSpec(memory_space=pltpu.SMEM)
ANY = pl.BlockSpec(memory_space=pl.ANY)
SMALL = pl.CostEstimate(flops=1000, bytes_accessed=1000, transcendentals=0)


def params(mib):
    return pltpu.CompilerParams(vmem_limit_bytes=mib * 2**20)


def local(state, adjoint, plan, valve):
    count = lax.axis_size("tm")
    sections = lax.axis_size("sec")
    instances, comps, beds, _, width = state.shape
    block = jax.ShapeDtypeStruct(state.shape, state.dtype)
    cells = jax.ShapeDtypeStruct((instances, 2 * len(MOVING), beds, width), state.dtype)
    across = [(i, (i + 1) % count if i % 2 else (i - 1) % count) for i in range(count)]
    on_chip = [(i, i ^ 1) for i in range(count)]
    far_state = lax.ppermute(state, "tm", across)
    cut = comps - 1
    far_adjoint = lax.ppermute(adjoint[:, :cut], "tm", across)

    last = adjoint[:, cut].reshape((instances * beds,) + state.shape[3:])
    via = [i for i in VIA if i < count]
    kept = instances * beds - SHARE * len(via)
    starts = [0, kept] + [kept + SHARE * n for n in range(len(via))]

    def over_both(x, pairs):
        return lax.ppermute(x, ("tm", "sec"), [(i * sections + j, k * sections + l) for (i, j), (k, l) in pairs])

    everywhere = [((i, j), (k, j)) for i, k in across for j in range(sections)]
    runs = [
        lax.ppermute(last[:kept], "tm", across),
        over_both(last[kept:], [pair for pair in everywhere if pair != SPARED]),
    ]

    def near_transfers():
        in_state = lax.ppermute(state, "tm", on_chip)
        in_adjoint = lax.ppermute(adjoint, "tm", on_chip)
        edge = pl.pallas_call(
            pick_kernel,
            out_shape=cells,
            in_specs=[VMEM, VMEM],
            out_specs=VMEM,
            compiler_params=params(16),
            cost_estimate=SMALL,
            name="pick",
        )(state, adjoint)
        return lax.ppermute(edge, "sec", [(i, i ^ 1) for i in range(sections)]), in_state, in_adjoint

    def nothing():
        return jnp.zeros(cells.shape, cells.dtype), state, adjoint

    near = lax.cond(lax.axis_index("tm") % 2 >= 0, near_transfers, nothing)
    half_way = [
        over_both(last[start : start + SHARE], [(SPARED[0], (i, 0))]) for start, i in zip(starts[2:], via)
    ]
    runs += [over_both(x, [((i, 0), SPARED[1])]) for x, i in zip(half_way, via)]
    res, adj = pl.pallas_call(
        main_kernel,
        out_shape=(block, block),
        in_specs=[SMEM] * 2 + [VMEM] * 5,
        out_specs=(VMEM, VMEM),
        compiler_params=params(24),
        cost_estimate=SMALL,
        name="local_part",
    )(plan, valve, state, adjoint, *near)

    def finish(name, scale, low, size, part, came, before, starts=(), begun=False):
        return pl.pallas_call(
            functools.partial(finish_kernel, scale, low, starts),
            out_shape=block,
            in_specs=[VMEM] * (1 + len(came)) + [ANY] * len(before),
            out_specs=ANY,
            scratch_shapes=[
                pltpu.VMEM((instances, size) + state.shape[2:], state.dtype),
                pltpu.SemaphoreType.DMA,
            ],
            input_output_aliases={1 + len(came): 0} if begun else {},
            compiler_params=params(16),
            cost_estimate=SMALL,
            name=name,
        )(part, *came, *before)

    residual = finish("finish_residual", 1.0, 0, comps, res, [far_state], runs[2:])
    begun = finish("finish_adjoint", -1.0, 0, cut, adj, [far_adjoint], [residual[0, 0, 0, :8]])
    return residual, finish("finish_last", -1.0, cut, 1, adj, runs, [begun], starts, True)


def solution(mesh):
    spec = P("tm", None, None, "sec", None)
    return jax.shard_map(
        local,
        mesh=mesh,
        in_specs=(spec, spec, P("tm", None), P("tm", None)),
        out_specs=(spec, spec),
        check_vma=False,
    )
```

```python
import functools

import jax
import jax.numpy as jnp
from jax import lax
from jax.experimental import pallas as pl
from jax.experimental.pallas import tpu as pltpu
from jax.sharding import PartitionSpec as P

STENCIL = (0.8, -0.2, 4.0 / 105.0, -1.0 / 280.0)
TIME_SCALE = 4.0
FLOW_VELOCITY = 1.0
AXIAL_DISPERSION = 0.3
RADIAL_SPREADING = 0.2
BINDING_STRENGTH = (1.5, 0.6)
HEAT_EXPONENT = (0.5, 0.3)
KINETIC = (1.2, 0.7)
CAPACITY = (2.0, 1.0)
SORPTION_HEAT = (0.4, 0.25)
PURGE_GAIN = 1.5

REACH = len(STENCIL)
WEIGHTS = tuple(TIME_SCALE * c for c in STENCIL)
MOVING = (0, 1, 2, 5)
CENTRE = FLOW_VELOCITY + 2.0 * AXIAL_DISPERSION + 2.0 * RADIAL_SPREADING
UPWIND = FLOW_VELOCITY + AXIAL_DISPERSION
SPARED = ((2, 0), (1, 0))
VIA = (5, 9)
SHARE = 3


def is_odd():
    return lax.rem(lax.axis_index("tm"), 2) == 1


def shifted(x, step, edge):
    cells = x.shape[0]
    row = lax.broadcasted_iota(jnp.int32, x.shape, 0)
    if step > 0:
        return jnp.where(row == 0, edge, pltpu.roll(x, 1, 0))
    return jnp.where(row == cells - 1, edge, pltpu.roll(x, cells - 1, 0))


def radial_pair(x):
    width = x.shape[1]
    lane = lax.broadcasted_iota(jnp.int32, x.shape, 1)
    lower = jnp.where(lane == 0, 0.0, pltpu.roll(x, 1, 1))
    upper = jnp.where(lane == width - 1, 0.0, pltpu.roll(x, width - 1, 1))
    return lower + upper


def transport(x, near, far):
    return CENTRE * x - UPWIND * near - AXIAL_DISPERSION * far - RADIAL_SPREADING * radial_pair(x)


def pick_kernel(state, adjoint, edge):
    instances, _, beds, cells, _ = state.shape
    first = lax.axis_index("sec") == 0

    def step(t, carry):
        for n, x in enumerate((state, adjoint)):
            for k, c in enumerate(MOVING):
                for b in range(beds):
                    row = jnp.where(first, x[t, c, b, cells - 1 :], x[t, c, b, :1])
                    edge[t, n * len(MOVING) + k, b : b + 1] = row
        return carry

    lax.fori_loop(0, instances, step, 0)


def from_before(line, t):
    total = 0.0
    for j in range(t, len(line)):
        total = total + WEIGHTS[t + len(line) - j - 1] * line[j]
    return total


def main_kernel(plan, valve, state, adjoint, edge, in_state, in_adjoint, res, adj):
    instances, comps, beds, cells, _ = res.shape
    odd = is_odd()
    first = lax.axis_index("sec") == 0
    last = lax.axis_index("sec") == lax.axis_size("sec") - 1

    def cell_block(i, carry):
        t = i // beds
        b = lax.rem(i, beds)
        x = [state[t, c, b] for c in range(comps)]
        m = [adjoint[t, c, b] for c in range(comps)]
        y1, y2, _, q1, q2, temp = x
        b1 = BINDING_STRENGTH[0] * jnp.exp(HEAT_EXPONENT[0] * temp)
        b2 = BINDING_STRENGTH[1] * jnp.exp(HEAT_EXPONENT[1] * temp)
        over = 1.0 / (1.0 + b1 * y1 + b2 * y2)
        slope1 = b1 * over
        slope2 = b2 * over
        cover1 = slope1 * y1
        cover2 = slope2 * y2
        rate1 = KINETIC[0] * (CAPACITY[0] * cover1 - q1)
        rate2 = KINETIC[1] * (CAPACITY[1] * cover2 - q2)
        m1 = m[0] - m[3] - SORPTION_HEAT[0] * m[5]
        m2 = m[1] - m[4] - SORPTION_HEAT[1] * m[5]
        g1 = (KINETIC[0] * CAPACITY[0]) * m1
        g2 = (KINETIC[1] * CAPACITY[1]) * m2
        h = g1 * cover1 + g2 * cover2
        e1 = g1 - h
        e2 = g2 - h
        source = {0: rate1, 1: rate2, 5: -SORPTION_HEAT[0] * rate1 - SORPTION_HEAT[1] * rate2}
        pulled = {
            0: slope1 * e1,
            1: slope2 * e2,
            5: HEAT_EXPONENT[0] * cover1 * e1 + HEAT_EXPONENT[1] * cover2 * e2,
        }
        for k, c in enumerate(MOVING):
            from_x = edge[t, k, b][None]
            from_m = edge[t, len(MOVING) + k, b][None]
            below_x = jnp.where(first, 0.0, from_x)
            above_x = jnp.where(last, 0.0, from_x)
            below_m = jnp.where(first, 0.0, from_m)
            above_m = jnp.where(last, 0.0, from_m)
            r = transport(x[c], shifted(x[c], 1, below_x), shifted(x[c], -1, above_x))
            a = transport(m[c], shifted(m[c], -1, above_m), shifted(m[c], 1, below_m))
            res[t, c, b] = r + source[c] if c in source else r
            adj[t, c, b] = a + pulled[c] if c in pulled else a
        res[t, 3, b] = -rate1
        res[t, 4, b] = -rate2
        adj[t, 3, b] = -KINETIC[0] * m1
        adj[t, 4, b] = -KINETIC[1] * m2
        return carry

    lax.fori_loop(0, instances * beds, cell_block, 0)

    @pl.when(last)
    def _():
        def purge(i, carry):
            t = i // beds
            b = lax.rem(i, beds)
            s = lax.rem(b + plan[t, b], beds)
            gain = PURGE_GAIN * valve[t, b].astype(jnp.float32)
            end = pl.ds(cells - 1, 1)
            for c in range(3):
                res[t, c, b, end] += gain * (state[t, c, b, end] - state[t, c, s, end])
                flow = gain * adjoint[t, c, b, end]
                adj[t, c, b, end] += flow
                adj[t, c, s, end] -= flow
            return carry

        lax.fori_loop(0, instances * beds, purge, 0)

    sign = jnp.where(odd, -1.0, 1.0)
    at = [jnp.where(odd, instances - 1 - t, t) for t in range(instances)]

    def time_block(i, carry):
        c = i // beds
        b = lax.rem(i, beds)
        for own, near, out, factor in ((state, in_state, res, sign), (adjoint, in_adjoint, adj, -sign)):
            line = [own[at[t], c, b] for t in range(instances)]
            line += [near[at[t], c, b] for t in range(instances)]
            for t in range(instances):
                total = 0.0
                for k in range(1, REACH + 1):
                    diff = line[t + k]
                    if t - k >= 0:
                        diff = diff - line[t - k]
                    total = total + WEIGHTS[k - 1] * diff
                out[at[t], c, b] += factor * total
        return carry

    lax.fori_loop(0, comps * beds, time_block, 0)


def finish_kernel(scale, low, starts, part, *rest):
    came, (out, whole, sem) = rest[: len(starts) or 1], rest[-3:]
    instances, size, beds, _, _ = whole.shape

    def moved(c):
        return pltpu.make_async_copy(whole.at[:, pl.ds(c, 1)], out.at[:, pl.ds(low + c, 1)], sem.at[c])

    def arrived(t, c, b):
        if not starts:
            return came[0][t, c, b]
        n = t * beds + b
        return sum(run[n - start] for run, start in zip(came, starts) if start <= n < start + run.shape[0])

    def finish(sign, at):
        def component(c, carry):
            for b in range(beds):
                line = [arrived(at[t], c, b) for t in range(instances)]
                for t in range(instances):
                    whole[at[t], c, b] = part[at[t], low + c, b] - sign * from_before(line, t)
            moved(c).start()
            return carry

        lax.fori_loop(0, size, component, 0)

    odd = is_odd()

    @pl.when(odd)
    def _():
        finish(-scale, list(reversed(range(instances))))

    @pl.when(jnp.logical_not(odd))
    def _():
        finish(scale, list(range(instances)))

    for c in range(size):
        moved(c).wait()


VMEM = pl.BlockSpec(memory_space=pltpu.VMEM)
SMEM = pl.BlockSpec(memory_space=pltpu.SMEM)
ANY = pl.BlockSpec(memory_space=pl.ANY)
SMALL = pl.CostEstimate(flops=1000, bytes_accessed=1000, transcendentals=0)


def params(mib):
    return pltpu.CompilerParams(vmem_limit_bytes=mib * 2**20)


def local(state, adjoint, plan, valve):
    count = lax.axis_size("tm")
    sections = lax.axis_size("sec")
    instances, comps, beds, _, width = state.shape
    block = jax.ShapeDtypeStruct(state.shape, state.dtype)
    cells = jax.ShapeDtypeStruct((instances, 2 * len(MOVING), beds, width), state.dtype)
    across = [(i, (i + 1) % count if i % 2 else (i - 1) % count) for i in range(count)]
    on_chip = [(i, i ^ 1) for i in range(count)]
    far_state = lax.ppermute(state, "tm", across)
    cut = comps - 1
    far_adjoint = lax.ppermute(adjoint[:, :cut], "tm", across)

    last = adjoint[:, cut].reshape((instances * beds,) + state.shape[3:])
    via = [i for i in VIA if i < count]
    kept = instances * beds - SHARE * len(via)
    starts = [0, kept] + [kept + SHARE * n for n in range(len(via))]

    def over_both(x, pairs):
        return lax.ppermute(x, ("tm", "sec"), [(i * sections + j, k * sections + l) for (i, j), (k, l) in pairs])

    everywhere = [((i, j), (k, j)) for i, k in across for j in range(sections)]
    runs = [
        lax.ppermute(last[:kept], "tm", across),
        over_both(last[kept:], [pair for pair in everywhere if pair != SPARED]),
    ]

    def near_transfers():
        in_state = lax.ppermute(state, "tm", on_chip)
        in_adjoint = lax.ppermute(adjoint, "tm", on_chip)
        edge = pl.pallas_call(
            pick_kernel,
            out_shape=cells,
            in_specs=[VMEM, VMEM],
            out_specs=VMEM,
            compiler_params=params(16),
            cost_estimate=SMALL,
            name="pick",
        )(state, adjoint)
        return lax.ppermute(edge, "sec", [(i, i ^ 1) for i in range(sections)]), in_state, in_adjoint

    def nothing():
        return jnp.zeros(cells.shape, cells.dtype), state, adjoint

    near = lax.cond(lax.axis_index("tm") % 2 >= 0, near_transfers, nothing)
    half_way = [
        over_both(last[start : start + SHARE], [(SPARED[0], (i, 0))]) for start, i in zip(starts[2:], via)
    ]
    runs += [over_both(x, [((i, 0), SPARED[1])]) for x, i in zip(half_way, via)]
    res, adj = pl.pallas_call(
        main_kernel,
        out_shape=(block, block),
        in_specs=[SMEM] * 2 + [VMEM] * 5,
        out_specs=(VMEM, VMEM),
        compiler_params=params(24),
        cost_estimate=SMALL,
        name="local_part",
    )(plan, valve, state, adjoint, *near)

    def finish(name, scale, low, size, part, came, before, starts=(), begun=False):
        return pl.pallas_call(
            functools.partial(finish_kernel, scale, low, starts),
            out_shape=block,
            in_specs=[VMEM] * (1 + len(came)) + [ANY] * len(before),
            out_specs=ANY,
            scratch_shapes=[
                pltpu.VMEM((instances, size) + state.shape[2:], state.dtype),
                pltpu.SemaphoreType.DMA((size,)),
            ],
            input_output_aliases={1 + len(came): 0} if begun else {},
            compiler_params=params(16),
            cost_estimate=SMALL,
            name=name,
        )(part, *came, *before)

    residual = finish("finish_residual", 1.0, 0, comps, res, [far_state], runs[2:])
    begun = finish("finish_adjoint", -1.0, 0, cut, adj, [far_adjoint], [residual[0, 0, 0, :8]])
    return residual, finish("finish_last", -1.0, cut, 1, adj, runs, [begun], starts, True)


def solution(mesh):
    spec = P("tm", None, None, "sec", None)
    return jax.shard_map(
        local,
        mesh=mesh,
        in_specs=(spec, spec, P("tm", None), P("tm", None)),
        out_specs=(spec, spec),
        check_vma=False,
    )
```

```python
import functools

import jax
import jax.numpy as jnp
from jax import lax
from jax.experimental import pallas as pl
from jax.experimental.pallas import tpu as pltpu
from jax.sharding import PartitionSpec as P

STENCIL = (0.8, -0.2, 4.0 / 105.0, -1.0 / 280.0)
TIME_SCALE = 4.0
FLOW_VELOCITY = 1.0
AXIAL_DISPERSION = 0.3
RADIAL_SPREADING = 0.2
BINDING_STRENGTH = (1.5, 0.6)
HEAT_EXPONENT = (0.5, 0.3)
KINETIC = (1.2, 0.7)
CAPACITY = (2.0, 1.0)
SORPTION_HEAT = (0.4, 0.25)
PURGE_GAIN = 1.5

REACH = len(STENCIL)
WEIGHTS = tuple(TIME_SCALE * c for c in STENCIL)
MOVING = (0, 1, 2, 5)
CENTRE = FLOW_VELOCITY + 2.0 * AXIAL_DISPERSION + 2.0 * RADIAL_SPREADING
UPWIND = FLOW_VELOCITY + AXIAL_DISPERSION
SPARED = ((2, 0), (1, 0))
VIA = (9, 13)
SHARE = 2


def is_odd():
    return lax.rem(lax.axis_index("tm"), 2) == 1


def shifted(x, step, edge):
    cells = x.shape[0]
    row = lax.broadcasted_iota(jnp.int32, x.shape, 0)
    if step > 0:
        return jnp.where(row == 0, edge, pltpu.roll(x, 1, 0))
    return jnp.where(row == cells - 1, edge, pltpu.roll(x, cells - 1, 0))


def radial_pair(x):
    width = x.shape[1]
    lane = lax.broadcasted_iota(jnp.int32, x.shape, 1)
    lower = jnp.where(lane == 0, 0.0, pltpu.roll(x, 1, 1))
    upper = jnp.where(lane == width - 1, 0.0, pltpu.roll(x, width - 1, 1))
    return lower + upper


def transport(x, near, far):
    return CENTRE * x - UPWIND * near - AXIAL_DISPERSION * far - RADIAL_SPREADING * radial_pair(x)


def pick_kernel(state, adjoint, edge):
    instances, _, beds, cells, _ = state.shape
    first = lax.axis_index("sec") == 0

    def step(t, carry):
        for n, x in enumerate((state, adjoint)):
            for k, c in enumerate(MOVING):
                for b in range(beds):
                    row = jnp.where(first, x[t, c, b, cells - 1 :], x[t, c, b, :1])
                    edge[t, n * len(MOVING) + k, b : b + 1] = row
        return carry

    lax.fori_loop(0, instances, step, 0)


def from_before(line, t):
    total = 0.0
    for j in range(t, len(line)):
        total = total + WEIGHTS[t + len(line) - j - 1] * line[j]
    return total


def main_kernel(plan, valve, state, adjoint, edge, in_state, in_adjoint, res, adj):
    instances, comps, beds, cells, _ = res.shape
    odd = is_odd()
    first = lax.axis_index("sec") == 0
    last = lax.axis_index("sec") == lax.axis_size("sec") - 1

    def cell_block(i, carry):
        t = i // beds
        b = lax.rem(i, beds)
        x = [state[t, c, b] for c in range(comps)]
        m = [adjoint[t, c, b] for c in range(comps)]
        y1, y2, _, q1, q2, temp = x
        b1 = BINDING_STRENGTH[0] * jnp.exp(HEAT_EXPONENT[0] * temp)
        b2 = BINDING_STRENGTH[1] * jnp.exp(HEAT_EXPONENT[1] * temp)
        over = 1.0 / (1.0 + b1 * y1 + b2 * y2)
        slope1 = b1 * over
        slope2 = b2 * over
        cover1 = slope1 * y1
        cover2 = slope2 * y2
        rate1 = KINETIC[0] * (CAPACITY[0] * cover1 - q1)
        rate2 = KINETIC[1] * (CAPACITY[1] * cover2 - q2)
        m1 = m[0] - m[3] - SORPTION_HEAT[0] * m[5]
        m2 = m[1] - m[4] - SORPTION_HEAT[1] * m[5]
        g1 = (KINETIC[0] * CAPACITY[0]) * m1
        g2 = (KINETIC[1] * CAPACITY[1]) * m2
        h = g1 * cover1 + g2 * cover2
        e1 = g1 - h
        e2 = g2 - h
        source = {0: rate1, 1: rate2, 5: -SORPTION_HEAT[0] * rate1 - SORPTION_HEAT[1] * rate2}
        pulled = {
            0: slope1 * e1,
            1: slope2 * e2,
            5: HEAT_EXPONENT[0] * cover1 * e1 + HEAT_EXPONENT[1] * cover2 * e2,
        }
        for k, c in enumerate(MOVING):
            from_x = edge[t, k, b][None]
            from_m = edge[t, len(MOVING) + k, b][None]
            below_x = jnp.where(first, 0.0, from_x)
            above_x = jnp.where(last, 0.0, from_x)
            below_m = jnp.where(first, 0.0, from_m)
            above_m = jnp.where(last, 0.0, from_m)
            r = transport(x[c], shifted(x[c], 1, below_x), shifted(x[c], -1, above_x))
            a = transport(m[c], shifted(m[c], -1, above_m), shifted(m[c], 1, below_m))
            res[t, c, b] = r + source[c] if c in source else r
            adj[t, c, b] = a + pulled[c] if c in pulled else a
        res[t, 3, b] = -rate1
        res[t, 4, b] = -rate2
        adj[t, 3, b] = -KINETIC[0] * m1
        adj[t, 4, b] = -KINETIC[1] * m2
        return carry

    lax.fori_loop(0, instances * beds, cell_block, 0)

    @pl.when(last)
    def _():
        def purge(i, carry):
            t = i // beds
            b = lax.rem(i, beds)
            s = lax.rem(b + plan[t, b], beds)
            gain = PURGE_GAIN * valve[t, b].astype(jnp.float32)
            end = pl.ds(cells - 1, 1)
            for c in range(3):
                res[t, c, b, end] += gain * (state[t, c, b, end] - state[t, c, s, end])
                flow = gain * adjoint[t, c, b, end]
                adj[t, c, b, end] += flow
                adj[t, c, s, end] -= flow
            return carry

        lax.fori_loop(0, instances * beds, purge, 0)

    sign = jnp.where(odd, -1.0, 1.0)
    at = [jnp.where(odd, instances - 1 - t, t) for t in range(instances)]

    def time_block(i, carry):
        c = i // beds
        b = lax.rem(i, beds)
        for own, near, out, factor in ((state, in_state, res, sign), (adjoint, in_adjoint, adj, -sign)):
            line = [own[at[t], c, b] for t in range(instances)]
            line += [near[at[t], c, b] for t in range(instances)]
            for t in range(instances):
                total = 0.0
                for k in range(1, REACH + 1):
                    diff = line[t + k]
                    if t - k >= 0:
                        diff = diff - line[t - k]
                    total = total + WEIGHTS[k - 1] * diff
                out[at[t], c, b] += factor * total
        return carry

    lax.fori_loop(0, comps * beds, time_block, 0)


def finish_kernel(scale, low, starts, part, *rest):
    came, (out, whole, sem) = rest[: len(starts) or 1], rest[-3:]
    instances, size, beds, _, _ = whole.shape

    def moved(c):
        return pltpu.make_async_copy(whole.at[:, pl.ds(c, 1)], out.at[:, pl.ds(low + c, 1)], sem.at[c])

    def arrived(t, c, b):
        if not starts:
            return came[0][t, c, b]
        n = t * beds + b
        return sum(run[n - start] for run, start in zip(came, starts) if start <= n < start + run.shape[0])

    def finish(sign, at):
        def component(c, carry):
            for b in range(beds):
                line = [arrived(at[t], c, b) for t in range(instances)]
                for t in range(instances):
                    whole[at[t], c, b] = part[at[t], low + c, b] - sign * from_before(line, t)
            moved(c).start()
            return carry

        lax.fori_loop(0, size, component, 0)

    odd = is_odd()

    @pl.when(odd)
    def _():
        finish(-scale, list(reversed(range(instances))))

    @pl.when(jnp.logical_not(odd))
    def _():
        finish(scale, list(range(instances)))

    for c in range(size):
        moved(c).wait()


VMEM = pl.BlockSpec(memory_space=pltpu.VMEM)
SMEM = pl.BlockSpec(memory_space=pltpu.SMEM)
ANY = pl.BlockSpec(memory_space=pl.ANY)
SMALL = pl.CostEstimate(flops=1000, bytes_accessed=1000, transcendentals=0)


def params(mib):
    return pltpu.CompilerParams(vmem_limit_bytes=mib * 2**20)


def local(state, adjoint, plan, valve):
    count = lax.axis_size("tm")
    sections = lax.axis_size("sec")
    instances, comps, beds, _, width = state.shape
    block = jax.ShapeDtypeStruct(state.shape, state.dtype)
    cells = jax.ShapeDtypeStruct((instances, 2 * len(MOVING), beds, width), state.dtype)
    across = [(i, (i + 1) % count if i % 2 else (i - 1) % count) for i in range(count)]
    on_chip = [(i, i ^ 1) for i in range(count)]
    far_state = lax.ppermute(state, "tm", across)
    cut = comps - 1
    far_adjoint = lax.ppermute(adjoint[:, :cut], "tm", across)

    last = adjoint[:, cut].reshape((instances * beds,) + state.shape[3:])
    via = [i for i in VIA if i < count]
    kept = instances * beds - SHARE * len(via)
    starts = [0, kept] + [kept + SHARE * n for n in range(len(via))]

    def over_both(x, pairs):
        return lax.ppermute(x, ("tm", "sec"), [(i * sections + j, k * sections + l) for (i, j), (k, l) in pairs])

    everywhere = [((i, j), (k, j)) for i, k in across for j in range(sections)]
    runs = [
        lax.ppermute(last[:kept], "tm", across),
        over_both(last[kept:], [pair for pair in everywhere if pair != SPARED]),
    ]

    def near_transfers():
        in_state = lax.ppermute(state, "tm", on_chip)
        in_adjoint = lax.ppermute(adjoint, "tm", on_chip)
        edge = pl.pallas_call(
            pick_kernel,
            out_shape=cells,
            in_specs=[VMEM, VMEM],
            out_specs=VMEM,
            compiler_params=params(16),
            cost_estimate=SMALL,
            name="pick",
        )(state, adjoint)
        return lax.ppermute(edge, "sec", [(i, i ^ 1) for i in range(sections)]), in_state, in_adjoint

    def nothing():
        return jnp.zeros(cells.shape, cells.dtype), state, adjoint

    near = lax.cond(lax.axis_index("tm") % 2 >= 0, near_transfers, nothing)
    half_way = [
        over_both(last[start : start + SHARE], [(SPARED[0], (i, 0))]) for start, i in zip(starts[2:], via)
    ]
    runs += [over_both(x, [((i, 0), SPARED[1])]) for x, i in zip(half_way, via)]
    res, adj = pl.pallas_call(
        main_kernel,
        out_shape=(block, block),
        in_specs=[SMEM] * 2 + [VMEM] * 5,
        out_specs=(VMEM, VMEM),
        compiler_params=params(24),
        cost_estimate=SMALL,
        name="local_part",
    )(plan, valve, state, adjoint, *near)

    def finish(name, scale, low, size, part, came, before, starts=(), begun=False):
        return pl.pallas_call(
            functools.partial(finish_kernel, scale, low, starts),
            out_shape=block,
            in_specs=[VMEM] * (1 + len(came)) + [ANY] * len(before),
            out_specs=ANY,
            scratch_shapes=[
                pltpu.VMEM((instances, size) + state.shape[2:], state.dtype),
                pltpu.SemaphoreType.DMA((size,)),
            ],
            input_output_aliases={1 + len(came): 0} if begun else {},
            compiler_params=params(16),
            cost_estimate=SMALL,
            name=name,
        )(part, *came, *before)

    residual = finish("finish_residual", 1.0, 0, comps, res, [far_state], runs[2:])
    begun = finish("finish_adjoint", -1.0, 0, cut, adj, [far_adjoint], [residual[0, 0, 0, :8]])
    return residual, finish("finish_last", -1.0, cut, 1, adj, runs, [begun], starts, True)


def solution(mesh):
    spec = P("tm", None, None, "sec", None)
    return jax.shard_map(
        local,
        mesh=mesh,
        in_specs=(spec, spec, P("tm", None), P("tm", None)),
        out_specs=(spec, spec),
        check_vma=False,
    )
```
